32 devices in a mesh: sib: 2 (over x), leaf: 16 (over z, y, core).
Axes of the slice: x: 2, y: 2, z: 4, core: 2. Of those that a mesh axis runs over, the one named last changes fastest.
Arguments:
- t_int: float32 [16, 512, 1024], P('leaf', 'sib'), as said below
- t_ext: float32 [16, 512, 512], P('leaf', 'sib'), may hold values from -6 to 6
- iface_map: int32 [16, 512], P('leaf'), may hold values from 0 to 511, each once within a row
Outputs:
- own_map: float32 [16, 512, 512], P('leaf', 'sib')
- cross_map: float32 [16, 512, 512], P('leaf', 'sib')
- solution_op: float32 [16, 512, 512], P('leaf', 'sib')
The draws below stay inside these ranges and needn't reach their ends.
Inputs may be any that keep to these rules, and one draw needn't show every extreme that they name: For each box, the last 512 columns of t_int form a symmetric matrix equal to the identity plus a positive semidefinite matrix. `iface_map`: each row is a permutation of 0 to 511.
All inputs are finite; a program needn't handle non-finite values.
Results may differ from the reference program's by a relative error of at most 0.0003.
Values sent between devices are 32-bit elements; how exact they have to be, the bound alone decides.
No kernel may reach another device: no remote copies, remote signals or barrier semaphores. Data moves between devices by JAX's collectives and lax.ppermute only.
A program may use at most 64 MiB of HBM per device.

```python
import jax
import jax.numpy as jnp
from jax import lax

NE = 512
NI = 512
BOXES = 16
PAIRS = 8


def draw_t_int(key, part):
    key_cross = jax.random.fold_in(jax.random.fold_in(key, 11), 0)
    key_gram = jax.random.fold_in(jax.random.fold_in(key, 11), 1)
    key_column = jax.random.fold_in(jax.random.fold_in(key, 11), 3)
    column_scale = jnp.exp(jax.random.uniform(key_column, (BOXES, 1, NI), jnp.float32, -3.5, 3.5))
    coupling = 0.25 * jax.random.normal(key_cross, (BOXES, NI, NE), jnp.float32)
    factor = jax.random.normal(key_gram, (BOXES, NI, NI), jnp.float32)
    factor = factor * column_scale
    gram = jnp.einsum('bik,bjk->bij', factor, factor, precision=jax.lax.Precision.HIGHEST) / NI
    gram = 0.5 * (gram + jnp.swapaxes(gram, 1, 2)) + jnp.eye(NI, dtype=jnp.float32)[None]
    return jnp.concatenate([coupling, gram], axis=2).astype(jnp.float32)


def block_scale(key, extent, shards, smallest, largest):
    loudness, own = 1.0, jax.random.fold_in(key, 6)
    for position, shards_of in shards:
        steps = jnp.exp(jax.random.uniform(jax.random.fold_in(own, position), (shards_of,), jnp.float32, smallest / len(shards), largest / len(shards)))
        loudness = loudness * jnp.repeat(steps, extent[position] // shards_of).reshape([-1 if axis == position else 1 for axis in range(len(extent))])
    return loudness


def scatter_about(own_key, shape, width, most, shards=(), kind=jnp.bfloat16):
    level = block_scale(own_key, shape, shards, -0.22, 0.18) if shards else 1.0
    result = jax.random.normal(own_key, shape, jnp.float32) * width * level
    return jnp.minimum(jnp.maximum(result, -most), most).astype(kind)


def setup_inputs(seed: int = 0) -> dict:
    arg_keys = jax.random.split(jax.random.key(seed), 4)
    return {
        "t_int": draw_t_int(jax.random.fold_in(arg_keys[3], 71), 0),
        "t_ext": scatter_about(arg_keys[1], (BOXES, NE, NE), 1.0, 6.0, ((0, 16), (1, 2)), jnp.float32),
        "iface_map": jax.vmap(lambda own: jax.random.permutation(own, NI))(jax.random.split(arg_keys[2], BOXES)).reshape((BOXES, NI)).astype(jnp.int32),
    }


def common_order(matrix, index_map):
    inverse = jnp.zeros((NI,), jnp.int32).at[index_map].set(jnp.arange(NI, dtype=jnp.int32))
    picked = matrix[inverse]
    return (picked[:, :NE], picked[:, NE + inverse])

def lower_solve(factor, right_side, flipped):
    return lax.linalg.triangular_solve(factor, right_side, left_side=True, lower=True, transpose_a=flipped)

def product(left, right):
    return jnp.dot(left.astype(jnp.float32), right.astype(jnp.float32), precision=lax.Precision.HIGHEST, preferred_element_type=jnp.float32)

def merge_pair(inputs):
    first_rows, second_rows, first_ext, second_ext, first_map, second_map = inputs
    outer_a, iface_a = common_order(first_rows, first_map)
    outer_b, iface_b = common_order(second_rows, second_map)
    factor = jnp.linalg.cholesky(iface_a + iface_b)
    solved_a = lower_solve(factor, outer_a, False)
    solved_b = lower_solve(factor, outer_b, False)
    own_a = first_ext - product(solved_a.T, solved_a)
    own_b = second_ext - product(solved_b.T, solved_b)
    cross_a = -product(solved_a.T, solved_b)
    cross_b = -product(solved_b.T, solved_a)
    sol_a = -lower_solve(factor, solved_a, True)
    sol_b = -lower_solve(factor, solved_b, True)
    return (own_a, own_b, cross_a, cross_b, sol_a, sol_b)

def reference(t_int, t_ext, iface_map):
    inputs = (t_int[:PAIRS], t_int[PAIRS:], t_ext[:PAIRS], t_ext[PAIRS:], iface_map[:PAIRS], iface_map[PAIRS:])
    own_a, own_b, cross_a, cross_b, sol_a, sol_b = lax.map(merge_pair, inputs)
    own_map = jnp.concatenate([own_a, own_b], axis=0)
    cross_map = jnp.concatenate([cross_a, cross_b], axis=0)
    solution_op = jnp.concatenate([sol_a, sol_b], axis=0)
    return (own_map, cross_map, solution_op)
```

```python
import functools

import jax
import jax.numpy as jnp
from jax import lax
from jax.experimental import pallas as pl
from jax.experimental.pallas import tpu as pltpu
from jax.sharding import PartitionSpec as P

F32 = jnp.float32
BF16 = jnp.bfloat16
TILE = 128
VMEM_LIMIT = 48 * 2**20


def split3(x):
    high = x.astype(BF16).astype(F32)
    rest = x - high
    middle = rest.astype(BF16).astype(F32)
    return high, middle, rest - middle


def contract(left, right, dims):
    return lax.dot_general(left, right, (dims, ((), ())), preferred_element_type=F32)


def full(left, right, dims=((1,), (0,))):
    return lax.dot_general(
        left, right, (dims, ((), ())), precision=lax.Precision.HIGHEST, preferred_element_type=F32
    )


def three_pass(left, right, dims):
    lh, rh = left.astype(BF16), right.astype(BF16)
    ll, rl = (left - lh.astype(F32)).astype(BF16), (right - rh.astype(F32)).astype(BF16)
    return contract(lh, rh, dims) + (contract(lh, rl, dims) + contract(ll, rh, dims))


def pick_left(onehot, x, dims):
    high, middle, low = (part.astype(BF16) for part in split3(x))
    return contract(onehot, high, dims) + (contract(onehot, middle, dims) + contract(onehot, low, dims))


def pick_right(x, onehot, dims):
    high, middle, low = (part.astype(BF16) for part in split3(x))
    return contract(high, onehot, dims) + (contract(middle, onehot, dims) + contract(low, onehot, dims))


def over_lanes(x, lane):
    return jnp.broadcast_to(x[:, lane : lane + 1], (8, TILE))


def over_rows(x, row):
    return jnp.broadcast_to(x[row : row + 1, :], (8, TILE))


def reciprocal(d):
    r = pltpu.reciprocal(d, approx=True)
    return r * (2.0 - d * r)


def invert_tile(work, slabs=2):
    width = 8 * slabs
    lane = lax.broadcasted_iota(jnp.int32, (8, TILE), 1)
    row = lax.broadcasted_iota(jnp.int32, (8, TILE), 0)
    lane_all = lax.broadcasted_iota(jnp.int32, (TILE, TILE), 1)
    is_row = [row == j for j in range(8)]
    for base in range(0, TILE, width):
        old = [work[base + 8 * s : base + 8 * s + 8, :] for s in range(slabs)]
        columns = [[over_lanes(old[s], base + m) for s in range(slabs)] for m in range(width)]
        inside = (lane >= base) & (lane < base + width)
        new = [
            jnp.where(inside, jnp.where(lane - base - 8 * s == row, 1.0, 0.0).astype(F32), old[s])
            for s in range(slabs)
        ]
        pivot = over_rows(columns[0][0], 0)
        for j in range(width):
            js, jr = divmod(j, 8)
            inverse = reciprocal(pivot)
            here = columns[j]
            scaled = [c * inverse for c in here]
            for m in range(j + 1, width):
                picked = over_rows(columns[m][js], jr)
                if m == j + 1:
                    later = [columns[m][s] - (here[s] * picked) * inverse for s in range(slabs)]
                    pivot = over_rows(later[m // 8], m % 8)
                else:
                    later = [columns[m][s] - scaled[s] * picked for s in range(slabs)]
                later[js] = jnp.where(is_row[jr], picked * inverse, later[js])
                columns[m] = later
            picked = over_rows(new[js], jr)
            later = [new[s] - scaled[s] * picked for s in range(slabs)]
            later[js] = jnp.where(is_row[jr], picked * inverse, later[js])
            new = later
        panel = jnp.concatenate(new, axis=0)
        sign = jnp.where(lane < base, -1.0, jnp.where(inside, 0.0, 1.0)).astype(F32)
        ah, am, al = split3(jnp.concatenate([x * sign for x in old], axis=0))
        bh, bm, bl = split3(panel)
        left = jnp.concatenate([ah, ah, am, am, ah, al], axis=0).astype(BF16)
        right = jnp.concatenate([bh, bm, bh, bm, bl, bh], axis=0).astype(BF16)
        change = contract(left, right, ((0,), (0,)))
        inside_all = (lane_all >= base) & (lane_all < base + width)
        rest = jnp.where(inside_all, 0.0, work) - change
        work = jnp.concatenate(
            [x for x in (rest[:base], panel, rest[base + width :]) if x.shape[0]], axis=0
        )
    return work


def eliminate(a_ref, g_ref, steps):
    size = a_ref.shape[0]
    for k in steps:
        at, after = k * TILE, (k + 1) * TILE
        own = slice(at, after)
        inverse = invert_tile(a_ref[own, own])
        right = full(inverse, g_ref[own, :])
        g_ref[own, :] = right
        if after < size:
            old = a_ref[own, after:]
            panel = full(inverse, old)
            a_ref[own, after:] = panel
        for i in range(k + 1, size // TILE):
            rows = slice(i * TILE, (i + 1) * TILE)
            factor = old[:, (i - k - 1) * TILE : (i - k) * TILE]
            a_ref[rows, i * TILE :] = a_ref[rows, i * TILE :] - full(
                factor, panel[:, (i - k - 1) * TILE :], ((0,), (0,))
            )
            g_ref[rows, :] = g_ref[rows, :] - full(factor, right, ((0,), (0,)))
        for i in range(k):
            rows = slice(i * TILE, (i + 1) * TILE)
            factor = a_ref[rows, own]
            if after < size:
                a_ref[rows, after:] = a_ref[rows, after:] - full(factor, panel)
            g_ref[rows, :] = g_ref[rows, :] - full(factor, right)


def call(body, outs, scratch=(), **cost):
    return pl.pallas_call(
        body,
        out_shape=outs,
        scratch_shapes=list(scratch),
        compiler_params=pltpu.CompilerParams(vmem_limit_bytes=VMEM_LIMIT),
        **cost,
    )


def solve_body(a_ref, r_ref, g_ref, a_work):
    a_work[...] = a_ref[...]
    g_ref[...] = r_ref[...]
    eliminate(a_work, g_ref, range(a_ref.shape[0] // TILE))


def solve(a, r):
    return call(
        solve_body, jax.ShapeDtypeStruct(r.shape, F32), [pltpu.VMEM(a.shape, F32)]
    )(a, r)


def first_body(
    half, t_ref, diag_ref, near_ref, far_ref, other_ref, column_ref, row_ref, first_ref, a_out, g_out, p_out, m_work
):
    n = 2 * half
    q = half // 2
    width = t_ref.shape[1] - n
    mine = first_ref[0]

    def block(i, j):
        return (slice(i * q, (i + 1) * q), slice(j * q, (j + 1) * q))

    def part(ref, i):
        return ref[i * q : (i + 1) * q, :]

    def put(i, j, value):
        m_work[block(i, j)] = value
        if i != j:
            m_work[block(j, i)] = value.T

    for base, ref in ((0, near_ref), (2, far_ref)):
        put(base, base, part(ref, 0))
        put(base, base + 1, part(ref, 1))
        put(base + 1, base + 1, part(ref, 2))
    put(0, 3, part(near_ref, 3))
    put(2, 1, part(far_ref, 3))

    @pl.when(mine == 0)
    def _():
        put(0, 2, part(near_ref, 4))
        put(3, 1, part(far_ref, 4))

    @pl.when(mine != 0)
    def _():
        put(1, 3, part(near_ref, 4))
        put(2, 0, part(far_ref, 4))

    same = column_ref[...] == row_ref[...]
    onehot = jnp.where(same, 1.0, 0.0).astype(BF16)
    p_out[...] = onehot
    moved = pick_right(m_work[...], onehot, ((1,), (1,)))
    here = pl.ds(pl.multiple_of(width + mine * half, half), half)
    there = pl.ds(pl.multiple_of(width + (1 - mine) * half, half), half)
    a_out[0:half, 0:half] = t_ref[:, here]
    a_out[0:half, half:n] = t_ref[:, there]
    a_out[block(2, 2)] = part(diag_ref, 0)
    a_out[block(2, 3)] = part(diag_ref, 1)
    a_out[block(3, 3)] = part(diag_ref, 2)
    for i in range(n // TILE):
        rows, later = slice(i * TILE, (i + 1) * TILE), slice(i * TILE, n)
        a_out[rows, later] = a_out[rows, later] + pick_left(onehot[rows, :], moved[:, later], ((1,), (0,)))
    g_out[0:half, :] = t_ref[:, 0:width]
    g_out[half:n, :] = other_ref[...]
    eliminate(a_out, g_out, range(n // TILE // 2))


def second_body(
    half, a_ref, g_in, p_ref, t_ref, other_ref, ext_ref, row_ref, first_ref, own_ref, sol_ref, h_ref, a_work, g_work
):
    n = 2 * half
    mine = first_ref[0]
    a_work[...] = a_ref[...]
    g_work[...] = g_in[...]
    eliminate(a_work, g_work, range(n // TILE // 2, n // TILE))
    block = pl.ds(pl.multiple_of(mine * half, half), half)
    g = g_work[...]
    h_ref[...] = pick_left(p_ref[...], g_work[:, block], ((0,), (0,)))
    left = jnp.concatenate([t_ref[:, block], other_ref[:, block]], axis=0)
    own_ref[...] = ext_ref[...] - three_pass(left, g, ((0,), (0,)))
    target = lax.broadcasted_iota(jnp.int32, (half, n), 0) + mine * half
    onehot = jnp.where(row_ref[...] == target, 1.0, 0.0).astype(BF16)
    sol_ref[...] = -pick_left(onehot, g, ((1,), (0,)))


def cross_body(h_ref, near_ref, far_ref, out_ref):
    half = near_ref.shape[0]
    out_ref[...] = -(
        three_pass(h_ref[0:half, :], near_ref[...], ((0,), (0,)))
        + three_pass(h_ref[half:, :], far_ref[...], ((0,), (0,)))
    )


def sibling(x):
    size = lax.axis_size("leaf")
    return lax.ppermute(x, "leaf", [(i, i ^ size // 2) for i in range(size)])


def across(x):
    return lax.ppermute(x, "sib", [(0, 1), (1, 0)])


def two_shards(t_int, t_ext, iface_map):
    t_int, t_ext = t_int[0], t_ext[0]
    half, n = t_int.shape[0], iface_map.shape[1]
    q, width = half // 2, t_int.shape[1] - n
    mine = lax.axis_index("sib")
    here, there = width + mine * half, width + (1 - mine) * half
    cut = lambda row, column: lax.dynamic_slice(t_int, (row, column), (q, q))
    diag = jnp.concatenate([cut(0, here), cut(0, here + q), cut(q, here + q)], axis=0)
    packed = jnp.concatenate([diag, cut(0, there + q), cut(mine * q, there + mine * q)], axis=0)
    near = sibling(packed)
    other_map = sibling(iface_map)
    diag_other = across(diag)
    outer = t_int[:, :width]
    outer_other = across(outer)
    far = across(near)
    outer_late, _ = lax.optimization_barrier((outer, near))
    outer_near = sibling(outer_late)
    rolled = lambda m: lax.dynamic_slice(jnp.concatenate([m, m], axis=1), (0, mine * half), (1, n))
    own_row, other_row = rolled(iface_map), rolled(other_map)
    first = mine.astype(jnp.int32).reshape(1)

    f = lambda *shape: jax.ShapeDtypeStruct(shape, F32)
    vmem, smem = pl.BlockSpec(memory_space=pltpu.VMEM), pl.BlockSpec(memory_space=pltpu.SMEM)
    a, g, onehot = pl.pallas_call(
        functools.partial(first_body, half),
        out_shape=(f(n, n), f(n, width), jax.ShapeDtypeStruct((n, n), BF16)),
        in_specs=[vmem] * 7 + [smem],
        scratch_shapes=[pltpu.VMEM((n, n), F32)],
        compiler_params=pltpu.CompilerParams(vmem_limit_bytes=VMEM_LIMIT),
    )(t_int, diag_other, near, far, outer_other, own_row.reshape(n, 1), other_row, first)
    a, g, outer_near = lax.optimization_barrier((a, g, outer_near))
    outer_far = across(outer_near)
    own_map, solution_op, h = pl.pallas_call(
        functools.partial(second_body, half),
        out_shape=(f(half, width), f(half, width), f(n, half)),
        in_specs=[vmem] * 7 + [smem],
        scratch_shapes=[pltpu.VMEM((n, n), F32), pltpu.VMEM((n, width), F32)],
        compiler_params=pltpu.CompilerParams(vmem_limit_bytes=VMEM_LIMIT),
    )(a, g, onehot, t_int, outer_other, t_ext, own_row, first)
    cross_map = call(cross_body, f(half, width))(h, outer_near, outer_far)
    return own_map[None], cross_map[None], solution_op[None]


def common_order(matrix, index_map):
    points = index_map.shape[0]
    inverse = jnp.zeros((points,), jnp.int32).at[index_map].set(jnp.arange(points, dtype=jnp.int32))
    picked = matrix[inverse]
    outer_width = matrix.shape[1] - points
    return (picked[:, :outer_width], picked[:, outer_width + inverse])


def many_shards(t_int, t_ext, iface_map):
    shard_rows = t_ext.shape[1]
    first_row = lax.axis_index("sib") * shard_rows
    near_rows, other_map = sibling((t_int, iface_map))
    own_rows = lax.all_gather(t_int, "sib", axis=1, tiled=True)
    other_rows = lax.all_gather(near_rows, "sib", axis=1, tiled=True)
    own_outer, own_iface = common_order(own_rows[0], iface_map[0])
    other_outer, other_iface = common_order(other_rows[0], other_map[0])
    g = solve(own_iface + other_iface, own_outer)
    product = lambda left, right: full(left, right, ((0,), (0,)))
    left = lax.dynamic_slice_in_dim(own_outer, first_row, shard_rows, 1)
    left_g = lax.dynamic_slice_in_dim(g, first_row, shard_rows, 1)
    own_map = t_ext - product(left, g)[None]
    cross_map = -product(left_g, other_outer)[None]
    solution_op = -lax.dynamic_slice_in_dim(g, first_row, shard_rows, 0)[None]
    return own_map, cross_map, solution_op


def solution(mesh):
    placed = P("leaf", "sib", None)
    return jax.shard_map(
        two_shards if mesh.shape["sib"] == 2 else many_shards,
        mesh=mesh,
        in_specs=(placed, placed, P("leaf", None)),
        out_specs=(placed, placed, placed),
        check_vma=False,
    )
```

```python
import functools

import jax
import jax.numpy as jnp
from jax import lax
from jax.experimental import pallas as pl
from jax.experimental.pallas import tpu as pltpu
from jax.sharding import PartitionSpec as P

F32 = jnp.float32
BF16 = jnp.bfloat16
TILE = 128
VMEM_LIMIT = 48 * 2**20


def split3(x):
    high = x.astype(BF16).astype(F32)
    rest = x - high
    middle = rest.astype(BF16).astype(F32)
    return high, middle, rest - middle


def contract(left, right, dims):
    return lax.dot_general(left, right, (dims, ((), ())), preferred_element_type=F32)


def full(left, right, dims=((1,), (0,))):
    return lax.dot_general(
        left, right, (dims, ((), ())), precision=lax.Precision.HIGHEST, preferred_element_type=F32
    )


def three_pass(left, right, dims):
    lh, rh = left.astype(BF16), right.astype(BF16)
    ll, rl = (left - lh.astype(F32)).astype(BF16), (right - rh.astype(F32)).astype(BF16)
    return contract(lh, rh, dims) + (contract(lh, rl, dims) + contract(ll, rh, dims))


def pick_left(onehot, x, dims):
    high, middle, low = (part.astype(BF16) for part in split3(x))
    return contract(onehot, high, dims) + (contract(onehot, middle, dims) + contract(onehot, low, dims))


def pick_right(x, onehot, dims):
    high, middle, low = (part.astype(BF16) for part in split3(x))
    return contract(high, onehot, dims) + (contract(middle, onehot, dims) + contract(low, onehot, dims))


def over_lanes(x, lane):
    return jnp.broadcast_to(x[:, lane : lane + 1], (8, TILE))


def over_rows(x, row):
    return jnp.broadcast_to(x[row : row + 1, :], (8, TILE))


def reciprocal(d):
    r = pltpu.reciprocal(d, approx=True)
    return r * (2.0 - d * r)


def invert_tile(work, slabs=2):
    width = 8 * slabs
    lane = lax.broadcasted_iota(jnp.int32, (8, TILE), 1)
    row = lax.broadcasted_iota(jnp.int32, (8, TILE), 0)
    lane_all = lax.broadcasted_iota(jnp.int32, (TILE, TILE), 1)
    is_row = [row == j for j in range(8)]
    for base in range(0, TILE, width):
        old = [work[base + 8 * s : base + 8 * s + 8, :] for s in range(slabs)]
        columns = [[over_lanes(old[s], base + m) for s in range(slabs)] for m in range(width)]
        inside = (lane >= base) & (lane < base + width)
        new = [
            jnp.where(inside, jnp.where(lane - base - 8 * s == row, 1.0, 0.0).astype(F32), old[s])
            for s in range(slabs)
        ]
        pivot = over_rows(columns[0][0], 0)
        for j in range(width):
            js, jr = divmod(j, 8)
            inverse = reciprocal(pivot)
            here = columns[j]
            scaled = [c * inverse for c in here]
            for m in range(j + 1, width):
                picked = over_rows(columns[m][js], jr)
                if m == j + 1:
                    later = [columns[m][s] - (here[s] * picked) * inverse for s in range(slabs)]
                    pivot = over_rows(later[m // 8], m % 8)
                else:
                    later = [columns[m][s] - scaled[s] * picked for s in range(slabs)]
                later[js] = jnp.where(is_row[jr], picked * inverse, later[js])
                columns[m] = later
            picked = over_rows(new[js], jr)
            later = [new[s] - scaled[s] * picked for s in range(slabs)]
            later[js] = jnp.where(is_row[jr], picked * inverse, later[js])
            new = later
        panel = jnp.concatenate(new, axis=0)
        sign = jnp.where(lane < base, -1.0, jnp.where(inside, 0.0, 1.0)).astype(F32)
        ah, am, al = split3(jnp.concatenate([x * sign for x in old], axis=0))
        bh, bm, bl = split3(panel)
        left = jnp.concatenate([ah, ah, am, am, ah, al], axis=0).astype(BF16)
        right = jnp.concatenate([bh, bm, bh, bm, bl, bh], axis=0).astype(BF16)
        change = contract(left, right, ((0,), (0,)))
        inside_all = (lane_all >= base) & (lane_all < base + width)
        rest = jnp.where(inside_all, 0.0, work) - change
        work = jnp.concatenate(
            [x for x in (rest[:base], panel, rest[base + width :]) if x.shape[0]], axis=0
        )
    return work


def eliminate(a_ref, g_ref, steps):
    size = a_ref.shape[0]
    for k in steps:
        at, after = k * TILE, (k + 1) * TILE
        own = slice(at, after)
        inverse = invert_tile(a_ref[own, own])
        right = full(inverse, g_ref[own, :])
        g_ref[own, :] = right
        if after < size:
            old = a_ref[own, after:]
            panel = full(inverse, old)
            a_ref[own, after:] = panel
        for i in range(k + 1, size // TILE):
            rows = slice(i * TILE, (i + 1) * TILE)
            factor = old[:, (i - k - 1) * TILE : (i - k) * TILE]
            a_ref[rows, i * TILE :] = a_ref[rows, i * TILE :] - full(
                factor, panel[:, (i - k - 1) * TILE :], ((0,), (0,))
            )
            g_ref[rows, :] = g_ref[rows, :] - full(factor, right, ((0,), (0,)))
        for i in range(k):
            rows = slice(i * TILE, (i + 1) * TILE)
            factor = a_ref[rows, own]
            if after < size:
                a_ref[rows, after:] = a_ref[rows, after:] - full(factor, panel)
            g_ref[rows, :] = g_ref[rows, :] - full(factor, right)


def call(body, outs, scratch=(), **cost):
    return pl.pallas_call(
        body,
        out_shape=outs,
        scratch_shapes=list(scratch),
        compiler_params=pltpu.CompilerParams(vmem_limit_bytes=VMEM_LIMIT),
        **cost,
    )


def solve_body(a_ref, r_ref, g_ref, a_work):
    a_work[...] = a_ref[...]
    g_ref[...] = r_ref[...]
    eliminate(a_work, g_ref, range(a_ref.shape[0] // TILE))


def solve(a, r):
    return call(
        solve_body, jax.ShapeDtypeStruct(r.shape, F32), [pltpu.VMEM(a.shape, F32)]
    )(a, r)


def first_body(
    half, steps, t_ref, diag_ref, near_ref, near_side, far_ref, far_side, other_ref, column_ref, row_ref, first_ref, a_out, g_out, p_out, m_work
):
    n = 2 * half
    q = half // 2
    width = t_ref.shape[1] - n
    mine = first_ref[0]

    def block(i, j):
        return (slice(i * q, (i + 1) * q), slice(j * q, (j + 1) * q))

    def part(ref, i):
        return ref[i * q : (i + 1) * q, :]

    def put(i, j, value):
        m_work[block(i, j)] = value
        if i != j:
            m_work[block(j, i)] = value.T

    for base, ref in ((0, near_ref), (2, far_ref)):
        put(base, base, part(ref, 0))
        put(base, base + 1, part(ref, 1))
        put(base + 1, base + 1, part(ref, 2))
    put(0, 3, part(near_side, 0))
    put(2, 1, part(far_side, 0))

    @pl.when(mine == 0)
    def _():
        put(0, 2, part(near_side, 1))
        put(3, 1, part(far_side, 1))

    @pl.when(mine != 0)
    def _():
        put(1, 3, part(near_side, 1))
        put(2, 0, part(far_side, 1))

    same = column_ref[...] == row_ref[...]
    onehot = jnp.where(same, 1.0, 0.0).astype(BF16)
    p_out[...] = onehot
    moved = pick_right(m_work[...], onehot, ((1,), (1,)))
    here = pl.ds(pl.multiple_of(width + mine * half, half), half)
    there = pl.ds(pl.multiple_of(width + (1 - mine) * half, half), half)
    a_out[0:half, 0:half] = t_ref[:, here]
    a_out[0:half, half:n] = t_ref[:, there]
    a_out[block(2, 2)] = part(diag_ref, 0)
    a_out[block(2, 3)] = part(diag_ref, 1)
    a_out[block(3, 3)] = part(diag_ref, 2)
    for i in range(n // TILE):
        rows, later = slice(i * TILE, (i + 1) * TILE), slice(i * TILE, n)
        a_out[rows, later] = a_out[rows, later] + pick_left(onehot[rows, :], moved[:, later], ((1,), (0,)))
    g_out[0:half, :] = t_ref[:, 0:width]
    g_out[half:n, :] = other_ref[...]
    eliminate(a_out, g_out, steps)


def middle_body(steps, a_in, g_in, a_out, g_out):
    a_out[...] = a_in[...]
    g_out[...] = g_in[...]
    eliminate(a_out, g_out, steps)


def last_body(
    half, steps, a_ref, g_in, p_ref, t_ref, other_ref, ext_ref, row_ref, first_ref, own_ref, sol_ref, h_ref, a_work, g_work
):
    n = 2 * half
    mine = first_ref[0]
    a_work[...] = a_ref[...]
    g_work[...] = g_in[...]
    eliminate(a_work, g_work, steps)
    block = pl.ds(pl.multiple_of(mine * half, half), half)
    g = g_work[...]
    h_ref[...] = pick_left(p_ref[...], g_work[:, block], ((0,), (0,)))
    left = jnp.concatenate([t_ref[:, block], other_ref[:, block]], axis=0)
    own_ref[...] = ext_ref[...] - three_pass(left, g, ((0,), (0,)))
    target = lax.broadcasted_iota(jnp.int32, (half, n), 0) + mine * half
    onehot = jnp.where(row_ref[...] == target, 1.0, 0.0).astype(BF16)
    sol_ref[...] = -pick_left(onehot, g, ((1,), (0,)))


def cross_body(h_ref, *refs):
    *parts, out_ref = refs
    total, at = None, 0
    for ref in parts:
        end = at + ref.shape[0]
        term = three_pass(h_ref[at:end, :], ref[...], ((0,), (0,)))
        total, at = term if total is None else total + term, end
    out_ref[...] = -total


def pack_body(half, t_ref, first_ref, diag_ref, side_ref, outer_ref, *rest):
    *chunks, sems = rest
    q = half // 2
    width = outer_ref.shape[1]
    mine = first_ref[0]
    here, there = width + mine * half, width + (1 - mine) * half

    def cut(row, column):
        return t_ref.at[pl.ds(pl.multiple_of(row, q), q), pl.ds(pl.multiple_of(column, q), q)]

    moves = [
        (cut(0, here), diag_ref.at[0:q, :]),
        (cut(0, here + q), diag_ref.at[q : 2 * q, :]),
        (cut(q, here + q), diag_ref.at[2 * q : 3 * q, :]),
        (cut(0, there + q), side_ref.at[0:q, :]),
        (cut(mine * q, there + mine * q), side_ref.at[q : 2 * q, :]),
        (t_ref.at[:, 0:width], outer_ref),
    ]
    at = 0
    for chunk in chunks:
        moves.append((t_ref.at[at : at + chunk.shape[0], 0:width], chunk))
        at += chunk.shape[0]
    copies = [pltpu.make_async_copy(x, y, sems.at[i]) for i, (x, y) in enumerate(moves)]
    for copy in copies:
        copy.start()
    for copy in copies:
        copy.wait()


def sibling(x):
    size = lax.axis_size("leaf")
    return lax.ppermute(x, "leaf", [(i, i ^ size // 2) for i in range(size)])


def across(x):
    return lax.ppermute(x, "sib", [(0, 1), (1, 0)])


def kernel(body, outs, places, scratch=()):
    return pl.pallas_call(
        body,
        out_shape=outs,
        in_specs=[pl.BlockSpec(memory_space=place) for place in places],
        scratch_shapes=list(scratch),
        compiler_params=pltpu.CompilerParams(vmem_limit_bytes=VMEM_LIMIT),
    )


def pack(t_int, first, half, width, chunk_rows):
    f = lambda *shape: jax.ShapeDtypeStruct(shape, F32)
    q = half // 2
    outs = [f(3 * q, q), f(2 * q, q), f(half, width)] + [f(rows, width) for rows in chunk_rows]
    return pl.pallas_call(
        functools.partial(pack_body, half),
        out_shape=outs,
        in_specs=[pl.BlockSpec(memory_space=pl.ANY), pl.BlockSpec(memory_space=pltpu.SMEM)],
        out_specs=[pl.BlockSpec(memory_space=pl.ANY)] * len(outs),
        scratch_shapes=[pltpu.SemaphoreType.DMA((6 + len(chunk_rows),))],
    )(t_int, first)


def two_shards(t_int, t_ext, iface_map):
    t_int, t_ext = t_int[0], t_ext[0]
    half, n = t_int.shape[0], iface_map.shape[1]
    width = t_int.shape[1] - n
    tiles = n // TILE
    mine = lax.axis_index("sib").astype(jnp.int32)
    first = mine.reshape(1)
    diag, side, outer, chunk_a, chunk_b = pack(t_int, first, half, width, (half // 2, half // 2))
    near, near_side = sibling(diag), sibling(side)
    other_map = sibling(iface_map)
    diag_other, outer_other = across(diag), across(outer)
    near_held, diag_other = lax.optimization_barrier((near, diag_other))
    far = across(near_held)
    side_held, outer_other = lax.optimization_barrier((near_side, outer_other))
    far_side = across(side_held)
    chunk_a, chunk_b, _, _ = lax.optimization_barrier((chunk_a, chunk_b, near_held, near_side))
    near_a, near_b = sibling(chunk_a), sibling(chunk_b)
    rolled = lambda m: lax.dynamic_slice(jnp.concatenate([m, m], axis=1), (0, mine * half), (1, n))
    own_row, other_row = rolled(iface_map), rolled(other_map)

    f = lambda *shape: jax.ShapeDtypeStruct(shape, F32)
    vmem, smem = pltpu.VMEM, pltpu.SMEM
    a, g, onehot = kernel(
        functools.partial(first_body, half, range(tiles // 2)),
        (f(n, n), f(n, width), jax.ShapeDtypeStruct((n, n), BF16)),
        [vmem] * 9 + [smem],
        [pltpu.VMEM((n, n), F32)],
    )(t_int, diag_other, near, near_side, far, far_side, outer_other, own_row.reshape(n, 1), other_row, first)
    a, g, near_a = lax.optimization_barrier((a, g, near_a))
    far_a = across(near_a)
    a, g = kernel(
        functools.partial(middle_body, range(tiles // 2, tiles - 1)), (f(n, n), f(n, width)), [vmem] * 2
    )(a, g)
    a, g, near_b, far_a = lax.optimization_barrier((a, g, near_b, far_a))
    far_b = across(near_b)
    own_map, solution_op, h = kernel(
        functools.partial(last_body, half, range(tiles - 1, tiles)),
        (f(half, width), f(half, width), f(n, half)),
        [vmem] * 7 + [smem],
        [pltpu.VMEM((n, n), F32), pltpu.VMEM((n, width), F32)],
    )(a, g, onehot, t_int, outer_other, t_ext, own_row, first)
    cross_map = kernel(cross_body, f(half, width), [vmem] * 5)(h, near_a, near_b, far_a, far_b)
    return own_map[None], cross_map[None], solution_op[None]


def common_order(matrix, index_map):
    points = index_map.shape[0]
    inverse = jnp.zeros((points,), jnp.int32).at[index_map].set(jnp.arange(points, dtype=jnp.int32))
    picked = matrix[inverse]
    outer_width = matrix.shape[1] - points
    return (picked[:, :outer_width], picked[:, outer_width + inverse])


def many_shards(t_int, t_ext, iface_map):
    shard_rows = t_ext.shape[1]
    first_row = lax.axis_index("sib") * shard_rows
    near_rows, other_map = sibling((t_int, iface_map))
    own_rows = lax.all_gather(t_int, "sib", axis=1, tiled=True)
    other_rows = lax.all_gather(near_rows, "sib", axis=1, tiled=True)
    own_outer, own_iface = common_order(own_rows[0], iface_map[0])
    other_outer, other_iface = common_order(other_rows[0], other_map[0])
    g = solve(own_iface + other_iface, own_outer)
    product = lambda left, right: full(left, right, ((0,), (0,)))
    left = lax.dynamic_slice_in_dim(own_outer, first_row, shard_rows, 1)
    left_g = lax.dynamic_slice_in_dim(g, first_row, shard_rows, 1)
    own_map = t_ext - product(left, g)[None]
    cross_map = -product(left_g, other_outer)[None]
    solution_op = -lax.dynamic_slice_in_dim(g, first_row, shard_rows, 0)[None]
    return own_map, cross_map, solution_op


def solution(mesh):
    placed = P("leaf", "sib", None)
    return jax.shard_map(
        two_shards if mesh.shape["sib"] == 2 else many_shards,
        mesh=mesh,
        in_specs=(placed, placed, P("leaf", None)),
        out_specs=(placed, placed, placed),
        check_vma=False,
    )
```

```python
import functools

import jax
import jax.numpy as jnp
from jax import lax
from jax.experimental import pallas as pl
from jax.experimental.pallas import tpu as pltpu
from jax.sharding import PartitionSpec as P

F32 = jnp.float32
BF16 = jnp.bfloat16
TILE = 128
VMEM_LIMIT = 48 * 2**20


def split3(x):
    high = x.astype(BF16).astype(F32)
    rest = x - high
    middle = rest.astype(BF16).astype(F32)
    return high, middle, rest - middle


def contract(left, right, dims):
    return lax.dot_general(left, right, (dims, ((), ())), preferred_element_type=F32)


def full(left, right, dims=((1,), (0,))):
    return lax.dot_general(
        left, right, (dims, ((), ())), precision=lax.Precision.HIGHEST, preferred_element_type=F32
    )


def three_pass(left, right, dims):
    lh, rh = left.astype(BF16), right.astype(BF16)
    ll, rl = (left - lh.astype(F32)).astype(BF16), (right - rh.astype(F32)).astype(BF16)
    return contract(lh, rh, dims) + (contract(lh, rl, dims) + contract(ll, rh, dims))


def pick_left(onehot, x, dims):
    high, middle, low = (part.astype(BF16) for part in split3(x))
    return contract(onehot, high, dims) + (contract(onehot, middle, dims) + contract(onehot, low, dims))


def pick_right(x, onehot, dims):
    high, middle, low = (part.astype(BF16) for part in split3(x))
    return contract(high, onehot, dims) + (contract(middle, onehot, dims) + contract(low, onehot, dims))


def over_lanes(x, lane):
    return jnp.broadcast_to(x[:, lane : lane + 1], (8, TILE))


def over_rows(x, row):
    return jnp.broadcast_to(x[row : row + 1, :], (8, TILE))


def reciprocal(d):
    r = pltpu.reciprocal(d, approx=True)
    return r * (2.0 - d * r)


def invert_tile(work, slabs=2):
    width = 8 * slabs
    lane = lax.broadcasted_iota(jnp.int32, (8, TILE), 1)
    row = lax.broadcasted_iota(jnp.int32, (8, TILE), 0)
    lane_all = lax.broadcasted_iota(jnp.int32, (TILE, TILE), 1)
    is_row = [row == j for j in range(8)]
    for base in range(0, TILE, width):
        old = [work[base + 8 * s : base + 8 * s + 8, :] for s in range(slabs)]
        columns = [[over_lanes(old[s], base + m) for s in range(slabs)] for m in range(width)]
        inside = (lane >= base) & (lane < base + width)
        new = [
            jnp.where(inside, jnp.where(lane - base - 8 * s == row, 1.0, 0.0).astype(F32), old[s])
            for s in range(slabs)
        ]
        pivot = over_rows(columns[0][0], 0)
        for j in range(width):
            js, jr = divmod(j, 8)
            inverse = reciprocal(pivot)
            here = columns[j]
            scaled = [c * inverse for c in here]
            for m in range(j + 1, width):
                picked = over_rows(columns[m][js], jr)
                if m == j + 1:
                    later = [columns[m][s] - (here[s] * picked) * inverse for s in range(slabs)]
                    pivot = over_rows(later[m // 8], m % 8)
                else:
                    later = [columns[m][s] - scaled[s] * picked for s in range(slabs)]
                later[js] = jnp.where(is_row[jr], picked * inverse, later[js])
                columns[m] = later
            picked = over_rows(new[js], jr)
            later = [new[s] - scaled[s] * picked for s in range(slabs)]
            later[js] = jnp.where(is_row[jr], picked * inverse, later[js])
            new = later
        panel = jnp.concatenate(new, axis=0)
        sign = jnp.where(lane < base, -1.0, jnp.where(inside, 0.0, 1.0)).astype(F32)
        ah, am, al = split3(jnp.concatenate([x * sign for x in old], axis=0))
        bh, bm, bl = split3(panel)
        left = jnp.concatenate([ah, ah, am, am, ah, al], axis=0).astype(BF16)
        right = jnp.concatenate([bh, bm, bh, bm, bl, bh], axis=0).astype(BF16)
        change = contract(left, right, ((0,), (0,)))
        inside_all = (lane_all >= base) & (lane_all < base + width)
        rest = jnp.where(inside_all, 0.0, work) - change
        work = jnp.concatenate(
            [x for x in (rest[:base], panel, rest[base + width :]) if x.shape[0]], axis=0
        )
    return work


def eliminate(a_ref, g_ref, steps):
    size = a_ref.shape[0]
    for k in steps:
        at, after = k * TILE, (k + 1) * TILE
        own = slice(at, after)
        inverse = invert_tile(a_ref[own, own])
        right = full(inverse, g_ref[own, :])
        g_ref[own, :] = right
        if after < size:
            old = a_ref[own, after:]
            panel = full(inverse, old)
            a_ref[own, after:] = panel
        for i in range(k + 1, size // TILE):
            rows = slice(i * TILE, (i + 1) * TILE)
            factor = old[:, (i - k - 1) * TILE : (i - k) * TILE]
            a_ref[rows, i * TILE :] = a_ref[rows, i * TILE :] - full(
                factor, panel[:, (i - k - 1) * TILE :], ((0,), (0,))
            )
            g_ref[rows, :] = g_ref[rows, :] - full(factor, right, ((0,), (0,)))
        for i in range(k):
            rows = slice(i * TILE, (i + 1) * TILE)
            factor = a_ref[rows, own]
            if after < size:
                a_ref[rows, after:] = a_ref[rows, after:] - full(factor, panel)
            g_ref[rows, :] = g_ref[rows, :] - full(factor, right)


def call(body, outs, scratch=(), **cost):
    return pl.pallas_call(
        body,
        out_shape=outs,
        scratch_shapes=list(scratch),
        compiler_params=pltpu.CompilerParams(vmem_limit_bytes=VMEM_LIMIT),
        **cost,
    )


def solve_body(a_ref, r_ref, g_ref, a_work):
    a_work[...] = a_ref[...]
    g_ref[...] = r_ref[...]
    eliminate(a_work, g_ref, range(a_ref.shape[0] // TILE))


def solve(a, r):
    return call(
        solve_body, jax.ShapeDtypeStruct(r.shape, F32), [pltpu.VMEM(a.shape, F32)]
    )(a, r)


def first_body(
    half, steps, t_ref, diag_ref, near_ref, near_side, far_ref, far_side, other_ref, column_ref, row_ref, first_ref, a_out, g_out, p_out, m_work
):
    n = 2 * half
    q = half // 2
    width = t_ref.shape[1] - n
    mine = first_ref[0]

    def block(i, j):
        return (slice(i * q, (i + 1) * q), slice(j * q, (j + 1) * q))

    def part(ref, i):
        return ref[i * q : (i + 1) * q, :]

    def put(i, j, value):
        m_work[block(i, j)] = value
        if i != j:
            m_work[block(j, i)] = value.T

    for base, ref in ((0, near_ref), (2, far_ref)):
        put(base, base, part(ref, 0))
        put(base, base + 1, part(ref, 1))
        put(base + 1, base + 1, part(ref, 2))
    put(0, 3, part(near_side, 0))
    put(2, 1, part(far_side, 0))

    @pl.when(mine == 0)
    def _():
        put(0, 2, part(near_side, 1))
        put(3, 1, part(far_side, 1))

    @pl.when(mine != 0)
    def _():
        put(1, 3, part(near_side, 1))
        put(2, 0, part(far_side, 1))

    same = column_ref[...] == row_ref[...]
    onehot = jnp.where(same, 1.0, 0.0).astype(BF16)
    p_out[...] = onehot
    moved = pick_right(m_work[...], onehot, ((1,), (1,)))
    here = pl.ds(pl.multiple_of(width + mine * half, half), half)
    there = pl.ds(pl.multiple_of(width + (1 - mine) * half, half), half)
    a_out[0:half, 0:half] = t_ref[:, here]
    a_out[0:half, half:n] = t_ref[:, there]
    a_out[block(2, 2)] = part(diag_ref, 0)
    a_out[block(2, 3)] = part(diag_ref, 1)
    a_out[block(3, 3)] = part(diag_ref, 2)
    for i in range(n // TILE):
        rows, later = slice(i * TILE, (i + 1) * TILE), slice(i * TILE, n)
        a_out[rows, later] = a_out[rows, later] + pick_left(onehot[rows, :], moved[:, later], ((1,), (0,)))
    g_out[0:half, :] = t_ref[:, 0:width]
    g_out[half:n, :] = other_ref[...]
    eliminate(a_out, g_out, steps)


def middle_body(steps, a_in, g_in, a_out, g_out):
    a_out[...] = a_in[...]
    g_out[...] = g_in[...]
    eliminate(a_out, g_out, steps)


def last_body(
    half, steps, a_ref, g_in, p_ref, t_ref, other_ref, ext_ref, row_ref, first_ref, own_ref, sol_ref, h_ref, a_work, g_work
):
    n = 2 * half
    mine = first_ref[0]
    a_work[...] = a_ref[...]
    g_work[...] = g_in[...]
    eliminate(a_work, g_work, steps)
    block = pl.ds(pl.multiple_of(mine * half, half), half)
    g = g_work[...]
    h_ref[...] = pick_left(p_ref[...], g_work[:, block], ((0,), (0,)))
    left = jnp.concatenate([t_ref[:, block], other_ref[:, block]], axis=0)
    own_ref[...] = ext_ref[...] - three_pass(left, g, ((0,), (0,)))
    target = lax.broadcasted_iota(jnp.int32, (half, n), 0) + mine * half
    onehot = jnp.where(row_ref[...] == target, 1.0, 0.0).astype(BF16)
    sol_ref[...] = -pick_left(onehot, g, ((1,), (0,)))


def cross_body(h_ref, *refs):
    *parts, out_ref = refs
    total, at = None, 0
    for ref in parts:
        end = at + ref.shape[0]
        term = three_pass(h_ref[at:end, :], ref[...], ((0,), (0,)))
        total, at = term if total is None else total + term, end
    out_ref[...] = -total


def pack_body(half, t_ref, first_ref, diag_ref, side_ref, outer_ref, *rest):
    chunks = rest
    q = half // 2
    width = outer_ref.shape[1]
    mine = first_ref[0]
    here, there = width + mine * half, width + (1 - mine) * half

    def cut(row, column):
        return t_ref.at[pl.ds(pl.multiple_of(row, q), q), pl.ds(pl.multiple_of(column, q), q)]

    moves = [
        (cut(0, here), diag_ref.at[0:q, :]),
        (cut(0, here + q), diag_ref.at[q : 2 * q, :]),
        (cut(q, here + q), diag_ref.at[2 * q : 3 * q, :]),
        (cut(0, there + q), side_ref.at[0:q, :]),
        (cut(mine * q, there + mine * q), side_ref.at[q : 2 * q, :]),
        (t_ref.at[:, 0:width], outer_ref),
    ]
    at = 0
    for chunk in chunks:
        moves.append((t_ref.at[at : at + chunk.shape[0], 0:width], chunk))
        at += chunk.shape[0]
    for source, target in moves:
        target[...] = source[...]


def sibling(x):
    size = lax.axis_size("leaf")
    return lax.ppermute(x, "leaf", [(i, i ^ size // 2) for i in range(size)])


def across(x):
    return lax.ppermute(x, "sib", [(0, 1), (1, 0)])


def kernel(body, outs, places, scratch=()):
    return pl.pallas_call(
        body,
        out_shape=outs,
        in_specs=[pl.BlockSpec(memory_space=place) for place in places],
        scratch_shapes=list(scratch),
        compiler_params=pltpu.CompilerParams(vmem_limit_bytes=VMEM_LIMIT),
    )


def pack(t_int, first, half, width, chunk_rows):
    f = lambda *shape: jax.ShapeDtypeStruct(shape, F32)
    q = half // 2
    outs = [f(3 * q, q), f(2 * q, q), f(half, width)] + [f(rows, width) for rows in chunk_rows]
    return kernel(functools.partial(pack_body, half), outs, [pltpu.VMEM, pltpu.SMEM])(t_int, first)


def two_shards(t_int, t_ext, iface_map):
    t_int, t_ext = t_int[0], t_ext[0]
    half, n = t_int.shape[0], iface_map.shape[1]
    width = t_int.shape[1] - n
    tiles = n // TILE
    mine = lax.axis_index("sib").astype(jnp.int32)
    first = mine.reshape(1)
    diag, side, outer, chunk_a, chunk_b = pack(t_int, first, half, width, (half // 2, half // 2))
    near, near_side = sibling(diag), sibling(side)
    other_map = sibling(iface_map)
    diag_other, outer_other = across(diag), across(outer)
    near_held, diag_other = lax.optimization_barrier((near, diag_other))
    far = across(near_held)
    side_held, outer_other = lax.optimization_barrier((near_side, outer_other))
    far_side = across(side_held)
    chunk_a, chunk_b, _, _, other_map = lax.optimization_barrier(
        (chunk_a, chunk_b, near_held, near_side, other_map)
    )
    near_a, near_b = sibling(chunk_a), sibling(chunk_b)
    rolled = lambda m: lax.dynamic_slice(jnp.concatenate([m, m], axis=1), (0, mine * half), (1, n))
    own_row, other_row = rolled(iface_map), rolled(other_map)

    f = lambda *shape: jax.ShapeDtypeStruct(shape, F32)
    vmem, smem = pltpu.VMEM, pltpu.SMEM
    a, g, onehot = kernel(
        functools.partial(first_body, half, range(tiles // 2)),
        (f(n, n), f(n, width), jax.ShapeDtypeStruct((n, n), BF16)),
        [vmem] * 9 + [smem],
        [pltpu.VMEM((n, n), F32)],
    )(t_int, diag_other, near, near_side, far, far_side, outer_other, own_row.reshape(n, 1), other_row, first)
    a, g, near_a = lax.optimization_barrier((a, g, near_a))
    far_a = across(near_a)
    a, g = kernel(
        functools.partial(middle_body, range(tiles // 2, tiles - 1)), (f(n, n), f(n, width)), [vmem] * 2
    )(a, g)
    a, g, near_b, far_a = lax.optimization_barrier((a, g, near_b, far_a))
    far_b = across(near_b)
    own_map, solution_op, h = kernel(
        functools.partial(last_body, half, range(tiles - 1, tiles)),
        (f(half, width), f(half, width), f(n, half)),
        [vmem] * 7 + [smem],
        [pltpu.VMEM((n, n), F32), pltpu.VMEM((n, width), F32)],
    )(a, g, onehot, t_int, outer_other, t_ext, own_row, first)
    cross_map = kernel(cross_body, f(half, width), [vmem] * 5)(h, near_a, near_b, far_a, far_b)
    return own_map[None], cross_map[None], solution_op[None]


def common_order(matrix, index_map):
    points = index_map.shape[0]
    inverse = jnp.zeros((points,), jnp.int32).at[index_map].set(jnp.arange(points, dtype=jnp.int32))
    picked = matrix[inverse]
    outer_width = matrix.shape[1] - points
    return (picked[:, :outer_width], picked[:, outer_width + inverse])


def many_shards(t_int, t_ext, iface_map):
    shard_rows = t_ext.shape[1]
    first_row = lax.axis_index("sib") * shard_rows
    near_rows, other_map = sibling((t_int, iface_map))
    own_rows = lax.all_gather(t_int, "sib", axis=1, tiled=True)
    other_rows = lax.all_gather(near_rows, "sib", axis=1, tiled=True)
    own_outer, own_iface = common_order(own_rows[0], iface_map[0])
    other_outer, other_iface = common_order(other_rows[0], other_map[0])
    g = solve(own_iface + other_iface, own_outer)
    product = lambda left, right: full(left, right, ((0,), (0,)))
    left = lax.dynamic_slice_in_dim(own_outer, first_row, shard_rows, 1)
    left_g = lax.dynamic_slice_in_dim(g, first_row, shard_rows, 1)
    own_map = t_ext - product(left, g)[None]
    cross_map = -product(left_g, other_outer)[None]
    solution_op = -lax.dynamic_slice_in_dim(g, first_row, shard_rows, 0)[None]
    return own_map, cross_map, solution_op


def solution(mesh):
    placed = P("leaf", "sib", None)
    return jax.shard_map(
        two_shards if mesh.shape["sib"] == 2 else many_shards,
        mesh=mesh,
        in_specs=(placed, placed, P("leaf", None)),
        out_specs=(placed, placed, placed),
        check_vma=False,
    )
```

```python
import functools

import jax
import jax.numpy as jnp
from jax import lax
from jax.experimental import pallas as pl
from jax.experimental.pallas import tpu as pltpu
from jax.sharding import PartitionSpec as P

F32 = jnp.float32
BF16 = jnp.bfloat16
TILE = 128
VMEM_LIMIT = 48 * 2**20


def split3(x):
    high = x.astype(BF16).astype(F32)
    rest = x - high
    middle = rest.astype(BF16).astype(F32)
    return high, middle, rest - middle


def contract(left, right, dims):
    return lax.dot_general(left, right, (dims, ((), ())), preferred_element_type=F32)


def full(left, right, dims=((1,), (0,))):
    return lax.dot_general(
        left, right, (dims, ((), ())), precision=lax.Precision.HIGHEST, preferred_element_type=F32
    )


def three_pass(left, right, dims):
    lh, rh = left.astype(BF16), right.astype(BF16)
    ll, rl = (left - lh.astype(F32)).astype(BF16), (right - rh.astype(F32)).astype(BF16)
    return contract(lh, rh, dims) + (contract(lh, rl, dims) + contract(ll, rh, dims))


def pick_left(onehot, x, dims):
    high, middle, low = (part.astype(BF16) for part in split3(x))
    return contract(onehot, high, dims) + (contract(onehot, middle, dims) + contract(onehot, low, dims))


def pick_right(x, onehot, dims):
    high, middle, low = (part.astype(BF16) for part in split3(x))
    return contract(high, onehot, dims) + (contract(middle, onehot, dims) + contract(low, onehot, dims))


def over_lanes(x, lane):
    return jnp.broadcast_to(x[:, lane : lane + 1], (8, TILE))


def over_rows(x, row):
    return jnp.broadcast_to(x[row : row + 1, :], (8, TILE))


def invert_tile(work, slabs=2):
    width = 8 * slabs
    lane = lax.broadcasted_iota(jnp.int32, (8, TILE), 1)
    row = lax.broadcasted_iota(jnp.int32, (8, TILE), 0)
    lane_all = lax.broadcasted_iota(jnp.int32, (TILE, TILE), 1)
    is_row = [row == j for j in range(8)]

    def slab_list(x, base):
        return [x[base + 8 * s : base + 8 * s + 8, :] for s in range(slabs)]

    old = slab_list(work, 0)
    for base in range(0, TILE, width):
        after = base + width
        columns = [[over_lanes(x, base + m) for x in old] for m in range(width)]
        following = slab_list(work, after) if after < TILE else []
        factors = [[over_lanes(x, base + m) for x in following] for m in range(width)]
        inside = (lane >= base) & (lane < after)
        new = [
            jnp.where(inside, jnp.where(lane - base - 8 * s == row, 1.0, 0.0).astype(F32), old[s])
            for s in range(slabs)
        ]
        pivot = over_rows(columns[0][0], 0)
        scale = [None] * slabs
        for j in range(width):
            js, jr = divmod(j, 8)
            inverse = pltpu.reciprocal(pivot, approx=True)
            scale[js] = inverse if jr == 0 else jnp.where(is_row[jr], inverse, scale[js])
            here = list(columns[j])
            here[js] = jnp.where(is_row[jr], 0.0, here[js])
            scaled = [c * inverse for c in here]
            for m in range(j + 1, width):
                picked = over_rows(columns[m][js], jr)
                if m == j + 1:
                    columns[m] = [c - (h * picked) * inverse for c, h in zip(columns[m], here)]
                    pivot = over_rows(columns[m][m // 8], m % 8)
                else:
                    columns[m] = [c - h * picked for c, h in zip(columns[m], scaled)]
            picked = over_rows(new[js], jr)
            new = [x - h * picked for x, h in zip(new, scaled)]
        new = [x * y for x, y in zip(new, scale)]
        panel = jnp.concatenate(new, axis=0)
        sign = jnp.where(lane < base, -1.0, jnp.where(inside, 0.0, 1.0)).astype(F32)
        ah, am, al = split3(jnp.concatenate([x * sign for x in old], axis=0))
        bh, bm, bl = split3(panel)
        left = jnp.concatenate([ah, ah, am, am, ah, al], axis=0).astype(BF16)
        right = jnp.concatenate([bh, bm, bh, bm, bl, bh], axis=0).astype(BF16)
        change = contract(left, right, ((0,), (0,)))
        inside_all = (lane_all >= base) & (lane_all < after)
        rest = jnp.where(inside_all, 0.0, work) - change
        parts = [rest[:base], panel, rest[after:]]
        if following:
            rows = [over_rows(new[m // 8], m % 8) for m in range(width)]
            old = []
            for s in range(slabs):
                sums = []
                for q in range(4):
                    terms = [factors[m][s] * rows[m] for m in range(q, width, 4)]
                    sums.append(functools.reduce(lambda x, y: x + y, terms))
                old.append(jnp.where(inside, 0.0, following[s]) - ((sums[0] + sums[1]) + (sums[2] + sums[3])))
            parts = [rest[:base], panel, *old, rest[after + width :]]
        work = jnp.concatenate([x for x in parts if x.shape[0]], axis=0)
    return work


def eliminate(a_ref, g_ref, steps):
    size, rows_of_g = a_ref.shape[0], g_ref.shape[0]
    for k in steps:
        at, after = k * TILE, (k + 1) * TILE
        own = slice(at, after)
        inverse = invert_tile(a_ref[own, own])
        right = full(inverse, g_ref[own, :])
        g_ref[own, :] = right
        if after < size:
            old = a_ref[own, after:]
            panel = full(inverse, old)
            a_ref[own, after:] = panel
        for i in range(k + 1, size // TILE):
            rows = slice(i * TILE, (i + 1) * TILE)
            factor = old[:, (i - k - 1) * TILE : (i - k) * TILE]
            a_ref[rows, i * TILE :] = a_ref[rows, i * TILE :] - full(
                factor, panel[:, (i - k - 1) * TILE :], ((0,), (0,))
            )
            if (i + 1) * TILE <= rows_of_g:
                g_ref[rows, :] = g_ref[rows, :] - full(factor, right, ((0,), (0,)))
        for i in range(k):
            rows = slice(i * TILE, (i + 1) * TILE)
            factor = a_ref[rows, own]
            if after < size:
                a_ref[rows, after:] = a_ref[rows, after:] - full(factor, panel)
            g_ref[rows, :] = g_ref[rows, :] - full(factor, right)


def call(body, outs, scratch=(), **cost):
    return pl.pallas_call(
        body,
        out_shape=outs,
        scratch_shapes=list(scratch),
        compiler_params=pltpu.CompilerParams(vmem_limit_bytes=VMEM_LIMIT),
        **cost,
    )


def solve_body(a_ref, r_ref, g_ref, a_work):
    a_work[...] = a_ref[...]
    g_ref[...] = r_ref[...]
    eliminate(a_work, g_ref, range(a_ref.shape[0] // TILE))


def solve(a, r):
    return call(
        solve_body, jax.ShapeDtypeStruct(r.shape, F32), [pltpu.VMEM(a.shape, F32)]
    )(a, r)


def first_body(
    half, steps, t_ref, diag_ref, near_ref, near_side, far_ref, far_side, column_ref, row_ref, first_ref, a_out, b_out, p_out, m_work
):
    n = 2 * half
    q = half // 2
    width = t_ref.shape[1] - n
    mine = first_ref[0]

    def block(i, j):
        return (slice(i * q, (i + 1) * q), slice(j * q, (j + 1) * q))

    def part(ref, i):
        return ref[i * q : (i + 1) * q, :]

    def put(i, j, value):
        m_work[block(i, j)] = value
        if i != j:
            m_work[block(j, i)] = value.T

    for base, ref in ((0, near_ref), (2, far_ref)):
        put(base, base, part(ref, 0))
        put(base, base + 1, part(ref, 1))
        put(base + 1, base + 1, part(ref, 2))
    put(0, 3, part(near_side, 0))
    put(2, 1, part(far_side, 0))

    @pl.when(mine == 0)
    def _():
        put(0, 2, part(near_side, 1))
        put(3, 1, part(far_side, 1))

    @pl.when(mine != 0)
    def _():
        put(1, 3, part(near_side, 1))
        put(2, 0, part(far_side, 1))

    same = column_ref[...] == row_ref[...]
    onehot = jnp.where(same, 1.0, 0.0).astype(BF16)
    p_out[...] = onehot
    moved = pick_right(m_work[...], onehot, ((1,), (1,)))
    here = pl.ds(pl.multiple_of(width + mine * half, half), half)
    there = pl.ds(pl.multiple_of(width + (1 - mine) * half, half), half)
    a_out[0:half, 0:half] = t_ref[:, here]
    a_out[0:half, half:n] = t_ref[:, there]
    a_out[block(2, 2)] = part(diag_ref, 0)
    a_out[block(2, 3)] = part(diag_ref, 1)
    a_out[block(3, 3)] = part(diag_ref, 2)
    for i in range(n // TILE):
        rows, later = slice(i * TILE, (i + 1) * TILE), slice(i * TILE, n)
        a_out[rows, later] = a_out[rows, later] + pick_left(onehot[rows, :], moved[:, later], ((1,), (0,)))
    top = b_out.shape[0]
    on_diagonal = [lax.broadcasted_iota(jnp.int32, (top, top), axis) for axis in (0, 1)]
    b_out[...] = jnp.where(on_diagonal[0] == on_diagonal[1], 1.0, 0.0).astype(F32)
    eliminate(a_out, b_out, steps)


def middle_body(steps, a_in, b_ref, upper_ref, lower_ref, a_out, g_out):
    top, half = b_ref.shape[0], upper_ref.shape[0]
    a_out[...] = a_in[...]
    g_out[0:half, :] = upper_ref[...]
    g_out[half:, :] = lower_ref[...]
    first = g_out[0:top, :]
    g_out[top:, :] = g_out[top:, :] - full(a_in[0:top, top:], first, ((0,), (0,)))
    g_out[0:top, :] = full(b_ref[...], first)
    eliminate(a_out, g_out, steps)


def last_body(
    half, steps, a_ref, g_in, p_ref, t_ref, other_ref, ext_ref, row_ref, first_ref, own_ref, sol_ref, h_ref, a_work, g_work
):
    n = 2 * half
    mine = first_ref[0]
    a_work[...] = a_ref[...]
    g_work[...] = g_in[...]
    eliminate(a_work, g_work, steps)
    block = pl.ds(pl.multiple_of(mine * half, half), half)
    g = g_work[...]
    h_ref[...] = pick_left(p_ref[...], g_work[:, block], ((0,), (0,)))
    left = jnp.concatenate([t_ref[:, block], other_ref[:, block]], axis=0)
    own_ref[...] = ext_ref[...] - three_pass(left, g, ((0,), (0,)))
    target = lax.broadcasted_iota(jnp.int32, (half, n), 0) + mine * half
    onehot = jnp.where(row_ref[...] == target, 1.0, 0.0).astype(BF16)
    sol_ref[...] = -pick_left(onehot, g, ((1,), (0,)))


def cross_body(h_ref, *refs):
    *parts, out_ref = refs
    total, at = None, 0
    for ref in parts:
        end = at + ref.shape[0]
        term = three_pass(h_ref[at:end, :], ref[...], ((0,), (0,)))
        total, at = term if total is None else total + term, end
    out_ref[...] = -total


def pack_iface_body(half, width, t_ref, first_ref, diag_ref, side_ref):
    q = half // 2
    mine = first_ref[0]
    here, there = width + mine * half, width + (1 - mine) * half

    def cut(row, column):
        return t_ref[pl.ds(pl.multiple_of(row, q), q), pl.ds(pl.multiple_of(column, q), q)]

    diag_ref[0:q, :] = cut(0, here)
    diag_ref[q : 2 * q, :] = cut(0, here + q)
    diag_ref[2 * q : 3 * q, :] = cut(q, here + q)
    side_ref[0:q, :] = cut(0, there + q)
    side_ref[q : 2 * q, :] = cut(mine * q, there + mine * q)


def pack_outer_body(t_ref, outer_ref, *chunks):
    width = outer_ref.shape[1]
    outer_ref[...] = t_ref[:, 0:width]
    at = 0
    for chunk in chunks:
        chunk[...] = t_ref[at : at + chunk.shape[0], 0:width]
        at += chunk.shape[0]


def sibling(x):
    size = lax.axis_size("leaf")
    return lax.ppermute(x, "leaf", [(i, i ^ size // 2) for i in range(size)])


def across(x):
    return lax.ppermute(x, "sib", [(0, 1), (1, 0)])


def kernel(body, outs, places, scratch=(), flops=1e8):
    return pl.pallas_call(
        body,
        out_shape=outs,
        in_specs=[pl.BlockSpec(memory_space=place) for place in places],
        scratch_shapes=list(scratch),
        compiler_params=pltpu.CompilerParams(vmem_limit_bytes=VMEM_LIMIT),
        cost_estimate=pl.CostEstimate(flops=int(flops), bytes_accessed=1 << 20, transcendentals=0),
    )


def two_shards(t_int, t_ext, iface_map):
    t_int, t_ext = t_int[0], t_ext[0]
    half, n = t_int.shape[0], iface_map.shape[1]
    width = t_int.shape[1] - n
    tiles = n // TILE
    q = half // 2
    f = lambda *shape: jax.ShapeDtypeStruct(shape, F32)
    vmem, smem = pltpu.VMEM, pltpu.SMEM
    mine = lax.axis_index("sib").astype(jnp.int32)
    first = mine.reshape(1)
    diag, side = kernel(
        functools.partial(pack_iface_body, half, width), (f(3 * q, q), f(2 * q, q)), [vmem, smem]
    )(t_int, first)
    near, near_side = sibling(diag), sibling(side)
    other_map = sibling(iface_map)
    diag_other = across(diag)
    far = across(near)
    near_side, near = lax.optimization_barrier((near_side, near))
    far_side = across(near_side)
    outer, chunk_a, chunk_b = kernel(pack_outer_body, (f(half, width), f(q, width), f(q, width)), [vmem])(t_int)
    outer_late, _ = lax.optimization_barrier((outer, far))
    outer_other = across(outer_late)
    chunk_a, chunk_b, _, _, other_map = lax.optimization_barrier((chunk_a, chunk_b, near, near_side, other_map))
    near_a, near_b = sibling(chunk_a), sibling(chunk_b)
    rolled = lambda m: lax.dynamic_slice(jnp.concatenate([m, m], axis=1), (0, mine * half), (1, n))
    own_row, other_row = rolled(iface_map), rolled(other_map)

    top = tiles // 2 * TILE
    a, b, onehot = kernel(
        functools.partial(first_body, half, range(tiles // 2)),
        (f(n, n), f(top, top), jax.ShapeDtypeStruct((n, n), BF16)),
        [vmem] * 8 + [smem],
        [pltpu.VMEM((n, n), F32)],
        10e9,
    )(t_int, diag_other, near, near_side, far, far_side, own_row.reshape(n, 1), other_row, first)
    a, b, near_a = lax.optimization_barrier((a, b, near_a))
    far_a = across(near_a)
    a, g = kernel(
        functools.partial(middle_body, range(tiles // 2, tiles - 1)), (f(n, n), f(n, width)), [vmem] * 4, (), 5e9
    )(a, b, outer, outer_other)
    a, g, near_b, far_a = lax.optimization_barrier((a, g, near_b, far_a))
    far_b = across(near_b)
    own_map, solution_op, h = kernel(
        functools.partial(last_body, half, range(tiles - 1, tiles)),
        (f(half, width), f(half, width), f(n, half)),
        [vmem] * 7 + [smem],
        [pltpu.VMEM((n, n), F32), pltpu.VMEM((n, width), F32)],
        7e9,
    )(a, g, onehot, t_int, outer_other, t_ext, own_row, first)
    cross_map = kernel(cross_body, f(half, width), [vmem] * 5)(h, near_a, near_b, far_a, far_b)
    return own_map[None], cross_map[None], solution_op[None]


def common_order(matrix, index_map):
    points = index_map.shape[0]
    inverse = jnp.zeros((points,), jnp.int32).at[index_map].set(jnp.arange(points, dtype=jnp.int32))
    picked = matrix[inverse]
    outer_width = matrix.shape[1] - points
    return (picked[:, :outer_width], picked[:, outer_width + inverse])


def many_shards(t_int, t_ext, iface_map):
    shard_rows = t_ext.shape[1]
    first_row = lax.axis_index("sib") * shard_rows
    near_rows, other_map = sibling((t_int, iface_map))
    own_rows = lax.all_gather(t_int, "sib", axis=1, tiled=True)
    other_rows = lax.all_gather(near_rows, "sib", axis=1, tiled=True)
    own_outer, own_iface = common_order(own_rows[0], iface_map[0])
    other_outer, other_iface = common_order(other_rows[0], other_map[0])
    g = solve(own_iface + other_iface, own_outer)
    product = lambda left, right: full(left, right, ((0,), (0,)))
    left = lax.dynamic_slice_in_dim(own_outer, first_row, shard_rows, 1)
    left_g = lax.dynamic_slice_in_dim(g, first_row, shard_rows, 1)
    own_map = t_ext - product(left, g)[None]
    cross_map = -product(left_g, other_outer)[None]
    solution_op = -lax.dynamic_slice_in_dim(g, first_row, shard_rows, 0)[None]
    return own_map, cross_map, solution_op


def solution(mesh):
    placed = P("leaf", "sib", None)
    return jax.shard_map(
        two_shards if mesh.shape["sib"] == 2 else many_shards,
        mesh=mesh,
        in_specs=(placed, placed, P("leaf", None)),
        out_specs=(placed, placed, placed),
        check_vma=False,
    )
```

```python
import functools

import jax
import jax.numpy as jnp
from jax import lax
from jax.experimental import pallas as pl
from jax.experimental.pallas import tpu as pltpu
from jax.sharding import PartitionSpec as P

F32 = jnp.float32
BF16 = jnp.bfloat16
TILE = 128
CHUNKS = 4
VMEM_LIMIT = 48 * 2**20


def split3(x):
    high = x.astype(BF16).astype(F32)
    rest = x - high
    middle = rest.astype(BF16).astype(F32)
    return high, middle, rest - middle


def contract(left, right, dims):
    return lax.dot_general(left, right, (dims, ((), ())), preferred_element_type=F32)


def full(left, right, dims=((1,), (0,))):
    return lax.dot_general(
        left, right, (dims, ((), ())), precision=lax.Precision.HIGHEST, preferred_element_type=F32
    )


def three_pass(left, right, dims):
    lh, rh = left.astype(BF16), right.astype(BF16)
    ll, rl = (left - lh.astype(F32)).astype(BF16), (right - rh.astype(F32)).astype(BF16)
    return contract(lh, rh, dims) + (contract(lh, rl, dims) + contract(ll, rh, dims))


def pick_left(onehot, x, dims):
    high, middle, low = (part.astype(BF16) for part in split3(x))
    return contract(onehot, high, dims) + (contract(onehot, middle, dims) + contract(onehot, low, dims))


def pick_right(x, onehot, dims):
    high, middle, low = (part.astype(BF16) for part in split3(x))
    return contract(high, onehot, dims) + (contract(middle, onehot, dims) + contract(low, onehot, dims))


def over_lanes(x, lane):
    return jnp.broadcast_to(x[:, lane : lane + 1], (8, TILE))


def over_rows(x, row):
    return jnp.broadcast_to(x[row : row + 1, :], (8, TILE))


def invert_tile(work, slabs=2):
    width = 8 * slabs
    lane = lax.broadcasted_iota(jnp.int32, (8, TILE), 1)
    row = lax.broadcasted_iota(jnp.int32, (8, TILE), 0)
    lane_all = lax.broadcasted_iota(jnp.int32, (TILE, TILE), 1)
    is_row = [row == j for j in range(8)]

    def slab_list(x, base):
        return [x[base + 8 * s : base + 8 * s + 8, :] for s in range(slabs)]

    old = slab_list(work, 0)
    for base in range(0, TILE, width):
        after = base + width
        columns = [[over_lanes(x, base + m) for x in old] for m in range(width)]
        following = slab_list(work, after) if after < TILE else []
        factors = [[over_lanes(x, base + m) for x in following] for m in range(width)]
        inside = (lane >= base) & (lane < after)
        new = [
            jnp.where(inside, jnp.where(lane - base - 8 * s == row, 1.0, 0.0).astype(F32), old[s])
            for s in range(slabs)
        ]
        pivot = over_rows(columns[0][0], 0)
        scale = [None] * slabs
        for j in range(width):
            js, jr = divmod(j, 8)
            inverse = pltpu.reciprocal(pivot, approx=True)
            scale[js] = inverse if jr == 0 else jnp.where(is_row[jr], inverse, scale[js])
            here = list(columns[j])
            here[js] = jnp.where(is_row[jr], 0.0, here[js])
            scaled = [c * inverse for c in here]
            for m in range(j + 1, width):
                picked = over_rows(columns[m][js], jr)
                if m == j + 1:
                    columns[m] = [c - (h * picked) * inverse for c, h in zip(columns[m], here)]
                    pivot = over_rows(columns[m][m // 8], m % 8)
                else:
                    columns[m] = [c - h * picked for c, h in zip(columns[m], scaled)]
            picked = over_rows(new[js], jr)
            new = [x - h * picked for x, h in zip(new, scaled)]
        new = [x * y for x, y in zip(new, scale)]
        panel = jnp.concatenate(new, axis=0)
        sign = jnp.where(lane < base, -1.0, jnp.where(inside, 0.0, 1.0)).astype(F32)
        ah, am, al = split3(jnp.concatenate([x * sign for x in old], axis=0))
        bh, bm, bl = split3(panel)
        left = jnp.concatenate([ah, ah, am, am, ah, al], axis=0).astype(BF16)
        right = jnp.concatenate([bh, bm, bh, bm, bl, bh], axis=0).astype(BF16)
        change = contract(left, right, ((0,), (0,)))
        inside_all = (lane_all >= base) & (lane_all < after)
        rest = jnp.where(inside_all, 0.0, work) - change
        parts = [rest[:base], panel, rest[after:]]
        if following:
            rows = [over_rows(new[m // 8], m % 8) for m in range(width)]
            old = []
            for s in range(slabs):
                sums = []
                for q in range(4):
                    terms = [factors[m][s] * rows[m] for m in range(q, width, 4)]
                    sums.append(functools.reduce(lambda x, y: x + y, terms))
                old.append(jnp.where(inside, 0.0, following[s]) - ((sums[0] + sums[1]) + (sums[2] + sums[3])))
            parts = [rest[:base], panel, *old, rest[after + width :]]
        work = jnp.concatenate([x for x in parts if x.shape[0]], axis=0)
    return work


def eliminate(a_ref, g_ref, steps):
    size, rows_of_g = a_ref.shape[0], g_ref.shape[0]
    for k in steps:
        at, after = k * TILE, (k + 1) * TILE
        own = slice(at, after)
        inverse = invert_tile(a_ref[own, own])
        right = full(inverse, g_ref[own, :])
        g_ref[own, :] = right
        if after < size:
            old = a_ref[own, after:]
            panel = full(inverse, old)
            a_ref[own, after:] = panel
        for i in range(k + 1, size // TILE):
            rows = slice(i * TILE, (i + 1) * TILE)
            factor = old[:, (i - k - 1) * TILE : (i - k) * TILE]
            a_ref[rows, i * TILE :] = a_ref[rows, i * TILE :] - full(
                factor, panel[:, (i - k - 1) * TILE :], ((0,), (0,))
            )
            if (i + 1) * TILE <= rows_of_g:
                g_ref[rows, :] = g_ref[rows, :] - full(factor, right, ((0,), (0,)))
        for i in range(k):
            rows = slice(i * TILE, (i + 1) * TILE)
            factor = a_ref[rows, own]
            if after < size:
                a_ref[rows, after:] = a_ref[rows, after:] - full(factor, panel)
            g_ref[rows, :] = g_ref[rows, :] - full(factor, right)


def call(body, outs, scratch=(), **cost):
    return pl.pallas_call(
        body,
        out_shape=outs,
        scratch_shapes=list(scratch),
        compiler_params=pltpu.CompilerParams(vmem_limit_bytes=VMEM_LIMIT),
        **cost,
    )


def solve_body(a_ref, r_ref, g_ref, a_work):
    a_work[...] = a_ref[...]
    g_ref[...] = r_ref[...]
    eliminate(a_work, g_ref, range(a_ref.shape[0] // TILE))


def solve(a, r):
    return call(
        solve_body, jax.ShapeDtypeStruct(r.shape, F32), [pltpu.VMEM(a.shape, F32)]
    )(a, r)


def first_body(
    half, steps, t_ref, diag_ref, near_ref, far_ref, column_ref, row_ref, first_ref, a_out, b_out, p_out, m_work
):
    n = 2 * half
    q = half // 2
    width = t_ref.shape[1] - n
    mine = first_ref[0]

    def block(i, j):
        return (slice(i * q, (i + 1) * q), slice(j * q, (j + 1) * q))

    def part(ref, i):
        return ref[i * q : (i + 1) * q, :]

    def put(i, j, value):
        m_work[block(i, j)] = value
        if i != j:
            m_work[block(j, i)] = value.T

    for base, ref in ((0, near_ref), (2, far_ref)):
        put(base, base, part(ref, 0))
        put(base, base + 1, part(ref, 1))
        put(base + 1, base + 1, part(ref, 2))
    put(0, 3, part(near_ref, 3))
    put(2, 1, part(far_ref, 3))

    @pl.when(mine == 0)
    def _():
        put(0, 2, part(near_ref, 4))
        put(3, 1, part(far_ref, 4))

    @pl.when(mine != 0)
    def _():
        put(1, 3, part(near_ref, 4))
        put(2, 0, part(far_ref, 4))

    same = column_ref[...] == row_ref[...]
    onehot = jnp.where(same, 1.0, 0.0).astype(BF16)
    p_out[...] = onehot
    moved = pick_right(m_work[...], onehot, ((1,), (1,)))
    here = pl.ds(pl.multiple_of(width + mine * half, half), half)
    there = pl.ds(pl.multiple_of(width + (1 - mine) * half, half), half)
    a_out[0:half, 0:half] = t_ref[:, here]
    a_out[0:half, half:n] = t_ref[:, there]
    a_out[block(2, 2)] = part(diag_ref, 0)
    a_out[block(2, 3)] = part(diag_ref, 1)
    a_out[block(3, 3)] = part(diag_ref, 2)
    for i in range(n // TILE):
        rows, later = slice(i * TILE, (i + 1) * TILE), slice(i * TILE, n)
        a_out[rows, later] = a_out[rows, later] + pick_left(onehot[rows, :], moved[:, later], ((1,), (0,)))
    top = b_out.shape[0]
    on_diagonal = [lax.broadcasted_iota(jnp.int32, (top, top), axis) for axis in (0, 1)]
    b_out[...] = jnp.where(on_diagonal[0] == on_diagonal[1], 1.0, 0.0).astype(F32)
    eliminate(a_out, b_out, steps)


def middle_body(steps, a_in, b_ref, t_ref, early_ref, late_ref, a_out, g_out, other_out):
    top, half, q = b_ref.shape[0], t_ref.shape[0], early_ref.shape[1]
    width = g_out.shape[1]
    a_out[...] = a_in[...]
    for at, rows, columns in early_blocks(3 * q, early_ref.shape[0], q, width):
        other_out[0:rows, columns] = early_ref[at : at + rows, :]
    other_out[half - late_ref.shape[0] :, :] = late_ref[...]
    g_out[0:half, :] = t_ref[:, 0:width]
    g_out[half:, :] = other_out[...]
    first = g_out[0:top, :]
    g_out[top:, :] = g_out[top:, :] - full(a_in[0:top, top:], first, ((0,), (0,)))
    g_out[0:top, :] = full(b_ref[...], first)
    eliminate(a_out, g_out, steps)


def last_body(steps, a_ref, g_in, g_out, a_work):
    a_work[...] = a_ref[...]
    g_out[...] = g_in[...]
    eliminate(a_work, g_out, steps)


def cross_terms(h_ref, at, parts):
    total = None
    for ref in parts:
        term = three_pass(h_ref[at : at + ref.shape[0], :], ref[...], ((0,), (0,)))
        total = term if total is None else total + term
        at += ref.shape[0]
    return total


def output_body(
    half, g_ref, p_ref, t_ref, other_ref, ext_ref, row_ref, first_ref, *refs
):
    *parts, own_ref, sol_ref, h_ref, cross_ref = refs
    n = 2 * half
    mine = first_ref[0]
    block = pl.ds(pl.multiple_of(mine * half, half), half)
    g = g_ref[...]
    h_ref[...] = pick_left(p_ref[...], g_ref[:, block], ((0,), (0,)))
    left = jnp.concatenate([t_ref[:, block], other_ref[:, block]], axis=0)
    own_ref[...] = ext_ref[...] - three_pass(left, g, ((0,), (0,)))
    target = lax.broadcasted_iota(jnp.int32, (half, n), 0) + mine * half
    onehot = jnp.where(row_ref[...] == target, 1.0, 0.0).astype(BF16)
    sol_ref[...] = -pick_left(onehot, g, ((1,), (0,)))
    cross_ref[...] = cross_terms(h_ref, 0, parts)


def cross_body(h_ref, partial_ref, *refs):
    *parts, out_ref = refs
    at = h_ref.shape[0] - sum(ref.shape[0] for ref in parts)
    out_ref[...] = -(partial_ref[...] + cross_terms(h_ref, at, parts))


def pack_iface_body(half, width, t_ref, first_ref, pack_ref, early_ref):
    q = half // 2
    mine = first_ref[0]
    here, there = width + mine * half, width + (1 - mine) * half

    def cut(row, column):
        return t_ref[pl.ds(pl.multiple_of(row, q), q), pl.ds(pl.multiple_of(column, q), q)]

    for ref in (pack_ref, early_ref):
        ref[0:q, :] = cut(0, here)
        ref[q : 2 * q, :] = cut(0, here + q)
        ref[2 * q : 3 * q, :] = cut(q, here + q)
    pack_ref[3 * q : 4 * q, :] = cut(0, there + q)
    pack_ref[4 * q : 5 * q, :] = cut(mine * q, there + mine * q)
    for at, rows, columns in early_blocks(3 * q, early_ref.shape[0], q, width):
        early_ref[at : at + rows, :] = t_ref[0:rows, columns]


def early_blocks(start, end, q, width):
    rows = (end - start) * q // width
    return [(start + i * rows, rows, slice(i * q, (i + 1) * q)) for i in range(width // q)]


def pack_outer_body(t_ref, late_ref, *chunks):
    half, width = t_ref.shape[0], late_ref.shape[1]
    late_ref[...] = t_ref[half - late_ref.shape[0] :, 0:width]
    at = 0
    for chunk in chunks:
        chunk[...] = t_ref[at : at + chunk.shape[0], 0:width]
        at += chunk.shape[0]


def sibling(x):
    size = lax.axis_size("leaf")
    return lax.ppermute(x, "leaf", [(i, i ^ size // 2) for i in range(size)])


def across(x):
    return lax.ppermute(x, "sib", [(0, 1), (1, 0)])


def kernel(body, outs, places, scratch=(), flops=1e8):
    return pl.pallas_call(
        body,
        out_shape=outs,
        in_specs=[pl.BlockSpec(memory_space=place) for place in places],
        scratch_shapes=list(scratch),
        compiler_params=pltpu.CompilerParams(vmem_limit_bytes=VMEM_LIMIT),
        cost_estimate=pl.CostEstimate(flops=int(flops), bytes_accessed=1 << 20, transcendentals=0),
    )


def two_shards(t_int, t_ext, iface_map):
    t_int, t_ext = t_int[0], t_ext[0]
    half, n = t_int.shape[0], iface_map.shape[1]
    width = t_int.shape[1] - n
    tiles = n // TILE
    q = half // 2
    f = lambda *shape: jax.ShapeDtypeStruct(shape, F32)
    vmem, smem = pltpu.VMEM, pltpu.SMEM
    mine = lax.axis_index("sib").astype(jnp.int32)
    first = mine.reshape(1)
    other_map = sibling(iface_map)
    early_rows = half * 5 // 8
    packed, early = kernel(
        functools.partial(pack_iface_body, half, width),
        (f(5 * q, q), f(3 * q + early_rows * width // q, q)),
        [vmem, smem],
    )(t_int, first)
    near = sibling(packed)
    early_other = across(early)
    far = across(near)
    late, *chunks = kernel(
        pack_outer_body, [f(half - early_rows, width)] + [f(half // CHUNKS, width)] * CHUNKS, [vmem]
    )(t_int)
    late, _ = lax.optimization_barrier((late, far))
    late_other = across(late)
    *chunks, _, other_map = lax.optimization_barrier((*chunks, near, other_map))
    near_r = [sibling(chunk) for chunk in chunks]
    rolled = lambda m: lax.dynamic_slice(jnp.concatenate([m, m], axis=1), (0, mine * half), (1, n))
    own_row, other_row = rolled(iface_map), rolled(other_map)

    top = tiles // 2 * TILE
    a, b, onehot = kernel(
        functools.partial(first_body, half, range(tiles // 2)),
        (f(n, n), f(top, top), jax.ShapeDtypeStruct((n, n), BF16)),
        [vmem] * 6 + [smem],
        [pltpu.VMEM((n, n), F32)],
        10e9,
    )(t_int, early_other, near, far, own_row.reshape(n, 1), other_row, first)
    a, b, near_r[0] = lax.optimization_barrier((a, b, near_r[0]))
    far_r = [across(near_r[0])]
    a, g, other = kernel(
        functools.partial(middle_body, range(tiles // 2, tiles - 1)),
        (f(n, n), f(n, width), f(half, width)),
        [vmem] * 5,
        (),
        5e9,
    )(a, b, t_int, early_other, late_other)
    a, g, near_r[1] = lax.optimization_barrier((a, g, near_r[1]))
    far_r.append(across(near_r[1]))
    g = kernel(
        functools.partial(last_body, range(tiles - 1, tiles)), f(n, width), [vmem] * 2, [pltpu.VMEM((n, n), F32)], 5e9
    )(a, g)
    g, *near_r[2:] = lax.optimization_barrier((g, *near_r[2:]))
    far_r += [across(x) for x in near_r[2:]]
    parts = [*near_r, *far_r[:2]]
    own_map, solution_op, h, partial = kernel(
        functools.partial(output_body, half),
        (f(half, width), f(half, width), f(n, half), f(half, width)),
        [vmem] * 6 + [smem] + [vmem] * len(parts),
        (),
        4e9,
    )(g, onehot, t_int, other, t_ext, own_row, first, *parts)
    cross_map = kernel(cross_body, f(half, width), [vmem] * (CHUNKS))(h, partial, *far_r[2:])
    return own_map[None], cross_map[None], solution_op[None]


def common_order(matrix, index_map):
    points = index_map.shape[0]
    inverse = jnp.zeros((points,), jnp.int32).at[index_map].set(jnp.arange(points, dtype=jnp.int32))
    picked = matrix[inverse]
    outer_width = matrix.shape[1] - points
    return (picked[:, :outer_width], picked[:, outer_width + inverse])


def many_shards(t_int, t_ext, iface_map):
    shard_rows = t_ext.shape[1]
    first_row = lax.axis_index("sib") * shard_rows
    near_rows, other_map = sibling((t_int, iface_map))
    own_rows = lax.all_gather(t_int, "sib", axis=1, tiled=True)
    other_rows = lax.all_gather(near_rows, "sib", axis=1, tiled=True)
    own_outer, own_iface = common_order(own_rows[0], iface_map[0])
    other_outer, other_iface = common_order(other_rows[0], other_map[0])
    g = solve(own_iface + other_iface, own_outer)
    product = lambda left, right: full(left, right, ((0,), (0,)))
    left = lax.dynamic_slice_in_dim(own_outer, first_row, shard_rows, 1)
    left_g = lax.dynamic_slice_in_dim(g, first_row, shard_rows, 1)
    own_map = t_ext - product(left, g)[None]
    cross_map = -product(left_g, other_outer)[None]
    solution_op = -lax.dynamic_slice_in_dim(g, first_row, shard_rows, 0)[None]
    return own_map, cross_map, solution_op


def solution(mesh):
    placed = P("leaf", "sib", None)
    return jax.shard_map(
        two_shards if mesh.shape["sib"] == 2 else many_shards,
        mesh=mesh,
        in_specs=(placed, placed, P("leaf", None)),
        out_specs=(placed, placed, placed),
        check_vma=False,
    )
```

```python
import functools

import jax
import jax.numpy as jnp
from jax import lax
from jax.experimental import pallas as pl
from jax.experimental.pallas import tpu as pltpu
from jax.sharding import PartitionSpec as P

F32 = jnp.float32
BF16 = jnp.bfloat16
TILE = 128
PARTS = (4, 8, 4)
VMEM_LIMIT = 48 * 2**20


def split3(x):
    high = x.astype(BF16).astype(F32)
    rest = x - high
    middle = rest.astype(BF16).astype(F32)
    return high, middle, rest - middle


def contract(left, right, dims):
    return lax.dot_general(left, right, (dims, ((), ())), preferred_element_type=F32)


def full(left, right, dims=((1,), (0,))):
    return lax.dot_general(
        left, right, (dims, ((), ())), precision=lax.Precision.HIGHEST, preferred_element_type=F32
    )


def three_pass(left, right, dims):
    lh, rh = left.astype(BF16), right.astype(BF16)
    ll, rl = (left - lh.astype(F32)).astype(BF16), (right - rh.astype(F32)).astype(BF16)
    return contract(lh, rh, dims) + (contract(lh, rl, dims) + contract(ll, rh, dims))


def pick_left(onehot, x, dims):
    high, middle, low = (part.astype(BF16) for part in split3(x))
    return contract(onehot, high, dims) + (contract(onehot, middle, dims) + contract(onehot, low, dims))


def pick_right(x, onehot, dims):
    high, middle, low = (part.astype(BF16) for part in split3(x))
    return contract(high, onehot, dims) + (contract(middle, onehot, dims) + contract(low, onehot, dims))


def over_lanes(x, lane):
    return jnp.broadcast_to(x[:, lane : lane + 1], (8, TILE))


def over_rows(x, row):
    return jnp.broadcast_to(x[row : row + 1, :], (8, TILE))


def invert_tile(work, slabs=2):
    width = 8 * slabs
    lane = lax.broadcasted_iota(jnp.int32, (8, TILE), 1)
    row = lax.broadcasted_iota(jnp.int32, (8, TILE), 0)
    lane_all = lax.broadcasted_iota(jnp.int32, (TILE, TILE), 1)
    is_row = [row == j for j in range(8)]

    def slab_list(x, base):
        return [x[base + 8 * s : base + 8 * s + 8, :] for s in range(slabs)]

    old = slab_list(work, 0)
    for base in range(0, TILE, width):
        after = base + width
        columns = [[over_lanes(x, base + m) for x in old] for m in range(width)]
        following = slab_list(work, after) if after < TILE else []
        factors = [[over_lanes(x, base + m) for x in following] for m in range(width)]
        inside = (lane >= base) & (lane < after)
        new = [
            jnp.where(inside, jnp.where(lane - base - 8 * s == row, 1.0, 0.0).astype(F32), old[s])
            for s in range(slabs)
        ]
        pivot = over_rows(columns[0][0], 0)
        scale = [None] * slabs
        for j in range(width):
            js, jr = divmod(j, 8)
            inverse = pltpu.reciprocal(pivot, approx=True)
            scale[js] = inverse if jr == 0 else jnp.where(is_row[jr], inverse, scale[js])
            here = list(columns[j])
            here[js] = jnp.where(is_row[jr], 0.0, here[js])
            scaled = [c * inverse for c in here]
            for m in range(j + 1, width):
                picked = over_rows(columns[m][js], jr)
                if m == j + 1:
                    columns[m] = [c - (h * picked) * inverse for c, h in zip(columns[m], here)]
                    pivot = over_rows(columns[m][m // 8], m % 8)
                else:
                    columns[m] = [c - h * picked for c, h in zip(columns[m], scaled)]
            picked = over_rows(new[js], jr)
            new = [x - h * picked for x, h in zip(new, scaled)]
        new = [x * y for x, y in zip(new, scale)]
        panel = jnp.concatenate(new, axis=0)
        sign = jnp.where(lane < base, -1.0, jnp.where(inside, 0.0, 1.0)).astype(F32)
        ah, am, al = split3(jnp.concatenate([x * sign for x in old], axis=0))
        bh, bm, bl = split3(panel)
        left = jnp.concatenate([ah, ah, am, am, ah, al], axis=0).astype(BF16)
        right = jnp.concatenate([bh, bm, bh, bm, bl, bh], axis=0).astype(BF16)
        change = contract(left, right, ((0,), (0,)))
        inside_all = (lane_all >= base) & (lane_all < after)
        rest = jnp.where(inside_all, 0.0, work) - change
        parts = [rest[:base], panel, rest[after:]]
        if following:
            rows = [over_rows(new[m // 8], m % 8) for m in range(width)]
            old = []
            for s in range(slabs):
                sums = []
                for q in range(4):
                    terms = [factors[m][s] * rows[m] for m in range(q, width, 4)]
                    sums.append(functools.reduce(lambda x, y: x + y, terms))
                old.append(jnp.where(inside, 0.0, following[s]) - ((sums[0] + sums[1]) + (sums[2] + sums[3])))
            parts = [rest[:base], panel, *old, rest[after + width :]]
        work = jnp.concatenate([x for x in parts if x.shape[0]], axis=0)
    return work


def eliminate(a_ref, g_ref, steps):
    size, rows_of_g = a_ref.shape[0], g_ref.shape[0]
    for k in steps:
        at, after = k * TILE, (k + 1) * TILE
        own = slice(at, after)
        inverse = invert_tile(a_ref[own, own])
        right = full(inverse, g_ref[own, :])
        g_ref[own, :] = right
        if after < size:
            old = a_ref[own, after:]
            panel = full(inverse, old)
            a_ref[own, after:] = panel
        for i in range(k + 1, size // TILE):
            rows = slice(i * TILE, (i + 1) * TILE)
            factor = old[:, (i - k - 1) * TILE : (i - k) * TILE]
            a_ref[rows, i * TILE :] = a_ref[rows, i * TILE :] - full(
                factor, panel[:, (i - k - 1) * TILE :], ((0,), (0,))
            )
            if (i + 1) * TILE <= rows_of_g:
                g_ref[rows, :] = g_ref[rows, :] - full(factor, right, ((0,), (0,)))
        for i in range(k):
            rows = slice(i * TILE, (i + 1) * TILE)
            factor = a_ref[rows, own]
            if after < size:
                a_ref[rows, after:] = a_ref[rows, after:] - full(factor, panel)
            g_ref[rows, :] = g_ref[rows, :] - full(factor, right)


def call(body, outs, scratch=(), **cost):
    return pl.pallas_call(
        body,
        out_shape=outs,
        scratch_shapes=list(scratch),
        compiler_params=pltpu.CompilerParams(vmem_limit_bytes=VMEM_LIMIT),
        **cost,
    )


def solve_body(a_ref, r_ref, g_ref, a_work):
    a_work[...] = a_ref[...]
    g_ref[...] = r_ref[...]
    eliminate(a_work, g_ref, range(a_ref.shape[0] // TILE))


def solve(a, r):
    return call(
        solve_body, jax.ShapeDtypeStruct(r.shape, F32), [pltpu.VMEM(a.shape, F32)]
    )(a, r)


def tile_block(q, i, j):
    return (slice(i * q, (i + 1) * q), slice(j * q, (j + 1) * q))


def put_sibling(m_ref, ref, base, mine):
    q = ref.shape[1]
    other = 2 - base

    def put(i, j, at):
        value = ref[at * q : (at + 1) * q, :]
        m_ref[tile_block(q, i, j)] = value
        if i != j:
            m_ref[tile_block(q, j, i)] = value.T

    put(base, base, 0)
    put(base, base + 1, 1)
    put(base + 1, base + 1, 2)
    put(base, other + 1, 3)
    sender = mine if base == 0 else 1 - mine

    @pl.when(sender == 0)
    def _():
        put(base, other, 4)

    @pl.when(sender != 0)
    def _():
        put(base + 1, other + 1, 4)


def prepare_body(half, t_ref, early_ref, near_ref, column_ref, first_ref, a_out, m_out, p_out):
    n, q = 2 * half, half // 2
    width = t_ref.shape[1] - n
    mine = first_ref[0]
    put_sibling(m_out, near_ref, 0, mine)
    row = jnp.concatenate([near_ref[5 * q + i : 5 * q + i + 1, :] for i in range(n // q)], axis=1)
    p_out[...] = jnp.where(column_ref[...] == row, 1.0, 0.0).astype(BF16)
    here = pl.ds(pl.multiple_of(width + mine * half, half), half)
    there = pl.ds(pl.multiple_of(width + (1 - mine) * half, half), half)
    a_out[0:half, 0:half] = t_ref[:, here]
    a_out[0:half, half:n] = t_ref[:, there]
    a_out[tile_block(q, 2, 2)] = early_ref[0:q, :]
    a_out[tile_block(q, 2, 3)] = early_ref[q : 2 * q, :]
    a_out[tile_block(q, 3, 3)] = early_ref[2 * q : 3 * q, :]


def first_body(steps, a_in, m_in, p_ref, far_ref, first_ref, a_out, b_out, m_work):
    n = a_in.shape[0]
    m_work[...] = m_in[...]
    put_sibling(m_work, far_ref, 2, first_ref[0])
    moved = pick_right(m_work[...], p_ref[...], ((1,), (1,)))
    for i in range(n // TILE):
        rows, later = slice(i * TILE, (i + 1) * TILE), slice(i * TILE, n)
        a_out[rows, later] = a_in[rows, later] + pick_left(p_ref[rows, :], moved[:, later], ((1,), (0,)))
    top = b_out.shape[0]
    on_diagonal = [lax.broadcasted_iota(jnp.int32, (top, top), axis) for axis in (0, 1)]
    b_out[...] = jnp.where(on_diagonal[0] == on_diagonal[1], 1.0, 0.0).astype(F32)
    eliminate(a_out, b_out, steps)


def middle_body(steps, a_in, b_ref, t_ref, early_ref, late_ref, a_out, g_out, other_out):
    top, half, q = b_ref.shape[0], t_ref.shape[0], early_ref.shape[1]
    width = g_out.shape[1]
    a_out[...] = a_in[...]
    for at, rows, columns in early_blocks(3 * q, early_ref.shape[0], q, width):
        other_out[0:rows, columns] = early_ref[at : at + rows, :]
    other_out[half - late_ref.shape[0] :, :] = late_ref[...]
    g_out[0:half, :] = t_ref[:, 0:width]
    g_out[half:, :] = other_out[...]
    first = g_out[0:top, :]
    g_out[top:, :] = g_out[top:, :] - full(a_in[0:top, top:], first, ((0,), (0,)))
    g_out[0:top, :] = full(b_ref[...], first)
    eliminate(a_out, g_out, steps)


def last_body(steps, a_ref, g_in, g_out, a_work):
    a_work[...] = a_ref[...]
    g_out[...] = g_in[...]
    eliminate(a_work, g_out, steps)


def cross_terms(h_ref, at, parts):
    total = None
    for ref in parts:
        term = three_pass(h_ref[at : at + ref.shape[0], :], ref[...], ((0,), (0,)))
        total = term if total is None else total + term
        at += ref.shape[0]
    return total


def output_body(
    half, g_ref, p_ref, t_ref, other_ref, ext_ref, row_ref, first_ref, *refs
):
    *parts, own_ref, sol_ref, h_ref, cross_ref = refs
    n = 2 * half
    mine = first_ref[0]
    block = pl.ds(pl.multiple_of(mine * half, half), half)
    g = g_ref[...]
    h_ref[...] = pick_left(p_ref[...], g_ref[:, block], ((0,), (0,)))
    left = jnp.concatenate([t_ref[:, block], other_ref[:, block]], axis=0)
    own_ref[...] = ext_ref[...] - three_pass(left, g, ((0,), (0,)))
    target = lax.broadcasted_iota(jnp.int32, (half, n), 0) + mine * half
    onehot = jnp.where(row_ref[...].astype(jnp.int32) == target, 1.0, 0.0).astype(BF16)
    sol_ref[...] = -pick_left(onehot, g, ((1,), (0,)))
    cross_ref[...] = cross_terms(h_ref, 0, parts)


def cross_body(h_ref, partial_ref, *refs):
    *parts, out_ref = refs
    at = h_ref.shape[0] - sum(ref.shape[0] for ref in parts)
    out_ref[...] = -(partial_ref[...] + cross_terms(h_ref, at, parts))


def pack_iface_body(half, width, t_ref, map_ref, first_ref, pack_ref, early_ref, row_ref, column_ref):
    q, n = half // 2, 2 * half
    mine = first_ref[0]
    here, there = width + mine * half, width + (1 - mine) * half

    def cut(row, column):
        return t_ref[pl.ds(pl.multiple_of(row, q), q), pl.ds(pl.multiple_of(column, q), q)]

    diagonal = [cut(0, here), cut(0, here + q), cut(q, here + q)]
    for i, block in enumerate([*diagonal, cut(0, there + q), cut(mine * q, there + mine * q)]):
        pack_ref[i * q : (i + 1) * q, :] = block
    for i, block in enumerate(diagonal):
        early_ref[i * q : (i + 1) * q, :] = block
    for at, rows, columns in early_blocks(3 * q, early_ref.shape[0], q, width):
        early_ref[at : at + rows, :] = t_ref[0:rows, columns]
    spans = [pl.ds(pl.multiple_of(x * half, half), half) for x in (mine, 1 - mine)]
    row = jnp.concatenate([map_ref[:, span] for span in spans], axis=1).astype(F32)
    row_ref[...] = row
    column_ref[...] = jnp.broadcast_to(row, (8, n)).T[:, 0:1]
    parts = [row[:, i * q : (i + 1) * q] for i in range(n // q)]
    pack_ref[5 * q :, :] = jnp.concatenate(parts + parts, axis=0)[0:8, :]


def early_blocks(start, end, q, width):
    rows = (end - start) * q // width
    return [(start + i * rows, rows, slice(i * q, (i + 1) * q)) for i in range(width // q)]


def pack_outer_body(t_ref, late_ref, *chunks):
    half, width = t_ref.shape[0], late_ref.shape[1]
    late_ref[...] = t_ref[half - late_ref.shape[0] :, 0:width]
    at = 0
    for chunk in chunks:
        chunk[...] = t_ref[at : at + chunk.shape[0], 0:width]
        at += chunk.shape[0]


def sibling(x):
    size = lax.axis_size("leaf")
    return lax.ppermute(x, "leaf", [(i, i ^ size // 2) for i in range(size)])


def across(x):
    return lax.ppermute(x, "sib", [(0, 1), (1, 0)])


def kernel(body, outs, places, scratch=(), flops=1e8):
    return pl.pallas_call(
        body,
        out_shape=outs,
        in_specs=[pl.BlockSpec(memory_space=place) for place in places],
        scratch_shapes=list(scratch),
        compiler_params=pltpu.CompilerParams(vmem_limit_bytes=VMEM_LIMIT),
        cost_estimate=pl.CostEstimate(flops=int(flops), bytes_accessed=1 << 20, transcendentals=0),
    )


def two_shards(t_int, t_ext, iface_map):
    t_int, t_ext = t_int[0], t_ext[0]
    half, n = t_int.shape[0], iface_map.shape[1]
    width = t_int.shape[1] - n
    tiles = n // TILE
    q = half // 2
    f = lambda *shape: jax.ShapeDtypeStruct(shape, F32)
    vmem, smem = pltpu.VMEM, pltpu.SMEM
    mine = lax.axis_index("sib").astype(jnp.int32)
    first = mine.reshape(1)
    early_rows = half * 5 // 8
    packed, early, own_row, column = kernel(
        functools.partial(pack_iface_body, half, width),
        (f(5 * q + 8, q), f(3 * q + early_rows * width // q, q), f(1, n), f(n, 1)),
        [vmem, vmem, smem],
    )(t_int, iface_map, first)
    near = sibling(packed)
    early_other = across(early)
    far = across(near)
    late, *chunks = kernel(
        pack_outer_body, [f(half - early_rows, width)] + [f(half * part // 16, width) for part in PARTS], [vmem]
    )(t_int)
    late, _ = lax.optimization_barrier((late, far))
    late_other = across(late)
    *chunks, _ = lax.optimization_barrier((*chunks, near))
    near_r = [sibling(chunk) for chunk in chunks]
    a, m, onehot = kernel(
        functools.partial(prepare_body, half),
        (f(n, n), f(n, n), jax.ShapeDtypeStruct((n, n), BF16)),
        [vmem] * 4 + [smem],
    )(t_int, early_other, near, column, first)
    top = tiles // 2 * TILE
    a, b = kernel(
        functools.partial(first_body, range(tiles // 2)),
        (f(n, n), f(top, top)),
        [vmem] * 4 + [smem],
        [pltpu.VMEM((n, n), F32)],
        10e9,
    )(a, m, onehot, far, first)
    a, b, near_r[0] = lax.optimization_barrier((a, b, near_r[0]))
    far_r = [across(near_r[0])]
    a, g, other = kernel(
        functools.partial(middle_body, range(tiles // 2, tiles - 1)),
        (f(n, n), f(n, width), f(half, width)),
        [vmem] * 5,
        (),
        5e9,
    )(a, b, t_int, early_other, late_other)
    a, g, near_r[1] = lax.optimization_barrier((a, g, near_r[1]))
    far_r.append(across(near_r[1]))
    g = kernel(
        functools.partial(last_body, range(tiles - 1, tiles)), f(n, width), [vmem] * 2, [pltpu.VMEM((n, n), F32)], 5e9
    )(a, g)
    g, near_r[2] = lax.optimization_barrier((g, near_r[2]))
    far_r.append(across(near_r[2]))
    parts = [*near_r, *far_r[:2]]
    own_map, solution_op, h, partial = kernel(
        functools.partial(output_body, half),
        (f(half, width), f(half, width), f(n, half), f(half, width)),
        [vmem] * 6 + [smem] + [vmem] * len(parts),
        (),
        4e9,
    )(g, onehot, t_int, other, t_ext, own_row, first, *parts)
    cross_map = kernel(cross_body, f(half, width), [vmem] * 3)(h, partial, far_r[2])
    return own_map[None], cross_map[None], solution_op[None]


def common_order(matrix, index_map):
    points = index_map.shape[0]
    inverse = jnp.zeros((points,), jnp.int32).at[index_map].set(jnp.arange(points, dtype=jnp.int32))
    picked = matrix[inverse]
    outer_width = matrix.shape[1] - points
    return (picked[:, :outer_width], picked[:, outer_width + inverse])


def many_shards(t_int, t_ext, iface_map):
    shard_rows = t_ext.shape[1]
    first_row = lax.axis_index("sib") * shard_rows
    near_rows, other_map = sibling((t_int, iface_map))
    own_rows = lax.all_gather(t_int, "sib", axis=1, tiled=True)
    other_rows = lax.all_gather(near_rows, "sib", axis=1, tiled=True)
    own_outer, own_iface = common_order(own_rows[0], iface_map[0])
    other_outer, other_iface = common_order(other_rows[0], other_map[0])
    g = solve(own_iface + other_iface, own_outer)
    product = lambda left, right: full(left, right, ((0,), (0,)))
    left = lax.dynamic_slice_in_dim(own_outer, first_row, shard_rows, 1)
    left_g = lax.dynamic_slice_in_dim(g, first_row, shard_rows, 1)
    own_map = t_ext - product(left, g)[None]
    cross_map = -product(left_g, other_outer)[None]
    solution_op = -lax.dynamic_slice_in_dim(g, first_row, shard_rows, 0)[None]
    return own_map, cross_map, solution_op


def solution(mesh):
    placed = P("leaf", "sib", None)
    return jax.shard_map(
        two_shards if mesh.shape["sib"] == 2 else many_shards,
        mesh=mesh,
        in_specs=(placed, placed, P("leaf", None)),
        out_specs=(placed, placed, placed),
        check_vma=False,
    )
```

```python
import functools

import jax
import jax.numpy as jnp
from jax import lax
from jax.experimental import pallas as pl
from jax.experimental.pallas import tpu as pltpu
from jax.sharding import PartitionSpec as P

F32 = jnp.float32
BF16 = jnp.bfloat16
TILE = 128
PARTS = (4, 8, 4)
VMEM_LIMIT = 48 * 2**20


def split3(x):
    high = x.astype(BF16).astype(F32)
    rest = x - high
    middle = rest.astype(BF16).astype(F32)
    return high, middle, rest - middle


def contract(left, right, dims):
    return lax.dot_general(left, right, (dims, ((), ())), preferred_element_type=F32)


def full(left, right, dims=((1,), (0,))):
    return lax.dot_general(
        left, right, (dims, ((), ())), precision=lax.Precision.HIGHEST, preferred_element_type=F32
    )


def three_pass(left, right, dims):
    lh, rh = left.astype(BF16), right.astype(BF16)
    ll, rl = (left - lh.astype(F32)).astype(BF16), (right - rh.astype(F32)).astype(BF16)
    return contract(lh, rh, dims) + (contract(lh, rl, dims) + contract(ll, rh, dims))


def pick_left(onehot, x, dims):
    high, middle, low = (part.astype(BF16) for part in split3(x))
    return contract(onehot, high, dims) + (contract(onehot, middle, dims) + contract(onehot, low, dims))


def pick_right(x, onehot, dims):
    high, middle, low = (part.astype(BF16) for part in split3(x))
    return contract(high, onehot, dims) + (contract(middle, onehot, dims) + contract(low, onehot, dims))


def over_lanes(x, lane):
    return jnp.broadcast_to(x[:, lane : lane + 1], (8, TILE))


def over_rows(x, row):
    return jnp.broadcast_to(x[row : row + 1, :], (8, TILE))


def invert_tile(work, slabs=2):
    width = 8 * slabs
    lane = lax.broadcasted_iota(jnp.int32, (8, TILE), 1)
    row = lax.broadcasted_iota(jnp.int32, (8, TILE), 0)
    lane_all = lax.broadcasted_iota(jnp.int32, (TILE, TILE), 1)
    is_row = [row == j for j in range(8)]

    def slab_list(x, base):
        return [x[base + 8 * s : base + 8 * s + 8, :] for s in range(slabs)]

    old = slab_list(work, 0)
    for base in range(0, TILE, width):
        after = base + width
        columns = [[over_lanes(x, base + m) for x in old] for m in range(width)]
        following = slab_list(work, after) if after < TILE else []
        factors = [[over_lanes(x, base + m) for x in following] for m in range(width)]
        inside = (lane >= base) & (lane < after)
        new = [
            jnp.where(inside, jnp.where(lane - base - 8 * s == row, 1.0, 0.0).astype(F32), old[s])
            for s in range(slabs)
        ]
        pivot = over_rows(columns[0][0], 0)
        scale = [None] * slabs
        for j in range(width):
            js, jr = divmod(j, 8)
            inverse = pltpu.reciprocal(pivot, approx=True)
            scale[js] = inverse if jr == 0 else jnp.where(is_row[jr], inverse, scale[js])
            here = list(columns[j])
            here[js] = jnp.where(is_row[jr], 0.0, here[js])
            scaled = [c * inverse for c in here]
            for m in range(j + 1, width):
                picked = over_rows(columns[m][js], jr)
                if m == j + 1:
                    columns[m] = [c - (h * picked) * inverse for c, h in zip(columns[m], here)]
                    pivot = over_rows(columns[m][m // 8], m % 8)
                else:
                    columns[m] = [c - h * picked for c, h in zip(columns[m], scaled)]
            picked = over_rows(new[js], jr)
            new = [x - h * picked for x, h in zip(new, scaled)]
        new = [x * y for x, y in zip(new, scale)]
        panel = jnp.concatenate(new, axis=0)
        sign = jnp.where(lane < base, -1.0, jnp.where(inside, 0.0, 1.0)).astype(F32)
        ah, am, al = split3(jnp.concatenate([x * sign for x in old], axis=0))
        bh, bm, bl = split3(panel)
        left = jnp.concatenate([ah, ah, am, am, ah, al], axis=0).astype(BF16)
        right = jnp.concatenate([bh, bm, bh, bm, bl, bh], axis=0).astype(BF16)
        change = contract(left, right, ((0,), (0,)))
        inside_all = (lane_all >= base) & (lane_all < after)
        rest = jnp.where(inside_all, 0.0, work) - change
        parts = [rest[:base], panel, rest[after:]]
        if following:
            rows = [over_rows(new[m // 8], m % 8) for m in range(width)]
            old = []
            for s in range(slabs):
                sums = []
                for q in range(4):
                    terms = [factors[m][s] * rows[m] for m in range(q, width, 4)]
                    sums.append(functools.reduce(lambda x, y: x + y, terms))
                old.append(jnp.where(inside, 0.0, following[s]) - ((sums[0] + sums[1]) + (sums[2] + sums[3])))
            parts = [rest[:base], panel, *old, rest[after + width :]]
        work = jnp.concatenate([x for x in parts if x.shape[0]], axis=0)
    return work


def eliminate(a_ref, g_ref, steps):
    size, rows_of_g = a_ref.shape[0], g_ref.shape[0]
    for k in steps:
        at, after = k * TILE, (k + 1) * TILE
        own = slice(at, after)
        inverse = invert_tile(a_ref[own, own])
        right = full(inverse, g_ref[own, :])
        g_ref[own, :] = right
        if after < size:
            old = a_ref[own, after:]
            panel = full(inverse, old)
            a_ref[own, after:] = panel
        for i in range(k + 1, size // TILE):
            rows = slice(i * TILE, (i + 1) * TILE)
            factor = old[:, (i - k - 1) * TILE : (i - k) * TILE]
            a_ref[rows, i * TILE :] = a_ref[rows, i * TILE :] - full(
                factor, panel[:, (i - k - 1) * TILE :], ((0,), (0,))
            )
            if (i + 1) * TILE <= rows_of_g:
                g_ref[rows, :] = g_ref[rows, :] - full(factor, right, ((0,), (0,)))
        for i in range(k):
            rows = slice(i * TILE, (i + 1) * TILE)
            factor = a_ref[rows, own]
            if after < size:
                a_ref[rows, after:] = a_ref[rows, after:] - full(factor, panel)
            g_ref[rows, :] = g_ref[rows, :] - full(factor, right)


def call(body, outs, scratch=(), **cost):
    return pl.pallas_call(
        body,
        out_shape=outs,
        scratch_shapes=list(scratch),
        compiler_params=pltpu.CompilerParams(vmem_limit_bytes=VMEM_LIMIT),
        **cost,
    )


def solve_body(a_ref, r_ref, g_ref, a_work):
    a_work[...] = a_ref[...]
    g_ref[...] = r_ref[...]
    eliminate(a_work, g_ref, range(a_ref.shape[0] // TILE))


def solve(a, r):
    return call(
        solve_body, jax.ShapeDtypeStruct(r.shape, F32), [pltpu.VMEM(a.shape, F32)]
    )(a, r)


def tile_block(q, i, j):
    return (slice(i * q, (i + 1) * q), slice(j * q, (j + 1) * q))


def put_sibling(m_ref, diag_ref, side_ref, base, mine):
    q = side_ref.shape[1]
    other = 2 - base

    def put(i, j, value):
        m_ref[tile_block(q, i, j)] = value
        if i != j:
            m_ref[tile_block(q, j, i)] = value.T

    first, cross, second = unpack_diagonal(diag_ref)
    put(base, base, first)
    put(base, base + 1, cross)
    put(base + 1, base + 1, second)
    put(base, other + 1, side_ref[0:q, :])
    sender = mine if base == 0 else 1 - mine

    @pl.when(sender == 0)
    def _():
        put(base, other, side_ref[q : 2 * q, :])

    @pl.when(sender != 0)
    def _():
        put(base + 1, other + 1, side_ref[q : 2 * q, :])


def pack_diagonal(first, cross, second):
    q = first.shape[0]
    e = q // 2
    lane = lax.broadcasted_iota(jnp.int32, (e, q), 1)
    corners = jnp.where(lane < e, second[0:e, :], first[e:, :])
    return [cross, first[0:e, :], second[e:, :], corners]


def unpack_diagonal(ref):
    q = ref.shape[1]
    e = q // 2
    upper, lower, corners = ref[q : q + e, :], ref[q + e : 2 * q, :], ref[2 * q : 2 * q + e, :]
    first = jnp.concatenate([upper, jnp.concatenate([upper.T[e:, :], corners[:, e:]], axis=1)], axis=0)
    second = jnp.concatenate([jnp.concatenate([corners[:, 0:e], lower.T[0:e, :]], axis=1), lower], axis=0)
    return first, ref[0:q, :], second


def prepare_body(half, t_ref, early_ref, near_ref, side_ref, column_ref, first_ref, a_out, m_out, p_out):
    n, q = 2 * half, half // 2
    width = t_ref.shape[1] - n
    mine = first_ref[0]
    put_sibling(m_out, near_ref, side_ref, 0, mine)
    at = 5 * q // 2
    row = jnp.concatenate([near_ref[at + i : at + i + 1, :] for i in range(n // q)], axis=1)
    p_out[...] = jnp.where(column_ref[...] == row, 1.0, 0.0).astype(BF16)
    here = pl.ds(pl.multiple_of(width + mine * half, half), half)
    there = pl.ds(pl.multiple_of(width + (1 - mine) * half, half), half)
    a_out[0:half, 0:half] = t_ref[:, here]
    a_out[0:half, half:n] = t_ref[:, there]
    first, cross, second = unpack_diagonal(early_ref)
    a_out[tile_block(q, 2, 2)] = first
    a_out[tile_block(q, 2, 3)] = cross
    a_out[tile_block(q, 3, 3)] = second


def first_body(steps, a_in, m_in, p_ref, far_ref, side_ref, first_ref, a_out, b_out, m_work):
    n = a_in.shape[0]
    m_work[...] = m_in[...]
    put_sibling(m_work, far_ref, side_ref, 2, first_ref[0])
    moved = pick_right(m_work[...], p_ref[...], ((1,), (1,)))
    for i in range(n // TILE):
        rows, later = slice(i * TILE, (i + 1) * TILE), slice(i * TILE, n)
        a_out[rows, later] = a_in[rows, later] + pick_left(p_ref[rows, :], moved[:, later], ((1,), (0,)))
    top = b_out.shape[0]
    on_diagonal = [lax.broadcasted_iota(jnp.int32, (top, top), axis) for axis in (0, 1)]
    b_out[...] = jnp.where(on_diagonal[0] == on_diagonal[1], 1.0, 0.0).astype(F32)
    eliminate(a_out, b_out, steps)


def middle_body(steps, a_in, b_ref, t_ref, other_ref, a_out, g_out):
    top, half = b_ref.shape[0], t_ref.shape[0]
    a_out[...] = a_in[...]
    g_out[0:half, :] = t_ref[:, 0 : g_out.shape[1]]
    g_out[half:, :] = other_ref[...]
    first = g_out[0:top, :]
    g_out[top:, :] = g_out[top:, :] - full(a_in[0:top, top:], first, ((0,), (0,)))
    g_out[0:top, :] = full(b_ref[...], first)
    eliminate(a_out, g_out, steps)


def last_body(steps, a_ref, g_in, g_out, a_work):
    a_work[...] = a_ref[...]
    g_out[...] = g_in[...]
    eliminate(a_work, g_out, steps)


def cross_terms(h_ref, at, parts):
    total = None
    for ref in parts:
        term = three_pass(h_ref[at : at + ref.shape[0], :], ref[...], ((0,), (0,)))
        total = term if total is None else total + term
        at += ref.shape[0]
    return total


def output_body(
    half, g_ref, p_ref, t_ref, other_ref, ext_ref, row_ref, first_ref, *refs
):
    *parts, own_ref, sol_ref, h_ref, cross_ref = refs
    n = 2 * half
    mine = first_ref[0]
    block = pl.ds(pl.multiple_of(mine * half, half), half)
    g = g_ref[...]
    h_ref[...] = pick_left(p_ref[...], g_ref[:, block], ((0,), (0,)))
    left = jnp.concatenate([t_ref[:, block], other_ref[:, block]], axis=0)
    own_ref[...] = ext_ref[...] - three_pass(left, g, ((0,), (0,)))
    target = lax.broadcasted_iota(jnp.int32, (half, n), 0) + mine * half
    onehot = jnp.where(row_ref[...].astype(jnp.int32) == target, 1.0, 0.0).astype(BF16)
    sol_ref[...] = -pick_left(onehot, g, ((1,), (0,)))
    cross_ref[...] = cross_terms(h_ref, 0, parts)


def cross_body(h_ref, partial_ref, *refs):
    *parts, out_ref = refs
    at = h_ref.shape[0] - sum(ref.shape[0] for ref in parts)
    out_ref[...] = -(partial_ref[...] + cross_terms(h_ref, at, parts))


def pack_iface_body(half, width, t_ref, map_ref, first_ref, diag_ref, side_ref, row_ref, column_ref):
    q, n = half // 2, 2 * half
    mine = first_ref[0]
    here, there = width + mine * half, width + (1 - mine) * half

    def cut(row, column):
        return t_ref[pl.ds(pl.multiple_of(row, q), q), pl.ds(pl.multiple_of(column, q), q)]

    at = 0
    for block in pack_diagonal(cut(0, here), cut(0, here + q), cut(q, here + q)):
        diag_ref[at : at + block.shape[0], :] = block
        at += block.shape[0]
    side_ref[0:q, :] = cut(0, there + q)
    side_ref[q : 2 * q, :] = cut(mine * q, there + mine * q)
    spans = [pl.ds(pl.multiple_of(x * half, half), half) for x in (mine, 1 - mine)]
    row = jnp.concatenate([map_ref[:, span] for span in spans], axis=1).astype(F32)
    row_ref[...] = row
    column_ref[...] = jnp.broadcast_to(row, (8, n)).T[:, 0:1]
    parts = [row[:, i * q : (i + 1) * q] for i in range(n // q)]
    diag_ref[at:, :] = jnp.concatenate(parts + parts, axis=0)[0:8, :]


def pack_outer_body(t_ref, outer_ref, *chunks):
    outer_ref[...] = t_ref[:, 0 : outer_ref.shape[1]]
    at = 0
    for chunk in chunks:
        chunk[...] = t_ref[at : at + chunk.shape[0], 0 : chunk.shape[1]]
        at += chunk.shape[0]


def sibling(x):
    size = lax.axis_size("leaf")
    return lax.ppermute(x, "leaf", [(i, i ^ size // 2) for i in range(size)])


def across(x):
    return lax.ppermute(x, "sib", [(0, 1), (1, 0)])


def kernel(body, outs, places, scratch=(), flops=1e8):
    return pl.pallas_call(
        body,
        out_shape=outs,
        in_specs=[pl.BlockSpec(memory_space=place) for place in places],
        scratch_shapes=list(scratch),
        compiler_params=pltpu.CompilerParams(vmem_limit_bytes=VMEM_LIMIT),
        cost_estimate=pl.CostEstimate(flops=int(flops), bytes_accessed=1 << 20, transcendentals=0),
    )


def two_shards(t_int, t_ext, iface_map):
    t_int, t_ext = t_int[0], t_ext[0]
    half, n = t_int.shape[0], iface_map.shape[1]
    width = t_int.shape[1] - n
    tiles = n // TILE
    q = half // 2
    f = lambda *shape: jax.ShapeDtypeStruct(shape, F32)
    vmem, smem = pltpu.VMEM, pltpu.SMEM
    mine = lax.axis_index("sib").astype(jnp.int32)
    first = mine.reshape(1)
    diag, side, own_row, column = kernel(
        functools.partial(pack_iface_body, half, width),
        (f(5 * q // 2 + 8, q), f(2 * q, q), f(1, n), f(n, 1)),
        [vmem, vmem, smem],
    )(t_int, iface_map, first)
    near = sibling(diag)
    diag_other = across(diag)
    far = across(near)
    side, diag_other = lax.optimization_barrier((side, diag_other))
    near_side = sibling(side)
    near, near_side = lax.optimization_barrier((near, near_side))
    far_side = across(near_side)
    outer, *chunks = kernel(
        pack_outer_body, [f(half, width)] + [f(half * part // 16, width) for part in PARTS], [vmem]
    )(t_int)
    other = across(outer)
    leading, _ = lax.optimization_barrier((chunks[0], near_side))
    *following, _ = lax.optimization_barrier((*chunks[1:], far))
    near_r = [sibling(chunk) for chunk in (leading, *following)]
    a, m, onehot = kernel(
        functools.partial(prepare_body, half),
        (f(n, n), f(n, n), jax.ShapeDtypeStruct((n, n), BF16)),
        [vmem] * 5 + [smem],
    )(t_int, diag_other, near, near_side, column, first)
    top = tiles // 2 * TILE
    a, b = kernel(
        functools.partial(first_body, range(tiles // 2)),
        (f(n, n), f(top, top)),
        [vmem] * 5 + [smem],
        [pltpu.VMEM((n, n), F32)],
        10e9,
    )(a, m, onehot, far, far_side, first)
    a, b, near_r[0] = lax.optimization_barrier((a, b, near_r[0]))
    far_r = [across(near_r[0])]
    a, g = kernel(
        functools.partial(middle_body, range(tiles // 2, tiles - 1)), (f(n, n), f(n, width)), [vmem] * 4, (), 5e9
    )(a, b, t_int, other)
    a, g, near_r[1] = lax.optimization_barrier((a, g, near_r[1]))
    far_r.append(across(near_r[1]))
    g = kernel(
        functools.partial(last_body, range(tiles - 1, tiles)), f(n, width), [vmem] * 2, [pltpu.VMEM((n, n), F32)], 5e9
    )(a, g)
    g, near_r[2] = lax.optimization_barrier((g, near_r[2]))
    far_r.append(across(near_r[2]))
    parts = [*near_r, *far_r[:2]]
    own_map, solution_op, h, partial = kernel(
        functools.partial(output_body, half),
        (f(half, width), f(half, width), f(n, half), f(half, width)),
        [vmem] * 6 + [smem] + [vmem] * len(parts),
        (),
        4e9,
    )(g, onehot, t_int, other, t_ext, own_row, first, *parts)
    cross_map = kernel(cross_body, f(half, width), [vmem] * 3)(h, partial, far_r[2])
    return own_map[None], cross_map[None], solution_op[None]


def common_order(matrix, index_map):
    points = index_map.shape[0]
    inverse = jnp.zeros((points,), jnp.int32).at[index_map].set(jnp.arange(points, dtype=jnp.int32))
    picked = matrix[inverse]
    outer_width = matrix.shape[1] - points
    return (picked[:, :outer_width], picked[:, outer_width + inverse])


def many_shards(t_int, t_ext, iface_map):
    shard_rows = t_ext.shape[1]
    first_row = lax.axis_index("sib") * shard_rows
    near_rows, other_map = sibling((t_int, iface_map))
    own_rows = lax.all_gather(t_int, "sib", axis=1, tiled=True)
    other_rows = lax.all_gather(near_rows, "sib", axis=1, tiled=True)
    own_outer, own_iface = common_order(own_rows[0], iface_map[0])
    other_outer, other_iface = common_order(other_rows[0], other_map[0])
    g = solve(own_iface + other_iface, own_outer)
    product = lambda left, right: full(left, right, ((0,), (0,)))
    left = lax.dynamic_slice_in_dim(own_outer, first_row, shard_rows, 1)
    left_g = lax.dynamic_slice_in_dim(g, first_row, shard_rows, 1)
    own_map = t_ext - product(left, g)[None]
    cross_map = -product(left_g, other_outer)[None]
    solution_op = -lax.dynamic_slice_in_dim(g, first_row, shard_rows, 0)[None]
    return own_map, cross_map, solution_op


def solution(mesh):
    placed = P("leaf", "sib", None)
    return jax.shard_map(
        two_shards if mesh.shape["sib"] == 2 else many_shards,
        mesh=mesh,
        in_specs=(placed, placed, P("leaf", None)),
        out_specs=(placed, placed, placed),
        check_vma=False,
    )
```

```python
import functools

import jax
import jax.numpy as jnp
from jax import lax
from jax.experimental import pallas as pl
from jax.experimental.pallas import tpu as pltpu
from jax.sharding import PartitionSpec as P

F32 = jnp.float32
BF16 = jnp.bfloat16
TILE = 128
VMEM_LIMIT = 48 * 2**20


def split3(x):
    high = x.astype(BF16).astype(F32)
    rest = x - high
    middle = rest.astype(BF16).astype(F32)
    return high, middle, rest - middle


def contract(left, right, dims):
    return lax.dot_general(left, right, (dims, ((), ())), preferred_element_type=F32)


def full(left, right, dims=((1,), (0,))):
    return lax.dot_general(
        left, right, (dims, ((), ())), precision=lax.Precision.HIGHEST, preferred_element_type=F32
    )


def three_pass(left, right, dims):
    lh, rh = left.astype(BF16), right.astype(BF16)
    ll, rl = (left - lh.astype(F32)).astype(BF16), (right - rh.astype(F32)).astype(BF16)
    return contract(lh, rh, dims) + (contract(lh, rl, dims) + contract(ll, rh, dims))


def pick_left(onehot, x, dims):
    high, middle, low = (part.astype(BF16) for part in split3(x))
    return contract(onehot, high, dims) + (contract(onehot, middle, dims) + contract(onehot, low, dims))


def pick_right(x, onehot, dims):
    high, middle, low = (part.astype(BF16) for part in split3(x))
    return contract(high, onehot, dims) + (contract(middle, onehot, dims) + contract(low, onehot, dims))


def over_lanes(x, lane):
    return jnp.broadcast_to(x[:, lane : lane + 1], (8, TILE))


def over_rows(x, row):
    return jnp.broadcast_to(x[row : row + 1, :], (8, TILE))


def invert_tile(work, slabs=2):
    width = 8 * slabs
    lane = lax.broadcasted_iota(jnp.int32, (8, TILE), 1)
    row = lax.broadcasted_iota(jnp.int32, (8, TILE), 0)
    lane_all = lax.broadcasted_iota(jnp.int32, (TILE, TILE), 1)
    is_row = [row == j for j in range(8)]

    def slab_list(x, base):
        return [x[base + 8 * s : base + 8 * s + 8, :] for s in range(slabs)]

    old = slab_list(work, 0)
    for base in range(0, TILE, width):
        after = base + width
        columns = [[over_lanes(x, base + m) for x in old] for m in range(width)]
        following = slab_list(work, after) if after < TILE else []
        factors = [[over_lanes(x, base + m) for x in following] for m in range(width)]
        inside = (lane >= base) & (lane < after)
        new = [
            jnp.where(inside, jnp.where(lane - base - 8 * s == row, 1.0, 0.0).astype(F32), old[s])
            for s in range(slabs)
        ]
        pivot = over_rows(columns[0][0], 0)
        scale = [None] * slabs
        for j in range(width):
            js, jr = divmod(j, 8)
            inverse = pltpu.reciprocal(pivot, approx=True)
            scale[js] = inverse if jr == 0 else jnp.where(is_row[jr], inverse, scale[js])
            here = list(columns[j])
            here[js] = jnp.where(is_row[jr], 0.0, here[js])
            scaled = [c * inverse for c in here]
            for m in range(j + 1, width):
                picked = over_rows(columns[m][js], jr)
                if m == j + 1:
                    columns[m] = [c - (h * picked) * inverse for c, h in zip(columns[m], here)]
                    pivot = over_rows(columns[m][m // 8], m % 8)
                else:
                    columns[m] = [c - h * picked for c, h in zip(columns[m], scaled)]
            picked = over_rows(new[js], jr)
            new = [x - h * picked for x, h in zip(new, scaled)]
        new = [x * y for x, y in zip(new, scale)]
        panel = jnp.concatenate(new, axis=0)
        sign = jnp.where(lane < base, -1.0, jnp.where(inside, 0.0, 1.0)).astype(F32)
        ah, am, al = split3(jnp.concatenate([x * sign for x in old], axis=0))
        bh, bm, bl = split3(panel)
        left = jnp.concatenate([ah, ah, am, am, ah, al], axis=0).astype(BF16)
        right = jnp.concatenate([bh, bm, bh, bm, bl, bh], axis=0).astype(BF16)
        change = contract(left, right, ((0,), (0,)))
        inside_all = (lane_all >= base) & (lane_all < after)
        rest = jnp.where(inside_all, 0.0, work) - change
        parts = [rest[:base], panel, rest[after:]]
        if following:
            rows = [over_rows(new[m // 8], m % 8) for m in range(width)]
            old = []
            for s in range(slabs):
                sums = []
                for q in range(4):
                    terms = [factors[m][s] * rows[m] for m in range(q, width, 4)]
                    sums.append(functools.reduce(lambda x, y: x + y, terms))
                old.append(jnp.where(inside, 0.0, following[s]) - ((sums[0] + sums[1]) + (sums[2] + sums[3])))
            parts = [rest[:base], panel, *old, rest[after + width :]]
        work = jnp.concatenate([x for x in parts if x.shape[0]], axis=0)
    return work


def eliminate(a_ref, g_ref, steps):
    size, rows_of_g = a_ref.shape[0], g_ref.shape[0]
    for k in steps:
        at, after = k * TILE, (k + 1) * TILE
        own = slice(at, after)
        inverse = invert_tile(a_ref[own, own])
        right = full(inverse, g_ref[own, :])
        g_ref[own, :] = right
        if after < size:
            old = a_ref[own, after:]
            panel = full(inverse, old)
            a_ref[own, after:] = panel
        for i in range(k + 1, size // TILE):
            rows = slice(i * TILE, (i + 1) * TILE)
            factor = old[:, (i - k - 1) * TILE : (i - k) * TILE]
            a_ref[rows, i * TILE :] = a_ref[rows, i * TILE :] - full(
                factor, panel[:, (i - k - 1) * TILE :], ((0,), (0,))
            )
            if (i + 1) * TILE <= rows_of_g:
                g_ref[rows, :] = g_ref[rows, :] - full(factor, right, ((0,), (0,)))
        for i in range(k):
            rows = slice(i * TILE, (i + 1) * TILE)
            factor = a_ref[rows, own]
            if after < size:
                a_ref[rows, after:] = a_ref[rows, after:] - full(factor, panel)
            g_ref[rows, :] = g_ref[rows, :] - full(factor, right)


def call(body, outs, scratch=(), **cost):
    return pl.pallas_call(
        body,
        out_shape=outs,
        scratch_shapes=list(scratch),
        compiler_params=pltpu.CompilerParams(vmem_limit_bytes=VMEM_LIMIT),
        **cost,
    )


def solve_body(a_ref, r_ref, g_ref, a_work):
    a_work[...] = a_ref[...]
    g_ref[...] = r_ref[...]
    eliminate(a_work, g_ref, range(a_ref.shape[0] // TILE))


def solve(a, r):
    return call(
        solve_body, jax.ShapeDtypeStruct(r.shape, F32), [pltpu.VMEM(a.shape, F32)]
    )(a, r)


def tile_block(q, i, j):
    return (slice(i * q, (i + 1) * q), slice(j * q, (j + 1) * q))


def put_sibling(m_ref, diag_ref, side_ref, base, mine):
    q = side_ref.shape[1]
    other = 2 - base

    def put(i, j, value):
        m_ref[tile_block(q, i, j)] = value
        if i != j:
            m_ref[tile_block(q, j, i)] = value.T

    first, cross, second = unpack_diagonal(diag_ref)
    put(base, base, first)
    put(base, base + 1, cross)
    put(base + 1, base + 1, second)
    put(base, other + 1, side_ref[0:q, :])
    sender = mine if base == 0 else 1 - mine

    @pl.when(sender == 0)
    def _():
        put(base, other, side_ref[q : 2 * q, :])

    @pl.when(sender != 0)
    def _():
        put(base + 1, other + 1, side_ref[q : 2 * q, :])


def pack_diagonal(first, cross, second):
    q = first.shape[0]
    e = q // 2
    lane = lax.broadcasted_iota(jnp.int32, (e, q), 1)
    corners = jnp.where(lane < e, second[0:e, :], first[e:, :])
    return [cross, first[0:e, :], second[e:, :], corners]


def unpack_diagonal(ref):
    q = ref.shape[1]
    e = q // 2
    upper, lower, corners = ref[q : q + e, :], ref[q + e : 2 * q, :], ref[2 * q : 2 * q + e, :]
    first = jnp.concatenate([upper, jnp.concatenate([upper.T[e:, :], corners[:, e:]], axis=1)], axis=0)
    second = jnp.concatenate([jnp.concatenate([corners[:, 0:e], lower.T[0:e, :]], axis=1), lower], axis=0)
    return first, ref[0:q, :], second


def prepare_body(half, t_ref, early_ref, near_ref, side_ref, column_ref, first_ref, a_out, m_out, p_out, outer_out):
    n, q = 2 * half, half // 2
    width = t_ref.shape[1] - n
    mine = first_ref[0]
    put_sibling(m_out, near_ref, side_ref, 0, mine)
    at = 5 * q // 2
    row = jnp.concatenate([near_ref[at + i : at + i + 1, :] for i in range(n // q)], axis=1)
    p_out[...] = jnp.where(column_ref[...] == row, 1.0, 0.0).astype(BF16)
    here = pl.ds(pl.multiple_of(width + mine * half, half), half)
    there = pl.ds(pl.multiple_of(width + (1 - mine) * half, half), half)
    a_out[0:half, 0:half] = t_ref[:, here]
    a_out[0:half, half:n] = t_ref[:, there]
    first, cross, second = unpack_diagonal(early_ref)
    a_out[tile_block(q, 2, 2)] = first
    a_out[tile_block(q, 2, 3)] = cross
    a_out[tile_block(q, 3, 3)] = second
    outer_out[...] = t_ref[:, column_blocks(half, mine)[0]]


def first_body(steps, a_in, m_in, p_ref, far_ref, side_ref, first_ref, a_out, b_out, m_work):
    n = a_in.shape[0]
    m_work[...] = m_in[...]
    put_sibling(m_work, far_ref, side_ref, 2, first_ref[0])
    moved = pick_right(m_work[...], p_ref[...], ((1,), (1,)))
    for i in range(n // TILE):
        rows, later = slice(i * TILE, (i + 1) * TILE), slice(i * TILE, n)
        a_out[rows, later] = a_in[rows, later] + pick_left(p_ref[rows, :], moved[:, later], ((1,), (0,)))
    top = b_out.shape[0]
    on_diagonal = [lax.broadcasted_iota(jnp.int32, (top, top), axis) for axis in (0, 1)]
    b_out[...] = jnp.where(on_diagonal[0] == on_diagonal[1], 1.0, 0.0).astype(F32)
    eliminate(a_out, b_out, steps)


def middle_body(steps, a_in, b_ref, t_ref, mine_ref, others_ref, first_ref, a_out, g_out):
    top, half = b_ref.shape[0], t_ref.shape[0]
    here, there = column_blocks(half, first_ref[0])
    a_out[...] = a_in[...]
    g_out[0:half, :] = t_ref[:, 0 : g_out.shape[1]]
    g_out[half:, here] = mine_ref[...]
    g_out[half:, there] = others_ref[...]
    first = g_out[0:top, :]
    g_out[top:, :] = g_out[top:, :] - full(a_in[0:top, top:], first, ((0,), (0,)))
    g_out[0:top, :] = full(b_ref[...], first)
    eliminate(a_out, g_out, steps)


def column_blocks(half, mine):
    return [pl.ds(pl.multiple_of(x * half, half), half) for x in (mine, 1 - mine)]


def last_body(steps, a_ref, g_in, g_out, a_work):
    a_work[...] = a_ref[...]
    g_out[...] = g_in[...]
    eliminate(a_work, g_out, steps)


def send_body(half, g_ref, p_ref, chunk_ref, first_ref, h_out, send_out):
    _, there = column_blocks(half, first_ref[0])
    h = pick_left(p_ref[...], g_ref[:, there], ((0,), (0,)))
    h_out[...] = h
    send_out[...] = -three_pass(h, chunk_ref[...], ((0,), (0,)))


def send_more_body(h_ref, chunk_ref, send_out):
    send_out[...] = -three_pass(h_ref[...], chunk_ref[...], ((0,), (0,)))


def output_body(
    half, g_ref, p_ref, t_ref, mine_ref, others_ref, ext_ref, row_ref, first_ref, chunk_a, chunk_b, own_ref, sol_ref, keep_ref
):
    n, q = 2 * half, half // 2
    mine = first_ref[0]
    here, there = column_blocks(half, mine)
    g = g_ref[...]
    left = jnp.concatenate([t_ref[:, here], mine_ref[...]], axis=0)
    own_ref[...] = ext_ref[...] - three_pass(left, g, ((0,), (0,)))
    target = lax.broadcasted_iota(jnp.int32, (half, n), 0) + mine * half
    onehot = jnp.where(row_ref[...].astype(jnp.int32) == target, 1.0, 0.0).astype(BF16)
    sol_ref[...] = -pick_left(onehot, g, ((1,), (0,)))
    h = pick_left(p_ref[...], g_ref[:, here], ((0,), (0,)))
    for i, chunk in enumerate((chunk_a, chunk_b)):
        keep_ref[:, i * q : (i + 1) * q] = -three_pass(h, chunk[...], ((0,), (0,)))


def cross_body(keep_ref, first_part, second_part, first_ref, out_ref):
    half, q = keep_ref.shape[0], first_part.shape[1]
    mine = first_ref[0]
    here, _ = column_blocks(half, mine)
    out_ref[:, here] = keep_ref[...]
    for i, part in enumerate((first_part, second_part)):
        out_ref[:, pl.ds(pl.multiple_of((1 - mine) * half + i * q, q), q)] = part[...]


def pack_iface_body(half, width, t_ref, map_ref, first_ref, diag_ref, side_ref, outer_ref, row_ref, column_ref):
    q, n = half // 2, 2 * half
    mine = first_ref[0]
    here, there = width + mine * half, width + (1 - mine) * half

    def cut(row, column):
        return t_ref[pl.ds(pl.multiple_of(row, q), q), pl.ds(pl.multiple_of(column, q), q)]

    at = 0
    for block in pack_diagonal(cut(0, here), cut(0, here + q), cut(q, here + q)):
        diag_ref[at : at + block.shape[0], :] = block
        at += block.shape[0]
    side_ref[0:q, :] = cut(0, there + q)
    side_ref[q : 2 * q, :] = cut(mine * q, there + mine * q)
    spans = column_blocks(half, mine)
    outer_ref[...] = t_ref[:, spans[1]]
    row = jnp.concatenate([map_ref[:, span] for span in spans], axis=1).astype(F32)
    row_ref[...] = row
    column_ref[...] = jnp.broadcast_to(row, (8, n)).T[:, 0:1]
    parts = [row[:, i * q : (i + 1) * q] for i in range(n // q)]
    diag_ref[at:, :] = jnp.concatenate(parts + parts, axis=0)[0:8, :]


def pack_outer_body(t_ref, mine_ref, first_ref, *chunks):
    half = t_ref.shape[0]
    mine = first_ref[0]
    for i, chunk in enumerate(chunks):
        width = chunk.shape[1]
        chunk[0:half, :] = t_ref[:, pl.ds(pl.multiple_of(mine * half + i * width, width), width)]
        chunk[half:, :] = mine_ref[:, i * width : (i + 1) * width]


def sibling(x):
    size = lax.axis_size("leaf")
    return lax.ppermute(x, "leaf", [(i, i ^ size // 2) for i in range(size)])


def across(x):
    return lax.ppermute(x, "sib", [(0, 1), (1, 0)])


def kernel(body, outs, places, scratch=(), flops=1e8):
    return pl.pallas_call(
        body,
        out_shape=outs,
        in_specs=[pl.BlockSpec(memory_space=place) for place in places],
        scratch_shapes=list(scratch),
        compiler_params=pltpu.CompilerParams(vmem_limit_bytes=VMEM_LIMIT),
        cost_estimate=pl.CostEstimate(flops=int(flops), bytes_accessed=1 << 20, transcendentals=0),
    )


def two_shards(t_int, t_ext, iface_map):
    t_int, t_ext = t_int[0], t_ext[0]
    half, n = t_int.shape[0], iface_map.shape[1]
    width = t_int.shape[1] - n
    tiles = n // TILE
    q = half // 2
    f = lambda *shape: jax.ShapeDtypeStruct(shape, F32)
    vmem, smem = pltpu.VMEM, pltpu.SMEM
    mine = lax.axis_index("sib").astype(jnp.int32)
    first = mine.reshape(1)
    diag, side, outer, own_row, column = kernel(
        functools.partial(pack_iface_body, half, width),
        (f(5 * q // 2 + 8, q), f(2 * q, q), f(half, half), f(1, n), f(n, 1)),
        [vmem, vmem, smem],
    )(t_int, iface_map, first)
    near = sibling(diag)
    diag_other = across(diag)
    far = across(near)
    side, outer, diag_other = lax.optimization_barrier((side, outer, diag_other))
    near_side = sibling(side)
    outer_mine = across(outer)
    near, near_side = lax.optimization_barrier((near, near_side))
    far_side = across(near_side)
    chunks = kernel(pack_outer_body, [f(n, q)] * 2, [vmem, vmem, smem])(t_int, outer_mine, first)
    *chunks, _ = lax.optimization_barrier((*chunks, near_side))
    near_r = [sibling(chunk) for chunk in chunks]
    first_late, *_ = lax.optimization_barrier((first, *chunks))
    a, m, onehot, outer = kernel(
        functools.partial(prepare_body, half),
        (f(n, n), f(n, n), jax.ShapeDtypeStruct((n, n), BF16), f(half, half)),
        [vmem] * 5 + [smem],
    )(t_int, diag_other, near, near_side, column, first_late)
    outer_others = across(outer)
    top = tiles // 2 * TILE
    a, b = kernel(
        functools.partial(first_body, range(tiles // 2)),
        (f(n, n), f(top, top)),
        [vmem] * 5 + [smem],
        [pltpu.VMEM((n, n), F32)],
        10e9,
    )(a, m, onehot, far, far_side, first)
    a, g = kernel(
        functools.partial(middle_body, range(tiles // 2, tiles - 1)),
        (f(n, n), f(n, width)),
        [vmem] * 5 + [smem],
        (),
        5e9,
    )(a, b, t_int, outer_mine, outer_others, first)
    g = kernel(
        functools.partial(last_body, range(tiles - 1, tiles)), f(n, width), [vmem] * 2, [pltpu.VMEM((n, n), F32)], 5e9
    )(a, g)
    h, send = kernel(
        functools.partial(send_body, half), (f(n, half), f(half, q)), [vmem] * 3 + [smem], (), 1e9
    )(g, onehot, near_r[0], first)
    cross_a = across(send)
    cross_b = across(kernel(send_more_body, f(half, q), [vmem] * 2, (), 5e9)(h, near_r[1]))
    own_map, solution_op, keep = kernel(
        functools.partial(output_body, half),
        (f(half, width), f(half, width), f(half, half)),
        [vmem] * 7 + [smem] + [vmem] * 2,
        (),
        1e6,
    )(g, onehot, t_int, outer_mine, outer_others, t_ext, own_row, first, *near_r)
    cross_map = kernel(cross_body, f(half, width), [vmem] * 3 + [smem])(keep, cross_a, cross_b, first)
    return own_map[None], cross_map[None], solution_op[None]


def common_order(matrix, index_map):
    points = index_map.shape[0]
    inverse = jnp.zeros((points,), jnp.int32).at[index_map].set(jnp.arange(points, dtype=jnp.int32))
    picked = matrix[inverse]
    outer_width = matrix.shape[1] - points
    return (picked[:, :outer_width], picked[:, outer_width + inverse])


def many_shards(t_int, t_ext, iface_map):
    shard_rows = t_ext.shape[1]
    first_row = lax.axis_index("sib") * shard_rows
    near_rows, other_map = sibling((t_int, iface_map))
    own_rows = lax.all_gather(t_int, "sib", axis=1, tiled=True)
    other_rows = lax.all_gather(near_rows, "sib", axis=1, tiled=True)
    own_outer, own_iface = common_order(own_rows[0], iface_map[0])
    other_outer, other_iface = common_order(other_rows[0], other_map[0])
    g = solve(own_iface + other_iface, own_outer)
    product = lambda left, right: full(left, right, ((0,), (0,)))
    left = lax.dynamic_slice_in_dim(own_outer, first_row, shard_rows, 1)
    left_g = lax.dynamic_slice_in_dim(g, first_row, shard_rows, 1)
    own_map = t_ext - product(left, g)[None]
    cross_map = -product(left_g, other_outer)[None]
    solution_op = -lax.dynamic_slice_in_dim(g, first_row, shard_rows, 0)[None]
    return own_map, cross_map, solution_op


def solution(mesh):
    placed = P("leaf", "sib", None)
    return jax.shard_map(
        two_shards if mesh.shape["sib"] == 2 else many_shards,
        mesh=mesh,
        in_specs=(placed, placed, P("leaf", None)),
        out_specs=(placed, placed, placed),
        check_vma=False,
    )
```

```python
import functools

import jax
import jax.numpy as jnp
from jax import lax
from jax.experimental import pallas as pl
from jax.experimental.pallas import tpu as pltpu
from jax.sharding import PartitionSpec as P

F32 = jnp.float32
BF16 = jnp.bfloat16
TILE = 128
VMEM_LIMIT = 48 * 2**20


def split3(x):
    high = x.astype(BF16).astype(F32)
    rest = x - high
    middle = rest.astype(BF16).astype(F32)
    return high, middle, rest - middle


def contract(left, right, dims):
    return lax.dot_general(left, right, (dims, ((), ())), preferred_element_type=F32)


def full(left, right, dims=((1,), (0,))):
    return lax.dot_general(
        left, right, (dims, ((), ())), precision=lax.Precision.HIGHEST, preferred_element_type=F32
    )


def three_pass(left, right, dims):
    lh, rh = left.astype(BF16), right.astype(BF16)
    ll, rl = (left - lh.astype(F32)).astype(BF16), (right - rh.astype(F32)).astype(BF16)
    return contract(lh, rh, dims) + (contract(lh, rl, dims) + contract(ll, rh, dims))


def pick_left(onehot, x, dims):
    high, middle, low = (part.astype(BF16) for part in split3(x))
    return contract(onehot, high, dims) + (contract(onehot, middle, dims) + contract(onehot, low, dims))


def pick_right(x, onehot, dims):
    high, middle, low = (part.astype(BF16) for part in split3(x))
    return contract(high, onehot, dims) + (contract(middle, onehot, dims) + contract(low, onehot, dims))


def over_lanes(x, lane):
    return jnp.broadcast_to(x[:, lane : lane + 1], (8, TILE))


def over_rows(x, row):
    return jnp.broadcast_to(x[row : row + 1, :], (8, TILE))


def invert_tile(work, slabs=2):
    width = 8 * slabs
    lane = lax.broadcasted_iota(jnp.int32, (8, TILE), 1)
    row = lax.broadcasted_iota(jnp.int32, (8, TILE), 0)
    lane_all = lax.broadcasted_iota(jnp.int32, (TILE, TILE), 1)
    is_row = [row == j for j in range(8)]

    def slab_list(x, base):
        return [x[base + 8 * s : base + 8 * s + 8, :] for s in range(slabs)]

    old = slab_list(work, 0)
    for base in range(0, TILE, width):
        after = base + width
        columns = [[over_lanes(x, base + m) for x in old] for m in range(width)]
        following = slab_list(work, after) if after < TILE else []
        factors = [[over_lanes(x, base + m) for x in following] for m in range(width)]
        inside = (lane >= base) & (lane < after)
        new = [
            jnp.where(inside, jnp.where(lane - base - 8 * s == row, 1.0, 0.0).astype(F32), old[s])
            for s in range(slabs)
        ]
        pivot = over_rows(columns[0][0], 0)
        scale = [None] * slabs
        for j in range(width):
            js, jr = divmod(j, 8)
            inverse = pltpu.reciprocal(pivot, approx=True)
            scale[js] = inverse if jr == 0 else jnp.where(is_row[jr], inverse, scale[js])
            here = list(columns[j])
            here[js] = jnp.where(is_row[jr], 0.0, here[js])
            scaled = [c * inverse for c in here]
            for m in range(j + 1, width):
                picked = over_rows(columns[m][js], jr)
                if m == j + 1:
                    columns[m] = [c - (h * picked) * inverse for c, h in zip(columns[m], here)]
                    pivot = over_rows(columns[m][m // 8], m % 8)
                else:
                    columns[m] = [c - h * picked for c, h in zip(columns[m], scaled)]
            picked = over_rows(new[js], jr)
            new = [x - h * picked for x, h in zip(new, scaled)]
        new = [x * y for x, y in zip(new, scale)]
        panel = jnp.concatenate(new, axis=0)
        sign = jnp.where(lane < base, -1.0, jnp.where(inside, 0.0, 1.0)).astype(F32)
        ah, am, al = split3(jnp.concatenate([x * sign for x in old], axis=0))
        bh, bm, bl = split3(panel)
        left = jnp.concatenate([ah, ah, am, am, ah, al], axis=0).astype(BF16)
        right = jnp.concatenate([bh, bm, bh, bm, bl, bh], axis=0).astype(BF16)
        change = contract(left, right, ((0,), (0,)))
        inside_all = (lane_all >= base) & (lane_all < after)
        rest = jnp.where(inside_all, 0.0, work) - change
        parts = [rest[:base], panel, rest[after:]]
        if following:
            rows = [over_rows(new[m // 8], m % 8) for m in range(width)]
            old = []
            for s in range(slabs):
                sums = []
                for q in range(4):
                    terms = [factors[m][s] * rows[m] for m in range(q, width, 4)]
                    sums.append(functools.reduce(lambda x, y: x + y, terms))
                old.append(jnp.where(inside, 0.0, following[s]) - ((sums[0] + sums[1]) + (sums[2] + sums[3])))
            parts = [rest[:base], panel, *old, rest[after + width :]]
        work = jnp.concatenate([x for x in parts if x.shape[0]], axis=0)
    return work


def eliminate(a_ref, g_ref, steps):
    size, rows_of_g = a_ref.shape[0], g_ref.shape[0]
    for k in steps:
        at, after = k * TILE, (k + 1) * TILE
        own = slice(at, after)
        inverse = invert_tile(a_ref[own, own])
        right = full(inverse, g_ref[own, :])
        g_ref[own, :] = right
        if after < size:
            old = a_ref[own, after:]
            panel = full(inverse, old)
            a_ref[own, after:] = panel
        for i in range(k + 1, size // TILE):
            rows = slice(i * TILE, (i + 1) * TILE)
            factor = old[:, (i - k - 1) * TILE : (i - k) * TILE]
            a_ref[rows, i * TILE :] = a_ref[rows, i * TILE :] - full(
                factor, panel[:, (i - k - 1) * TILE :], ((0,), (0,))
            )
            if (i + 1) * TILE <= rows_of_g:
                g_ref[rows, :] = g_ref[rows, :] - full(factor, right, ((0,), (0,)))
        for i in range(k):
            rows = slice(i * TILE, (i + 1) * TILE)
            factor = a_ref[rows, own]
            if after < size:
                a_ref[rows, after:] = a_ref[rows, after:] - full(factor, panel)
            g_ref[rows, :] = g_ref[rows, :] - full(factor, right)


def call(body, outs, scratch=(), **cost):
    return pl.pallas_call(
        body,
        out_shape=outs,
        scratch_shapes=list(scratch),
        compiler_params=pltpu.CompilerParams(vmem_limit_bytes=VMEM_LIMIT),
        **cost,
    )


def solve_body(a_ref, r_ref, g_ref, a_work):
    a_work[...] = a_ref[...]
    g_ref[...] = r_ref[...]
    eliminate(a_work, g_ref, range(a_ref.shape[0] // TILE))


def solve(a, r):
    return call(
        solve_body, jax.ShapeDtypeStruct(r.shape, F32), [pltpu.VMEM(a.shape, F32)]
    )(a, r)


def tile_block(q, i, j):
    return (slice(i * q, (i + 1) * q), slice(j * q, (j + 1) * q))


def put_sibling(m_ref, diag_ref, side_ref, base, mine):
    q = side_ref.shape[1]
    other = 2 - base

    def put(i, j, value):
        m_ref[tile_block(q, i, j)] = value
        if i != j:
            m_ref[tile_block(q, j, i)] = value.T

    first, cross, second = unpack_diagonal(diag_ref)
    put(base, base, first)
    put(base, base + 1, cross)
    put(base + 1, base + 1, second)
    put(base, other + 1, side_ref[0:q, :])
    sender = mine if base == 0 else 1 - mine

    @pl.when(sender == 0)
    def _():
        put(base, other, side_ref[q : 2 * q, :])

    @pl.when(sender != 0)
    def _():
        put(base + 1, other + 1, side_ref[q : 2 * q, :])


def pack_diagonal(first, cross, second):
    q = first.shape[0]
    e = q // 2
    lane = lax.broadcasted_iota(jnp.int32, (e, q), 1)
    corners = jnp.where(lane < e, second[0:e, :], first[e:, :])
    return [cross, first[0:e, :], second[e:, :], corners]


def unpack_diagonal(ref):
    q = ref.shape[1]
    e = q // 2
    upper, lower, corners = ref[q : q + e, :], ref[q + e : 2 * q, :], ref[2 * q : 2 * q + e, :]
    first = jnp.concatenate([upper, jnp.concatenate([upper.T[e:, :], corners[:, e:]], axis=1)], axis=0)
    second = jnp.concatenate([jnp.concatenate([corners[:, 0:e], lower.T[0:e, :]], axis=1), lower], axis=0)
    return first, ref[0:q, :], second


def prepare_body(half, t_ref, early_ref, near_ref, side_ref, column_ref, row_ref, first_ref, a_out, m_out, p_out, outer_out):
    n, q = 2 * half, half // 2
    width = t_ref.shape[1] - n
    mine = first_ref[0]
    put_sibling(m_out, near_ref, side_ref, 0, mine)
    p_out[...] = jnp.where(column_ref[...] == row_ref[...], 1.0, 0.0).astype(BF16)
    here = pl.ds(pl.multiple_of(width + mine * half, half), half)
    there = pl.ds(pl.multiple_of(width + (1 - mine) * half, half), half)
    a_out[0:half, 0:half] = t_ref[:, here]
    a_out[0:half, half:n] = t_ref[:, there]
    first, cross, second = unpack_diagonal(early_ref)
    a_out[tile_block(q, 2, 2)] = first
    a_out[tile_block(q, 2, 3)] = cross
    a_out[tile_block(q, 3, 3)] = second
    outer_out[...] = t_ref[:, column_blocks(half, mine)[0]]


def first_body(steps, a_in, m_in, p_ref, far_ref, side_ref, first_ref, a_out, b_out, m_work):
    n = a_in.shape[0]
    m_work[...] = m_in[...]
    put_sibling(m_work, far_ref, side_ref, 2, first_ref[0])
    moved = pick_right(m_work[...], p_ref[...], ((1,), (1,)))
    for i in range(n // TILE):
        rows, later = slice(i * TILE, (i + 1) * TILE), slice(i * TILE, n)
        a_out[rows, later] = a_in[rows, later] + pick_left(p_ref[rows, :], moved[:, later], ((1,), (0,)))
    top = b_out.shape[0]
    on_diagonal = [lax.broadcasted_iota(jnp.int32, (top, top), axis) for axis in (0, 1)]
    b_out[...] = jnp.where(on_diagonal[0] == on_diagonal[1], 1.0, 0.0).astype(F32)
    eliminate(a_out, b_out, steps)


def middle_body(steps, a_in, b_ref, t_ref, mine_ref, others_ref, first_ref, a_out, g_out):
    top, half = b_ref.shape[0], t_ref.shape[0]
    here, there = column_blocks(half, first_ref[0])
    a_out[...] = a_in[...]
    g_out[0:half, :] = t_ref[:, 0 : g_out.shape[1]]
    g_out[half:, here] = mine_ref[...]
    g_out[half:, there] = others_ref[...]
    first = g_out[0:top, :]
    g_out[top:, :] = g_out[top:, :] - full(a_in[0:top, top:], first, ((0,), (0,)))
    g_out[0:top, :] = full(b_ref[...], first)
    eliminate(a_out, g_out, steps)


def column_blocks(half, mine):
    return [pl.ds(pl.multiple_of(x * half, half), half) for x in (mine, 1 - mine)]


def last_body(steps, a_ref, g_in, g_out, a_work):
    a_work[...] = a_ref[...]
    g_out[...] = g_in[...]
    eliminate(a_work, g_out, steps)


def send_body(half, g_ref, p_ref, chunk_ref, first_ref, h_out, send_out):
    _, there = column_blocks(half, first_ref[0])
    h = pick_left(p_ref[...], g_ref[:, there], ((0,), (0,)))
    h_out[...] = h
    send_out[...] = -three_pass(h, chunk_ref[...], ((0,), (0,)))


def send_more_body(h_ref, chunk_ref, send_out):
    send_out[...] = -three_pass(h_ref[...], chunk_ref[...], ((0,), (0,)))


def output_body(
    half, g_ref, p_ref, t_ref, mine_ref, others_ref, ext_ref, row_ref, first_ref, chunk_a, chunk_b, own_ref, sol_ref, keep_ref
):
    n, q = 2 * half, half // 2
    mine = first_ref[0]
    here, there = column_blocks(half, mine)
    g = g_ref[...]
    left = jnp.concatenate([t_ref[:, here], mine_ref[...]], axis=0)
    own_ref[...] = ext_ref[...] - three_pass(left, g, ((0,), (0,)))
    target = lax.broadcasted_iota(jnp.int32, (half, n), 0) + mine * half
    onehot = jnp.where(row_ref[...].astype(jnp.int32) == target, 1.0, 0.0).astype(BF16)
    sol_ref[...] = -pick_left(onehot, g, ((1,), (0,)))
    h = pick_left(p_ref[...], g_ref[:, here], ((0,), (0,)))
    for i, chunk in enumerate((chunk_a, chunk_b)):
        keep_ref[:, i * q : (i + 1) * q] = -three_pass(h, chunk[...], ((0,), (0,)))


def cross_body(keep_ref, first_part, second_part, first_ref, out_ref):
    half, q = keep_ref.shape[0], first_part.shape[1]
    mine = first_ref[0]
    here, _ = column_blocks(half, mine)
    out_ref[:, here] = keep_ref[...]
    for i, part in enumerate((first_part, second_part)):
        out_ref[:, pl.ds(pl.multiple_of((1 - mine) * half + i * q, q), q)] = part[...]


def pack_iface_body(half, width, t_ref, first_ref, diag_ref, side_ref, outer_ref):
    q = half // 2
    mine = first_ref[0]
    here, there = width + mine * half, width + (1 - mine) * half

    def cut(row, column):
        return t_ref[pl.ds(pl.multiple_of(row, q), q), pl.ds(pl.multiple_of(column, q), q)]

    at = 0
    for block in pack_diagonal(cut(0, here), cut(0, here + q), cut(q, here + q)):
        diag_ref[at : at + block.shape[0], :] = block
        at += block.shape[0]
    side_ref[0:q, :] = cut(0, there + q)
    side_ref[q : 2 * q, :] = cut(mine * q, there + mine * q)
    outer_ref[...] = t_ref[:, column_blocks(half, mine)[1]]


def map_body(half, map_ref, first_ref, row_ref, column_ref):
    row = jnp.concatenate([map_ref[:, block] for block in column_blocks(half, first_ref[0])], axis=1).astype(F32)
    row_ref[...] = row
    column_ref[...] = jnp.broadcast_to(row, (8, 2 * half)).T[:, 0:1]


def pack_outer_body(t_ref, mine_ref, first_ref, *chunks):
    half = t_ref.shape[0]
    mine = first_ref[0]
    for i, chunk in enumerate(chunks):
        width = chunk.shape[1]
        chunk[0:half, :] = t_ref[:, pl.ds(pl.multiple_of(mine * half + i * width, width), width)]
        chunk[half:, :] = mine_ref[:, i * width : (i + 1) * width]


def sibling(x):
    size = lax.axis_size("leaf")
    return lax.ppermute(x, "leaf", [(i, i ^ size // 2) for i in range(size)])


def across(x):
    return lax.ppermute(x, "sib", [(0, 1), (1, 0)])


def kernel(body, outs, places, scratch=(), flops=1e8):
    return pl.pallas_call(
        body,
        out_shape=outs,
        in_specs=[pl.BlockSpec(memory_space=place) for place in places],
        scratch_shapes=list(scratch),
        compiler_params=pltpu.CompilerParams(vmem_limit_bytes=VMEM_LIMIT),
        cost_estimate=pl.CostEstimate(flops=int(flops), bytes_accessed=1 << 20, transcendentals=0),
    )


def two_shards(t_int, t_ext, iface_map):
    t_int, t_ext = t_int[0], t_ext[0]
    half, n = t_int.shape[0], iface_map.shape[1]
    width = t_int.shape[1] - n
    tiles = n // TILE
    q = half // 2
    f = lambda *shape: jax.ShapeDtypeStruct(shape, F32)
    vmem, smem = pltpu.VMEM, pltpu.SMEM
    mine = lax.axis_index("sib").astype(jnp.int32)
    first = mine.reshape(1)
    diag, side, outer = kernel(
        functools.partial(pack_iface_body, half, width),
        (f(5 * q // 2, q), f(2 * q, q), f(half, half)),
        [vmem, smem],
    )(t_int, first)
    near, near_side = sibling(diag), sibling(side)
    diag_other = across(diag)
    far = across(near)
    outer, diag_other = lax.optimization_barrier((outer, diag_other))
    outer_mine = across(outer)
    own_row, column = kernel(functools.partial(map_body, half), (f(1, n), f(n, 1)), [vmem, smem])(iface_map, first)
    other_row = sibling(own_row)
    near, near_side = lax.optimization_barrier((near, near_side))
    far_side = across(near_side)
    chunks = kernel(pack_outer_body, [f(n, q)] * 2, [vmem, vmem, smem])(t_int, outer_mine, first)
    *chunks, _, other_row = lax.optimization_barrier((*chunks, near_side, other_row))
    near_r = [sibling(chunk) for chunk in chunks]
    first_late, *_ = lax.optimization_barrier((first, *chunks))
    a, m, onehot, outer = kernel(
        functools.partial(prepare_body, half),
        (f(n, n), f(n, n), jax.ShapeDtypeStruct((n, n), BF16), f(half, half)),
        [vmem] * 6 + [smem],
    )(t_int, diag_other, near, near_side, column, other_row, first_late)
    outer_others = across(outer)
    top = tiles // 2 * TILE
    a, b = kernel(
        functools.partial(first_body, range(tiles // 2)),
        (f(n, n), f(top, top)),
        [vmem] * 5 + [smem],
        [pltpu.VMEM((n, n), F32)],
        10e9,
    )(a, m, onehot, far, far_side, first)
    a, g = kernel(
        functools.partial(middle_body, range(tiles // 2, tiles - 1)),
        (f(n, n), f(n, width)),
        [vmem] * 5 + [smem],
        (),
        5e9,
    )(a, b, t_int, outer_mine, outer_others, first)
    g = kernel(
        functools.partial(last_body, range(tiles - 1, tiles)), f(n, width), [vmem] * 2, [pltpu.VMEM((n, n), F32)], 5e9
    )(a, g)
    h, send = kernel(
        functools.partial(send_body, half), (f(n, half), f(half, q)), [vmem] * 3 + [smem], (), 1e9
    )(g, onehot, near_r[0], first)
    cross_a = across(send)
    cross_b = across(kernel(send_more_body, f(half, q), [vmem] * 2, (), 5e9)(h, near_r[1]))
    own_map, solution_op, keep = kernel(
        functools.partial(output_body, half),
        (f(half, width), f(half, width), f(half, half)),
        [vmem] * 7 + [smem] + [vmem] * 2,
        (),
        1e6,
    )(g, onehot, t_int, outer_mine, outer_others, t_ext, own_row, first, *near_r)
    cross_map = kernel(cross_body, f(half, width), [vmem] * 3 + [smem])(keep, cross_a, cross_b, first)
    return own_map[None], cross_map[None], solution_op[None]


def common_order(matrix, index_map):
    points = index_map.shape[0]
    inverse = jnp.zeros((points,), jnp.int32).at[index_map].set(jnp.arange(points, dtype=jnp.int32))
    picked = matrix[inverse]
    outer_width = matrix.shape[1] - points
    return (picked[:, :outer_width], picked[:, outer_width + inverse])


def many_shards(t_int, t_ext, iface_map):
    shard_rows = t_ext.shape[1]
    first_row = lax.axis_index("sib") * shard_rows
    near_rows, other_map = sibling((t_int, iface_map))
    own_rows = lax.all_gather(t_int, "sib", axis=1, tiled=True)
    other_rows = lax.all_gather(near_rows, "sib", axis=1, tiled=True)
    own_outer, own_iface = common_order(own_rows[0], iface_map[0])
    other_outer, other_iface = common_order(other_rows[0], other_map[0])
    g = solve(own_iface + other_iface, own_outer)
    product = lambda left, right: full(left, right, ((0,), (0,)))
    left = lax.dynamic_slice_in_dim(own_outer, first_row, shard_rows, 1)
    left_g = lax.dynamic_slice_in_dim(g, first_row, shard_rows, 1)
    own_map = t_ext - product(left, g)[None]
    cross_map = -product(left_g, other_outer)[None]
    solution_op = -lax.dynamic_slice_in_dim(g, first_row, shard_rows, 0)[None]
    return own_map, cross_map, solution_op


def solution(mesh):
    placed = P("leaf", "sib", None)
    return jax.shard_map(
        two_shards if mesh.shape["sib"] == 2 else many_shards,
        mesh=mesh,
        in_specs=(placed, placed, P("leaf", None)),
        out_specs=(placed, placed, placed),
        check_vma=False,
    )
```

```python
import functools

import jax
import jax.numpy as jnp
from jax import lax
from jax.experimental import pallas as pl
from jax.experimental.pallas import tpu as pltpu
from jax.sharding import PartitionSpec as P

F32 = jnp.float32
BF16 = jnp.bfloat16
TILE = 128
VMEM_LIMIT = 48 * 2**20


def split3(x):
    high = x.astype(BF16).astype(F32)
    rest = x - high
    middle = rest.astype(BF16).astype(F32)
    return high, middle, rest - middle


def contract(left, right, dims):
    return lax.dot_general(left, right, (dims, ((), ())), preferred_element_type=F32)


def full(left, right, dims=((1,), (0,))):
    return lax.dot_general(
        left, right, (dims, ((), ())), precision=lax.Precision.HIGHEST, preferred_element_type=F32
    )


def three_pass(left, right, dims):
    lh, rh = left.astype(BF16), right.astype(BF16)
    ll, rl = (left - lh.astype(F32)).astype(BF16), (right - rh.astype(F32)).astype(BF16)
    return contract(lh, rh, dims) + (contract(lh, rl, dims) + contract(ll, rh, dims))


def pick_left(onehot, x, dims):
    high, middle, low = (part.astype(BF16) for part in split3(x))
    return contract(onehot, high, dims) + (contract(onehot, middle, dims) + contract(onehot, low, dims))


def pick_right(x, onehot, dims):
    high, middle, low = (part.astype(BF16) for part in split3(x))
    return contract(high, onehot, dims) + (contract(middle, onehot, dims) + contract(low, onehot, dims))


def over_lanes(x, lane):
    return jnp.broadcast_to(x[:, lane : lane + 1], (8, TILE))


def over_rows(x, row):
    return jnp.broadcast_to(x[row : row + 1, :], (8, TILE))


def invert_tile(work, slabs=2):
    width = 8 * slabs
    lane = lax.broadcasted_iota(jnp.int32, (8, TILE), 1)
    row = lax.broadcasted_iota(jnp.int32, (8, TILE), 0)
    lane_all = lax.broadcasted_iota(jnp.int32, (TILE, TILE), 1)
    is_row = [row == j for j in range(8)]

    def slab_list(x, base):
        return [x[base + 8 * s : base + 8 * s + 8, :] for s in range(slabs)]

    old = slab_list(work, 0)
    for base in range(0, TILE, width):
        after = base + width
        columns = [[over_lanes(x, base + m) for x in old] for m in range(width)]
        following = slab_list(work, after) if after < TILE else []
        factors = [[over_lanes(x, base + m) for x in following] for m in range(width)]
        inside = (lane >= base) & (lane < after)
        new = [
            jnp.where(inside, jnp.where(lane - base - 8 * s == row, 1.0, 0.0).astype(F32), old[s])
            for s in range(slabs)
        ]
        pivot = over_rows(columns[0][0], 0)
        scale = [None] * slabs
        for j in range(width):
            js, jr = divmod(j, 8)
            inverse = pltpu.reciprocal(pivot, approx=True)
            scale[js] = inverse if jr == 0 else jnp.where(is_row[jr], inverse, scale[js])
            here = list(columns[j])
            here[js] = jnp.where(is_row[jr], 0.0, here[js])
            scaled = [c * inverse for c in here]
            for m in range(j + 1, width):
                picked = over_rows(columns[m][js], jr)
                if m == j + 1:
                    columns[m] = [c - (h * picked) * inverse for c, h in zip(columns[m], here)]
                    pivot = over_rows(columns[m][m // 8], m % 8)
                else:
                    columns[m] = [c - h * picked for c, h in zip(columns[m], scaled)]
            picked = over_rows(new[js], jr)
            new = [x - h * picked for x, h in zip(new, scaled)]
        new = [x * y for x, y in zip(new, scale)]
        panel = jnp.concatenate(new, axis=0)
        sign = jnp.where(lane < base, -1.0, jnp.where(inside, 0.0, 1.0)).astype(F32)
        ah, am, al = split3(jnp.concatenate([x * sign for x in old], axis=0))
        bh, bm, bl = split3(panel)
        left = jnp.concatenate([ah, ah, am, am, ah, al], axis=0).astype(BF16)
        right = jnp.concatenate([bh, bm, bh, bm, bl, bh], axis=0).astype(BF16)
        change = contract(left, right, ((0,), (0,)))
        inside_all = (lane_all >= base) & (lane_all < after)
        rest = jnp.where(inside_all, 0.0, work) - change
        parts = [rest[:base], panel, rest[after:]]
        if following:
            rows = [over_rows(new[m // 8], m % 8) for m in range(width)]
            old = []
            for s in range(slabs):
                sums = []
                for q in range(4):
                    terms = [factors[m][s] * rows[m] for m in range(q, width, 4)]
                    sums.append(functools.reduce(lambda x, y: x + y, terms))
                old.append(jnp.where(inside, 0.0, following[s]) - ((sums[0] + sums[1]) + (sums[2] + sums[3])))
            parts = [rest[:base], panel, *old, rest[after + width :]]
        work = jnp.concatenate([x for x in parts if x.shape[0]], axis=0)
    return work


def eliminate(a_ref, g_ref, steps):
    size, rows_of_g = a_ref.shape[0], g_ref.shape[0]
    for k in steps:
        at, after = k * TILE, (k + 1) * TILE
        own = slice(at, after)
        inverse = invert_tile(a_ref[own, own])
        right = full(inverse, g_ref[own, :])
        g_ref[own, :] = right
        if after < size:
            old = a_ref[own, after:]
            panel = full(inverse, old)
            a_ref[own, after:] = panel
        for i in range(k + 1, size // TILE):
            rows = slice(i * TILE, (i + 1) * TILE)
            factor = old[:, (i - k - 1) * TILE : (i - k) * TILE]
            a_ref[rows, i * TILE :] = a_ref[rows, i * TILE :] - full(
                factor, panel[:, (i - k - 1) * TILE :], ((0,), (0,))
            )
            if (i + 1) * TILE <= rows_of_g:
                g_ref[rows, :] = g_ref[rows, :] - full(factor, right, ((0,), (0,)))
        for i in range(k):
            rows = slice(i * TILE, (i + 1) * TILE)
            factor = a_ref[rows, own]
            if after < size:
                a_ref[rows, after:] = a_ref[rows, after:] - full(factor, panel)
            g_ref[rows, :] = g_ref[rows, :] - full(factor, right)


def call(body, outs, scratch=(), **cost):
    return pl.pallas_call(
        body,
        out_shape=outs,
        scratch_shapes=list(scratch),
        compiler_params=pltpu.CompilerParams(vmem_limit_bytes=VMEM_LIMIT),
        **cost,
    )


def solve_body(a_ref, r_ref, g_ref, a_work):
    a_work[...] = a_ref[...]
    g_ref[...] = r_ref[...]
    eliminate(a_work, g_ref, range(a_ref.shape[0] // TILE))


def solve(a, r):
    return call(
        solve_body, jax.ShapeDtypeStruct(r.shape, F32), [pltpu.VMEM(a.shape, F32)]
    )(a, r)


def tile_block(q, i, j):
    return (slice(i * q, (i + 1) * q), slice(j * q, (j + 1) * q))


def put_sibling(m_ref, diag_ref, side_ref, base, mine):
    q = side_ref.shape[1]
    other = 2 - base

    def put(i, j, value):
        m_ref[tile_block(q, i, j)] = value
        if i != j:
            m_ref[tile_block(q, j, i)] = value.T

    first, cross, second = unpack_diagonal(diag_ref)
    put(base, base, first)
    put(base, base + 1, cross)
    put(base + 1, base + 1, second)
    put(base, other + 1, side_ref[0:q, :])
    sender = mine if base == 0 else 1 - mine

    @pl.when(sender == 0)
    def _():
        put(base, other, side_ref[q : 2 * q, :])

    @pl.when(sender != 0)
    def _():
        put(base + 1, other + 1, side_ref[q : 2 * q, :])


def pack_diagonal(first, cross, second):
    q = first.shape[0]
    e = q // 2
    lane = lax.broadcasted_iota(jnp.int32, (e, q), 1)
    corners = jnp.where(lane < e, second[0:e, :], first[e:, :])
    return [cross, first[0:e, :], second[e:, :], corners]


def unpack_diagonal(ref):
    q = ref.shape[1]
    e = q // 2
    upper, lower, corners = ref[q : q + e, :], ref[q + e : 2 * q, :], ref[2 * q : 2 * q + e, :]
    first = jnp.concatenate([upper, jnp.concatenate([upper.T[e:, :], corners[:, e:]], axis=1)], axis=0)
    second = jnp.concatenate([jnp.concatenate([corners[:, 0:e], lower.T[0:e, :]], axis=1), lower], axis=0)
    return first, ref[0:q, :], second


def prepare_body(half, t_ref, early_ref, near_ref, side_ref, column_ref, first_ref, a_out, m_out, p_out, outer_out):
    n, q = 2 * half, half // 2
    width = t_ref.shape[1] - n
    mine = first_ref[0]
    put_sibling(m_out, near_ref, side_ref, 0, mine)
    at = 5 * q // 2
    row = jnp.concatenate([near_ref[at + i : at + i + 1, :] for i in range(n // q)], axis=1)
    p_out[...] = jnp.where(column_ref[...] == row, 1.0, 0.0).astype(BF16)
    here = pl.ds(pl.multiple_of(width + mine * half, half), half)
    there = pl.ds(pl.multiple_of(width + (1 - mine) * half, half), half)
    a_out[0:half, 0:half] = t_ref[:, here]
    a_out[0:half, half:n] = t_ref[:, there]
    first, cross, second = unpack_diagonal(early_ref)
    a_out[tile_block(q, 2, 2)] = first
    a_out[tile_block(q, 2, 3)] = cross
    a_out[tile_block(q, 3, 3)] = second
    outer_out[...] = t_ref[:, column_blocks(half, mine)[0]]


def first_body(steps, a_in, m_in, p_ref, far_ref, side_ref, first_ref, a_out, b_out, m_work):
    n = a_in.shape[0]
    m_work[...] = m_in[...]
    put_sibling(m_work, far_ref, side_ref, 2, first_ref[0])
    moved = pick_right(m_work[...], p_ref[...], ((1,), (1,)))
    for i in range(n // TILE):
        rows, later = slice(i * TILE, (i + 1) * TILE), slice(i * TILE, n)
        a_out[rows, later] = a_in[rows, later] + pick_left(p_ref[rows, :], moved[:, later], ((1,), (0,)))
    top = b_out.shape[0]
    on_diagonal = [lax.broadcasted_iota(jnp.int32, (top, top), axis) for axis in (0, 1)]
    b_out[...] = jnp.where(on_diagonal[0] == on_diagonal[1], 1.0, 0.0).astype(F32)
    eliminate(a_out, b_out, steps)


def middle_body(steps, a_in, b_ref, t_ref, mine_ref, others_ref, first_ref, a_out, g_out):
    top, half = b_ref.shape[0], t_ref.shape[0]
    here, there = column_blocks(half, first_ref[0])
    a_out[...] = a_in[...]
    g_out[0:half, :] = t_ref[:, 0 : g_out.shape[1]]
    g_out[half:, here] = mine_ref[...]
    g_out[half:, there] = others_ref[...]
    first = g_out[0:top, :]
    g_out[top:, :] = g_out[top:, :] - full(a_in[0:top, top:], first, ((0,), (0,)))
    g_out[0:top, :] = full(b_ref[...], first)
    eliminate(a_out, g_out, steps)


def column_blocks(half, mine):
    return [pl.ds(pl.multiple_of(x * half, half), half) for x in (mine, 1 - mine)]


def last_body(steps, a_ref, g_in, g_out, a_work):
    a_work[...] = a_ref[...]
    g_out[...] = g_in[...]
    eliminate(a_work, g_out, steps)


def send_body(half, g_ref, p_ref, chunk_ref, first_ref, h_out, send_out):
    _, there = column_blocks(half, first_ref[0])
    h = pick_left(p_ref[...], g_ref[:, there], ((0,), (0,)))
    h_out[...] = h
    send_out[...] = -three_pass(h, chunk_ref[...], ((0,), (0,)))


def send_more_body(h_ref, chunk_ref, send_out):
    send_out[...] = -three_pass(h_ref[...], chunk_ref[...], ((0,), (0,)))


def output_body(
    half, g_ref, p_ref, t_ref, mine_ref, others_ref, ext_ref, row_ref, first_ref, chunk_a, chunk_b, own_ref, sol_ref, keep_ref
):
    n, q = 2 * half, half // 2
    mine = first_ref[0]
    here, there = column_blocks(half, mine)
    g = g_ref[...]
    left = jnp.concatenate([t_ref[:, here], mine_ref[...]], axis=0)
    own_ref[...] = ext_ref[...] - three_pass(left, g, ((0,), (0,)))
    target = lax.broadcasted_iota(jnp.int32, (half, n), 0) + mine * half
    onehot = jnp.where(row_ref[...].astype(jnp.int32) == target, 1.0, 0.0).astype(BF16)
    sol_ref[...] = -pick_left(onehot, g, ((1,), (0,)))
    h = pick_left(p_ref[...], g_ref[:, here], ((0,), (0,)))
    for i, chunk in enumerate((chunk_a, chunk_b)):
        keep_ref[:, i * q : (i + 1) * q] = -three_pass(h, chunk[...], ((0,), (0,)))


def cross_body(keep_ref, first_part, second_part, first_ref, out_ref):
    half, q = keep_ref.shape[0], first_part.shape[1]
    mine = first_ref[0]
    here, _ = column_blocks(half, mine)
    out_ref[:, here] = keep_ref[...]
    for i, part in enumerate((first_part, second_part)):
        out_ref[:, pl.ds(pl.multiple_of((1 - mine) * half + i * q, q), q)] = part[...]


def pack_iface_body(half, width, t_ref, map_ref, first_ref, diag_ref, side_ref, outer_ref, row_ref, column_ref):
    q, n = half // 2, 2 * half
    mine = first_ref[0]
    here, there = width + mine * half, width + (1 - mine) * half

    def cut(row, column):
        return t_ref[pl.ds(pl.multiple_of(row, q), q), pl.ds(pl.multiple_of(column, q), q)]

    at = 0
    for block in pack_diagonal(cut(0, here), cut(0, here + q), cut(q, here + q)):
        diag_ref[at : at + block.shape[0], :] = block
        at += block.shape[0]
    side_ref[0:q, :] = cut(0, there + q)
    side_ref[q : 2 * q, :] = cut(mine * q, there + mine * q)
    spans = column_blocks(half, mine)
    outer_ref[...] = t_ref[:, spans[1]]
    row = jnp.concatenate([map_ref[:, span] for span in spans], axis=1).astype(F32)
    row_ref[...] = row
    column_ref[...] = jnp.broadcast_to(row, (8, n)).T[:, 0:1]
    parts = [row[:, i * q : (i + 1) * q] for i in range(n // q)]
    diag_ref[at:, :] = jnp.concatenate(parts + parts, axis=0)[0:8, :]


def pack_outer_body(t_ref, mine_ref, first_ref, *chunks):
    half = t_ref.shape[0]
    mine = first_ref[0]
    for i, chunk in enumerate(chunks):
        width = chunk.shape[1]
        chunk[0:half, :] = t_ref[:, pl.ds(pl.multiple_of(mine * half + i * width, width), width)]
        chunk[half:, :] = mine_ref[:, i * width : (i + 1) * width]


def sibling(x):
    size = lax.axis_size("leaf")
    return lax.ppermute(x, "leaf", [(i, i ^ size // 2) for i in range(size)])


def across(x):
    return lax.ppermute(x, "sib", [(0, 1), (1, 0)])


def kernel(body, outs, places, scratch=(), flops=1e8):
    return pl.pallas_call(
        body,
        out_shape=outs,
        in_specs=[pl.BlockSpec(memory_space=place) for place in places],
        scratch_shapes=list(scratch),
        compiler_params=pltpu.CompilerParams(vmem_limit_bytes=VMEM_LIMIT),
        cost_estimate=pl.CostEstimate(flops=int(flops), bytes_accessed=1 << 20, transcendentals=0),
    )


def two_shards(t_int, t_ext, iface_map):
    t_int, t_ext = t_int[0], t_ext[0]
    half, n = t_int.shape[0], iface_map.shape[1]
    width = t_int.shape[1] - n
    tiles = n // TILE
    q = half // 2
    f = lambda *shape: jax.ShapeDtypeStruct(shape, F32)
    vmem, smem = pltpu.VMEM, pltpu.SMEM
    mine = lax.axis_index("sib").astype(jnp.int32)
    first = mine.reshape(1)
    diag, side, outer, own_row, column = kernel(
        functools.partial(pack_iface_body, half, width),
        (f(5 * q // 2 + 8, q), f(2 * q, q), f(half, half), f(1, n), f(n, 1)),
        [vmem, vmem, smem],
    )(t_int, iface_map, first)
    near = sibling(diag)
    diag_other = across(diag)
    far = across(near)
    near_side = sibling(side)
    outer_mine = across(outer)
    near, near_side = lax.optimization_barrier((near, near_side))
    far_side = across(near_side)
    chunks = kernel(pack_outer_body, [f(n, q)] * 2, [vmem, vmem, smem])(t_int, outer_mine, first)
    *chunks, _ = lax.optimization_barrier((*chunks, near_side))
    near_r = [sibling(chunk) for chunk in chunks]
    first_late, *_ = lax.optimization_barrier((first, *chunks))
    a, m, onehot, outer = kernel(
        functools.partial(prepare_body, half),
        (f(n, n), f(n, n), jax.ShapeDtypeStruct((n, n), BF16), f(half, half)),
        [vmem] * 5 + [smem],
    )(t_int, diag_other, near, near_side, column, first_late)
    outer_others = across(outer)
    top = tiles // 2 * TILE
    a, b = kernel(
        functools.partial(first_body, range(tiles // 2)),
        (f(n, n), f(top, top)),
        [vmem] * 5 + [smem],
        [pltpu.VMEM((n, n), F32)],
        10e9,
    )(a, m, onehot, far, far_side, first)
    a, g = kernel(
        functools.partial(middle_body, range(tiles // 2, tiles - 1)),
        (f(n, n), f(n, width)),
        [vmem] * 5 + [smem],
        (),
        5e9,
    )(a, b, t_int, outer_mine, outer_others, first)
    g = kernel(
        functools.partial(last_body, range(tiles - 1, tiles)), f(n, width), [vmem] * 2, [pltpu.VMEM((n, n), F32)], 5e9
    )(a, g)
    h, send = kernel(
        functools.partial(send_body, half), (f(n, half), f(half, q)), [vmem] * 3 + [smem], (), 1e9
    )(g, onehot, near_r[0], first)
    cross_a = across(send)
    cross_b = across(kernel(send_more_body, f(half, q), [vmem] * 2, (), 5e9)(h, near_r[1]))
    own_map, solution_op, keep = kernel(
        functools.partial(output_body, half),
        (f(half, width), f(half, width), f(half, half)),
        [vmem] * 7 + [smem] + [vmem] * 2,
        (),
        1e6,
    )(g, onehot, t_int, outer_mine, outer_others, t_ext, own_row, first, *near_r)
    cross_map = kernel(cross_body, f(half, width), [vmem] * 3 + [smem])(keep, cross_a, cross_b, first)
    return own_map[None], cross_map[None], solution_op[None]


def common_order(matrix, index_map):
    points = index_map.shape[0]
    inverse = jnp.zeros((points,), jnp.int32).at[index_map].set(jnp.arange(points, dtype=jnp.int32))
    picked = matrix[inverse]
    outer_width = matrix.shape[1] - points
    return (picked[:, :outer_width], picked[:, outer_width + inverse])


def many_shards(t_int, t_ext, iface_map):
    shard_rows = t_ext.shape[1]
    first_row = lax.axis_index("sib") * shard_rows
    near_rows, other_map = sibling((t_int, iface_map))
    own_rows = lax.all_gather(t_int, "sib", axis=1, tiled=True)
    other_rows = lax.all_gather(near_rows, "sib", axis=1, tiled=True)
    own_outer, own_iface = common_order(own_rows[0], iface_map[0])
    other_outer, other_iface = common_order(other_rows[0], other_map[0])
    g = solve(own_iface + other_iface, own_outer)
    product = lambda left, right: full(left, right, ((0,), (0,)))
    left = lax.dynamic_slice_in_dim(own_outer, first_row, shard_rows, 1)
    left_g = lax.dynamic_slice_in_dim(g, first_row, shard_rows, 1)
    own_map = t_ext - product(left, g)[None]
    cross_map = -product(left_g, other_outer)[None]
    solution_op = -lax.dynamic_slice_in_dim(g, first_row, shard_rows, 0)[None]
    return own_map, cross_map, solution_op


def solution(mesh):
    placed = P("leaf", "sib", None)
    return jax.shard_map(
        two_shards if mesh.shape["sib"] == 2 else many_shards,
        mesh=mesh,
        in_specs=(placed, placed, P("leaf", None)),
        out_specs=(placed, placed, placed),
        check_vma=False,
    )
```

```python
import functools

import jax
import jax.numpy as jnp
from jax import lax
from jax.experimental import pallas as pl
from jax.experimental.pallas import tpu as pltpu
from jax.sharding import PartitionSpec as P

F32 = jnp.float32
BF16 = jnp.bfloat16
TILE = 128
VMEM_LIMIT = 48 * 2**20


def split3(x):
    high = x.astype(BF16).astype(F32)
    rest = x - high
    middle = rest.astype(BF16).astype(F32)
    return high, middle, rest - middle


def contract(left, right, dims):
    return lax.dot_general(left, right, (dims, ((), ())), preferred_element_type=F32)


def full(left, right, dims=((1,), (0,))):
    return lax.dot_general(
        left, right, (dims, ((), ())), precision=lax.Precision.HIGHEST, preferred_element_type=F32
    )


def three_pass(left, right, dims):
    lh, rh = left.astype(BF16), right.astype(BF16)
    ll, rl = (left - lh.astype(F32)).astype(BF16), (right - rh.astype(F32)).astype(BF16)
    return contract(lh, rh, dims) + (contract(lh, rl, dims) + contract(ll, rh, dims))


def pick_left(onehot, x, dims):
    high, middle, low = (part.astype(BF16) for part in split3(x))
    return contract(onehot, high, dims) + (contract(onehot, middle, dims) + contract(onehot, low, dims))


def pick_right(x, onehot, dims):
    high, middle, low = (part.astype(BF16) for part in split3(x))
    return contract(high, onehot, dims) + (contract(middle, onehot, dims) + contract(low, onehot, dims))


def over_lanes(x, lane):
    return jnp.broadcast_to(x[:, lane : lane + 1], (8, TILE))


def over_rows(x, row):
    return jnp.broadcast_to(x[row : row + 1, :], (8, TILE))


def invert_tile(work, slabs=2):
    width = 8 * slabs
    lane = lax.broadcasted_iota(jnp.int32, (8, TILE), 1)
    row = lax.broadcasted_iota(jnp.int32, (8, TILE), 0)
    lane_all = lax.broadcasted_iota(jnp.int32, (TILE, TILE), 1)
    is_row = [row == j for j in range(8)]

    def slab_list(x, base):
        return [x[base + 8 * s : base + 8 * s + 8, :] for s in range(slabs)]

    old = slab_list(work, 0)
    for base in range(0, TILE, width):
        after = base + width
        columns = [[over_lanes(x, base + m) for x in old] for m in range(width)]
        following = slab_list(work, after) if after < TILE else []
        factors = [[over_lanes(x, base + m) for x in following] for m in range(width)]
        inside = (lane >= base) & (lane < after)
        new = [
            jnp.where(inside, jnp.where(lane - base - 8 * s == row, 1.0, 0.0).astype(F32), old[s])
            for s in range(slabs)
        ]
        corner = [over_rows(columns[0][0], 0), over_rows(columns[1][0], 0), over_rows(columns[1][0], 1)]
        scale = [None] * slabs
        for j in range(width):
            js, jr = divmod(j, 8)
            if j % 2 == 0:
                a, b, c = corner
                inverse = pltpu.reciprocal(a, approx=True)
                inverse_next = a * pltpu.reciprocal(a * c - b * b, approx=True)
            else:
                inverse = inverse_next
            scale[js] = inverse if jr == 0 else jnp.where(is_row[jr], inverse, scale[js])
            here = list(columns[j])
            here[js] = jnp.where(is_row[jr], 0.0, here[js])
            scaled = [c * inverse for c in here]
            for m in range(j + 1, width):
                picked = over_rows(columns[m][js], jr)
                if j % 2 == 1 and m <= j + 2:
                    columns[m] = [x - (h * picked) * inverse for x, h in zip(columns[m], here)]
                else:
                    columns[m] = [x - h * picked for x, h in zip(columns[m], scaled)]
            if j % 2 == 1 and j + 1 < width:
                ms, mr = divmod(j + 1, 8)
                left, right = columns[j + 1][ms], columns[j + 2][ms]
                corner = [over_rows(left, mr), over_rows(right, mr), over_rows(right, mr + 1)]
            picked = over_rows(new[js], jr)
            new = [x - h * picked for x, h in zip(new, scaled)]
        new = [x * y for x, y in zip(new, scale)]
        panel = jnp.concatenate(new, axis=0)
        sign = jnp.where(lane < base, -1.0, jnp.where(inside, 0.0, 1.0)).astype(F32)
        ah, am, al = split3(jnp.concatenate([x * sign for x in old], axis=0))
        bh, bm, bl = split3(panel)
        left = jnp.concatenate([ah, ah, am, am, ah, al], axis=0).astype(BF16)
        right = jnp.concatenate([bh, bm, bh, bm, bl, bh], axis=0).astype(BF16)
        change = contract(left, right, ((0,), (0,)))
        inside_all = (lane_all >= base) & (lane_all < after)
        rest = jnp.where(inside_all, 0.0, work) - change
        parts = [rest[:base], panel, rest[after:]]
        if following:
            rows = [over_rows(new[m // 8], m % 8) for m in range(width)]
            old = []
            for s in range(slabs):
                sums = []
                for q in range(4):
                    terms = [factors[m][s] * rows[m] for m in range(q, width, 4)]
                    sums.append(functools.reduce(lambda x, y: x + y, terms))
                old.append(jnp.where(inside, 0.0, following[s]) - ((sums[0] + sums[1]) + (sums[2] + sums[3])))
            parts = [rest[:base], panel, *old, rest[after + width :]]
        work = jnp.concatenate([x for x in parts if x.shape[0]], axis=0)
    return work


def eliminate(a_ref, g_ref, steps):
    size, rows_of_g = a_ref.shape[0], g_ref.shape[0]
    for k in steps:
        at, after = k * TILE, (k + 1) * TILE
        own = slice(at, after)
        inverse = invert_tile(a_ref[own, own])
        right = full(inverse, g_ref[own, :])
        g_ref[own, :] = right
        if after < size:
            old = a_ref[own, after:]
            panel = full(inverse, old)
            a_ref[own, after:] = panel
        for i in range(k + 1, size // TILE):
            rows = slice(i * TILE, (i + 1) * TILE)
            factor = old[:, (i - k - 1) * TILE : (i - k) * TILE]
            a_ref[rows, i * TILE :] = a_ref[rows, i * TILE :] - full(
                factor, panel[:, (i - k - 1) * TILE :], ((0,), (0,))
            )
            if (i + 1) * TILE <= rows_of_g:
                g_ref[rows, :] = g_ref[rows, :] - full(factor, right, ((0,), (0,)))
        for i in range(k):
            rows = slice(i * TILE, (i + 1) * TILE)
            factor = a_ref[rows, own]
            if after < size:
                a_ref[rows, after:] = a_ref[rows, after:] - full(factor, panel)
            g_ref[rows, :] = g_ref[rows, :] - full(factor, right)


def call(body, outs, scratch=(), **cost):
    return pl.pallas_call(
        body,
        out_shape=outs,
        scratch_shapes=list(scratch),
        compiler_params=pltpu.CompilerParams(vmem_limit_bytes=VMEM_LIMIT),
        **cost,
    )


def solve_body(a_ref, r_ref, g_ref, a_work):
    a_work[...] = a_ref[...]
    g_ref[...] = r_ref[...]
    eliminate(a_work, g_ref, range(a_ref.shape[0] // TILE))


def solve(a, r):
    return call(
        solve_body, jax.ShapeDtypeStruct(r.shape, F32), [pltpu.VMEM(a.shape, F32)]
    )(a, r)


def tile_block(q, i, j):
    return (slice(i * q, (i + 1) * q), slice(j * q, (j + 1) * q))


def put_sibling(m_ref, diag_ref, side_ref, base, mine):
    q = side_ref.shape[1]
    other = 2 - base

    def put(i, j, value):
        m_ref[tile_block(q, i, j)] = value
        if i != j:
            m_ref[tile_block(q, j, i)] = value.T

    first, cross, second = unpack_diagonal(diag_ref)
    put(base, base, first)
    put(base, base + 1, cross)
    put(base + 1, base + 1, second)
    put(base, other + 1, side_ref[0:q, :])
    sender = mine if base == 0 else 1 - mine

    @pl.when(sender == 0)
    def _():
        put(base, other, side_ref[q : 2 * q, :])

    @pl.when(sender != 0)
    def _():
        put(base + 1, other + 1, side_ref[q : 2 * q, :])


def pack_diagonal(first, cross, second):
    q = first.shape[0]
    e = q // 2
    lane = lax.broadcasted_iota(jnp.int32, (e, q), 1)
    corners = jnp.where(lane < e, second[0:e, :], first[e:, :])
    return [cross, first[0:e, :], second[e:, :], corners]


def unpack_diagonal(ref):
    q = ref.shape[1]
    e = q // 2
    upper, lower, corners = ref[q : q + e, :], ref[q + e : 2 * q, :], ref[2 * q : 2 * q + e, :]
    first = jnp.concatenate([upper, jnp.concatenate([upper.T[e:, :], corners[:, e:]], axis=1)], axis=0)
    second = jnp.concatenate([jnp.concatenate([corners[:, 0:e], lower.T[0:e, :]], axis=1), lower], axis=0)
    return first, ref[0:q, :], second


def prepare_body(half, t_ref, early_ref, near_ref, side_ref, column_ref, first_ref, a_out, m_out, p_out, outer_out):
    n, q = 2 * half, half // 2
    width = t_ref.shape[1] - n
    mine = first_ref[0]
    put_sibling(m_out, near_ref, side_ref, 0, mine)
    at = 5 * q // 2
    row = jnp.concatenate([near_ref[at + i : at + i + 1, :] for i in range(n // q)], axis=1)
    p_out[...] = jnp.where(column_ref[...] == row, 1.0, 0.0).astype(BF16)
    here = pl.ds(pl.multiple_of(width + mine * half, half), half)
    there = pl.ds(pl.multiple_of(width + (1 - mine) * half, half), half)
    a_out[0:half, 0:half] = t_ref[:, here]
    a_out[0:half, half:n] = t_ref[:, there]
    first, cross, second = unpack_diagonal(early_ref)
    a_out[tile_block(q, 2, 2)] = first
    a_out[tile_block(q, 2, 3)] = cross
    a_out[tile_block(q, 3, 3)] = second
    outer_out[...] = t_ref[:, column_blocks(half, mine)[0]]


def first_body(steps, a_in, m_in, p_ref, far_ref, side_ref, first_ref, a_out, b_out, scale_out, m_work):
    n = a_in.shape[0]
    m_work[...] = m_in[...]
    put_sibling(m_work, far_ref, side_ref, 2, first_ref[0])
    moved = pick_right(m_work[...], p_ref[...], ((1,), (1,)))
    tiles = [slice(i * TILE, (i + 1) * TILE) for i in range(n // TILE)]
    largest = [functools.reduce(jnp.maximum, [ref[tile, tile] for tile in tiles]) for ref in (a_in, m_work)]
    scale = lax.rsqrt(sum(jnp.max(x, axis=(0, 1), keepdims=True) for x in largest))
    scale_out[...] = jnp.broadcast_to(scale, scale_out.shape)
    for i, rows in enumerate(tiles):
        later = slice(i * TILE, n)
        both = a_in[rows, later] + pick_left(p_ref[rows, :], moved[:, later], ((1,), (0,)))
        a_out[rows, later] = both * scale
    top = b_out.shape[0]
    on_diagonal = [lax.broadcasted_iota(jnp.int32, (top, top), axis) for axis in (0, 1)]
    b_out[...] = jnp.where(on_diagonal[0] == on_diagonal[1], 1.0, 0.0).astype(F32)
    eliminate(a_out, b_out, steps)


def middle_body(k, a_ref, b_ref, t_ref, mine_ref, others_ref, scale_ref, first_ref, a_out, g_out):
    top, half, n, width = b_ref.shape[0], t_ref.shape[0], a_ref.shape[0], g_out.shape[1]
    own, last = slice(k * TILE, (k + 1) * TILE), slice((k + 1) * TILE, n)
    inverse = invert_tile(a_ref[own, own])
    here, there = column_blocks(half, first_ref[0])
    scale = scale_ref[0:1, 0:1]
    g_out[0:half, :] = t_ref[:, 0:width] * scale
    g_out[half:, here] = mine_ref[...] * scale
    g_out[half:, there] = others_ref[...] * scale
    first = g_out[0:top, :]
    rest = g_out[top:, :] - full(a_ref[0:top, top:], first, ((0,), (0,)))
    first = full(b_ref[...], first)
    old = a_ref[own, last]
    panel = full(inverse, old)
    a_out[last, last] = a_ref[last, last] - full(old, panel, ((0,), (0,)))
    right = full(inverse, rest[0:TILE, :])
    g_out[own, :] = right
    g_out[last, :] = rest[TILE:, :] - full(old, right, ((0,), (0,)))
    factor = a_ref[0:top, own]
    a_out[0:top, last] = a_ref[0:top, last] - full(factor, panel)
    a_out[own, last] = panel
    g_out[0:top, :] = first - full(factor, right)


def column_blocks(half, mine):
    return [pl.ds(pl.multiple_of(x * half, half), half) for x in (mine, 1 - mine)]


def last_body(k, a_ref, g_ref, g_out):
    own, before = slice(k * TILE, (k + 1) * TILE), slice(0, k * TILE)
    right = full(invert_tile(a_ref[own, own]), g_ref[own, :])
    g_out[own, :] = right
    g_out[before, :] = g_ref[before, :] - full(a_ref[before, own], right)


def send_body(half, g_ref, p_ref, chunk_ref, first_ref, h_out, send_out):
    _, there = column_blocks(half, first_ref[0])
    h = pick_left(p_ref[...], g_ref[:, there], ((0,), (0,)))
    h_out[...] = h
    send_out[...] = -three_pass(h, chunk_ref[...], ((0,), (0,)))


def send_more_body(h_ref, chunk_ref, send_out):
    send_out[...] = -three_pass(h_ref[...], chunk_ref[...], ((0,), (0,)))


def output_body(
    half, g_ref, p_ref, t_ref, mine_ref, others_ref, ext_ref, row_ref, first_ref, chunk_a, chunk_b, own_ref, sol_ref, keep_ref
):
    n, q = 2 * half, half // 2
    mine = first_ref[0]
    here, there = column_blocks(half, mine)
    g = g_ref[...]
    left = jnp.concatenate([t_ref[:, here], mine_ref[...]], axis=0)
    own_ref[...] = ext_ref[...] - three_pass(left, g, ((0,), (0,)))
    target = lax.broadcasted_iota(jnp.int32, (half, n), 0) + mine * half
    onehot = jnp.where(row_ref[...].astype(jnp.int32) == target, 1.0, 0.0).astype(BF16)
    sol_ref[...] = -pick_left(onehot, g, ((1,), (0,)))
    h = pick_left(p_ref[...], g_ref[:, here], ((0,), (0,)))
    for i, chunk in enumerate((chunk_a, chunk_b)):
        keep_ref[:, i * q : (i + 1) * q] = -three_pass(h, chunk[...], ((0,), (0,)))


def cross_body(keep_ref, first_part, second_part, first_ref, out_ref):
    half, q = keep_ref.shape[0], first_part.shape[1]
    mine = first_ref[0]
    here, _ = column_blocks(half, mine)
    out_ref[:, here] = keep_ref[...]
    for i, part in enumerate((first_part, second_part)):
        out_ref[:, pl.ds(pl.multiple_of((1 - mine) * half + i * q, q), q)] = part[...]


def pack_iface_body(half, width, t_ref, map_ref, first_ref, diag_ref, side_ref, outer_ref, row_ref, column_ref):
    q, n = half // 2, 2 * half
    mine = first_ref[0]
    here, there = width + mine * half, width + (1 - mine) * half

    def cut(row, column):
        return t_ref[pl.ds(pl.multiple_of(row, q), q), pl.ds(pl.multiple_of(column, q), q)]

    at = 0
    for block in pack_diagonal(cut(0, here), cut(0, here + q), cut(q, here + q)):
        diag_ref[at : at + block.shape[0], :] = block
        at += block.shape[0]
    side_ref[0:q, :] = cut(0, there + q)
    side_ref[q : 2 * q, :] = cut(mine * q, there + mine * q)
    spans = column_blocks(half, mine)
    outer_ref[...] = t_ref[:, spans[1]]
    row = jnp.concatenate([map_ref[:, span] for span in spans], axis=1).astype(F32)
    row_ref[...] = row
    column_ref[...] = jnp.broadcast_to(row, (8, n)).T[:, 0:1]
    parts = [row[:, i * q : (i + 1) * q] for i in range(n // q)]
    diag_ref[at:, :] = jnp.concatenate(parts + parts, axis=0)[0:8, :]


def pack_outer_body(t_ref, mine_ref, first_ref, *chunks):
    half = t_ref.shape[0]
    mine = first_ref[0]
    for i, chunk in enumerate(chunks):
        width = chunk.shape[1]
        chunk[0:half, :] = t_ref[:, pl.ds(pl.multiple_of(mine * half + i * width, width), width)]
        chunk[half:, :] = mine_ref[:, i * width : (i + 1) * width]


def sibling(x):
    size = lax.axis_size("leaf")
    return lax.ppermute(x, "leaf", [(i, i ^ size // 2) for i in range(size)])


def across(x):
    return lax.ppermute(x, "sib", [(0, 1), (1, 0)])


def kernel(body, outs, places, scratch=(), flops=1e8):
    return pl.pallas_call(
        body,
        out_shape=outs,
        in_specs=[pl.BlockSpec(memory_space=place) for place in places],
        scratch_shapes=list(scratch),
        compiler_params=pltpu.CompilerParams(vmem_limit_bytes=VMEM_LIMIT),
        cost_estimate=pl.CostEstimate(flops=int(flops), bytes_accessed=1 << 20, transcendentals=0),
    )


def two_shards(t_int, t_ext, iface_map):
    t_int, t_ext = t_int[0], t_ext[0]
    half, n = t_int.shape[0], iface_map.shape[1]
    width = t_int.shape[1] - n
    tiles = n // TILE
    q = half // 2
    f = lambda *shape: jax.ShapeDtypeStruct(shape, F32)
    vmem, smem = pltpu.VMEM, pltpu.SMEM
    mine = lax.axis_index("sib").astype(jnp.int32)
    first = mine.reshape(1)
    diag, side, outer, own_row, column = kernel(
        functools.partial(pack_iface_body, half, width),
        (f(5 * q // 2 + 8, q), f(2 * q, q), f(half, half), f(1, n), f(n, 1)),
        [vmem, vmem, smem],
    )(t_int, iface_map, first)
    near = sibling(diag)
    diag_other = across(diag)
    far = across(near)
    near_side = sibling(side)
    outer_mine = across(outer)
    near, near_side = lax.optimization_barrier((near, near_side))
    far_side = across(near_side)
    chunks = kernel(pack_outer_body, [f(n, q)] * 2, [vmem, vmem, smem])(t_int, outer_mine, first)
    *chunks, _ = lax.optimization_barrier((*chunks, near_side))
    near_r = [sibling(chunk) for chunk in chunks]
    first_late, *_ = lax.optimization_barrier((first, *chunks))
    a, m, onehot, outer = kernel(
        functools.partial(prepare_body, half),
        (f(n, n), f(n, n), jax.ShapeDtypeStruct((n, n), BF16), f(half, half)),
        [vmem] * 5 + [smem],
    )(t_int, diag_other, near, near_side, column, first_late)
    outer_others = across(outer)
    top = (tiles - 2) * TILE
    a, b, scale = kernel(
        functools.partial(first_body, range(tiles - 2)),
        (f(n, n), f(top, top), f(8, TILE)),
        [vmem] * 5 + [smem],
        [pltpu.VMEM((n, n), F32)],
        10e9,
    )(a, m, onehot, far, far_side, first)
    a, g = kernel(
        functools.partial(middle_body, tiles - 2), (f(n, n), f(n, width)), [vmem] * 6 + [smem], (), 5e9
    )(a, b, t_int, outer_mine, outer_others, scale, first)
    g = kernel(functools.partial(last_body, tiles - 1), f(n, width), [vmem] * 2, (), 5e9)(a, g)
    h, send = kernel(
        functools.partial(send_body, half), (f(n, half), f(half, q)), [vmem] * 3 + [smem], (), 1e9
    )(g, onehot, near_r[0], first)
    cross_a = across(send)
    cross_b = across(kernel(send_more_body, f(half, q), [vmem] * 2, (), 5e9)(h, near_r[1]))
    own_map, solution_op, keep = kernel(
        functools.partial(output_body, half),
        (f(half, width), f(half, width), f(half, half)),
        [vmem] * 7 + [smem] + [vmem] * 2,
        (),
        1e6,
    )(g, onehot, t_int, outer_mine, outer_others, t_ext, own_row, first, *near_r)
    cross_map = kernel(cross_body, f(half, width), [vmem] * 3 + [smem])(keep, cross_a, cross_b, first)
    return own_map[None], cross_map[None], solution_op[None]


def common_order(matrix, index_map):
    points = index_map.shape[0]
    inverse = jnp.zeros((points,), jnp.int32).at[index_map].set(jnp.arange(points, dtype=jnp.int32))
    picked = matrix[inverse]
    outer_width = matrix.shape[1] - points
    return (picked[:, :outer_width], picked[:, outer_width + inverse])


def many_shards(t_int, t_ext, iface_map):
    shard_rows = t_ext.shape[1]
    first_row = lax.axis_index("sib") * shard_rows
    near_rows, other_map = sibling((t_int, iface_map))
    own_rows = lax.all_gather(t_int, "sib", axis=1, tiled=True)
    other_rows = lax.all_gather(near_rows, "sib", axis=1, tiled=True)
    own_outer, own_iface = common_order(own_rows[0], iface_map[0])
    other_outer, other_iface = common_order(other_rows[0], other_map[0])
    g = solve(own_iface + other_iface, own_outer)
    product = lambda left, right: full(left, right, ((0,), (0,)))
    left = lax.dynamic_slice_in_dim(own_outer, first_row, shard_rows, 1)
    left_g = lax.dynamic_slice_in_dim(g, first_row, shard_rows, 1)
    own_map = t_ext - product(left, g)[None]
    cross_map = -product(left_g, other_outer)[None]
    solution_op = -lax.dynamic_slice_in_dim(g, first_row, shard_rows, 0)[None]
    return own_map, cross_map, solution_op


def solution(mesh):
    placed = P("leaf", "sib", None)
    return jax.shard_map(
        two_shards if mesh.shape["sib"] == 2 else many_shards,
        mesh=mesh,
        in_specs=(placed, placed, P("leaf", None)),
        out_specs=(placed, placed, placed),
        check_vma=False,
    )
```

```python
import functools

import jax
import jax.numpy as jnp
from jax import lax
from jax.experimental import pallas as pl
from jax.experimental.pallas import tpu as pltpu
from jax.sharding import PartitionSpec as P

F32 = jnp.float32
BF16 = jnp.bfloat16
TILE = 128
VMEM_LIMIT = 48 * 2**20


def split3(x):
    high = x.astype(BF16).astype(F32)
    rest = x - high
    middle = rest.astype(BF16).astype(F32)
    return high, middle, rest - middle


def contract(left, right, dims):
    return lax.dot_general(left, right, (dims, ((), ())), preferred_element_type=F32)


def full(left, right, dims=((1,), (0,))):
    return lax.dot_general(
        left, right, (dims, ((), ())), precision=lax.Precision.HIGHEST, preferred_element_type=F32
    )


def three_pass(left, right, dims):
    lh, rh = left.astype(BF16), right.astype(BF16)
    ll, rl = (left - lh.astype(F32)).astype(BF16), (right - rh.astype(F32)).astype(BF16)
    return contract(lh, rh, dims) + (contract(lh, rl, dims) + contract(ll, rh, dims))


def pick_left(onehot, x, dims):
    high, middle, low = (part.astype(BF16) for part in split3(x))
    return contract(onehot, high, dims) + (contract(onehot, middle, dims) + contract(onehot, low, dims))


def pick_right(x, onehot, dims):
    high, middle, low = (part.astype(BF16) for part in split3(x))
    return contract(high, onehot, dims) + (contract(middle, onehot, dims) + contract(low, onehot, dims))


def over_lanes(x, lane):
    return jnp.broadcast_to(x[:, lane : lane + 1], (8, TILE))


def over_rows(x, row):
    return jnp.broadcast_to(x[row : row + 1, :], (8, TILE))


def invert_tile(work, slabs=2):
    width = 8 * slabs
    lane = lax.broadcasted_iota(jnp.int32, (8, TILE), 1)
    row = lax.broadcasted_iota(jnp.int32, (8, TILE), 0)
    lane_all = lax.broadcasted_iota(jnp.int32, (TILE, TILE), 1)
    is_row = [row == j for j in range(8)]

    def slab_list(x, base):
        return [x[base + 8 * s : base + 8 * s + 8, :] for s in range(slabs)]

    old = slab_list(work, 0)
    for base in range(0, TILE, width):
        after = base + width
        columns = [[over_lanes(x, base + m) for x in old] for m in range(width)]
        following = slab_list(work, after) if after < TILE else []
        factors = [[over_lanes(x, base + m) for x in following] for m in range(width)]
        inside = (lane >= base) & (lane < after)
        new = [
            jnp.where(inside, jnp.where(lane - base - 8 * s == row, 1.0, 0.0).astype(F32), old[s])
            for s in range(slabs)
        ]
        corner = [over_rows(columns[0][0], 0), over_rows(columns[1][0], 0), over_rows(columns[1][0], 1)]
        scale = [None] * slabs
        for j in range(width):
            js, jr = divmod(j, 8)
            if j % 2 == 0:
                a, b, c = corner
                inverse = pltpu.reciprocal(a, approx=True)
                inverse_next = a * pltpu.reciprocal(a * c - b * b, approx=True)
            else:
                inverse = inverse_next
            scale[js] = inverse if jr == 0 else jnp.where(is_row[jr], inverse, scale[js])
            here = list(columns[j])
            here[js] = jnp.where(is_row[jr], 0.0, here[js])
            scaled = [c * inverse for c in here]
            for m in range(j + 1, width):
                picked = over_rows(columns[m][js], jr)
                if j % 2 == 1 and m <= j + 2:
                    columns[m] = [x - (h * picked) * inverse for x, h in zip(columns[m], here)]
                else:
                    columns[m] = [x - h * picked for x, h in zip(columns[m], scaled)]
            if j % 2 == 1 and j + 1 < width:
                ms, mr = divmod(j + 1, 8)
                left, right = columns[j + 1][ms], columns[j + 2][ms]
                corner = [over_rows(left, mr), over_rows(right, mr), over_rows(right, mr + 1)]
            picked = over_rows(new[js], jr)
            new = [x - h * picked for x, h in zip(new, scaled)]
        new = [x * y for x, y in zip(new, scale)]
        panel = jnp.concatenate(new, axis=0)
        sign = jnp.where(lane < base, -1.0, jnp.where(inside, 0.0, 1.0)).astype(F32)
        ah, am, al = split3(jnp.concatenate([x * sign for x in old], axis=0))
        bh, bm, bl = split3(panel)
        left = jnp.concatenate([ah, ah, am, am, ah, al], axis=0).astype(BF16)
        right = jnp.concatenate([bh, bm, bh, bm, bl, bh], axis=0).astype(BF16)
        change = contract(left, right, ((0,), (0,)))
        inside_all = (lane_all >= base) & (lane_all < after)
        rest = jnp.where(inside_all, 0.0, work) - change
        parts = [rest[:base], panel, rest[after:]]
        if following:
            rows = [over_rows(new[m // 8], m % 8) for m in range(width)]
            old = []
            for s in range(slabs):
                sums = []
                for q in range(4):
                    terms = [factors[m][s] * rows[m] for m in range(q, width, 4)]
                    sums.append(functools.reduce(lambda x, y: x + y, terms))
                old.append(jnp.where(inside, 0.0, following[s]) - ((sums[0] + sums[1]) + (sums[2] + sums[3])))
            parts = [rest[:base], panel, *old, rest[after + width :]]
        work = jnp.concatenate([x for x in parts if x.shape[0]], axis=0)
    return work


def eliminate(a_ref, g_ref, steps):
    size, rows_of_g = a_ref.shape[0], g_ref.shape[0]
    for k in steps:
        at, after = k * TILE, (k + 1) * TILE
        own = slice(at, after)
        inverse = invert_tile(a_ref[own, own])
        right = full(inverse, g_ref[own, :])
        g_ref[own, :] = right
        if after < size:
            old = a_ref[own, after:]
            panel = full(inverse, old)
            a_ref[own, after:] = panel
        for i in range(k + 1, size // TILE):
            rows = slice(i * TILE, (i + 1) * TILE)
            factor = old[:, (i - k - 1) * TILE : (i - k) * TILE]
            a_ref[rows, i * TILE :] = a_ref[rows, i * TILE :] - full(
                factor, panel[:, (i - k - 1) * TILE :], ((0,), (0,))
            )
            if (i + 1) * TILE <= rows_of_g:
                g_ref[rows, :] = g_ref[rows, :] - full(factor, right, ((0,), (0,)))
        for i in range(k):
            rows = slice(i * TILE, (i + 1) * TILE)
            factor = a_ref[rows, own]
            if after < size:
                a_ref[rows, after:] = a_ref[rows, after:] - full(factor, panel)
            g_ref[rows, :] = g_ref[rows, :] - full(factor, right)


def call(body, outs, scratch=(), **cost):
    return pl.pallas_call(
        body,
        out_shape=outs,
        scratch_shapes=list(scratch),
        compiler_params=pltpu.CompilerParams(vmem_limit_bytes=VMEM_LIMIT),
        **cost,
    )


def solve_body(a_ref, r_ref, g_ref, a_work):
    a_work[...] = a_ref[...]
    g_ref[...] = r_ref[...]
    eliminate(a_work, g_ref, range(a_ref.shape[0] // TILE))


def solve(a, r):
    return call(
        solve_body, jax.ShapeDtypeStruct(r.shape, F32), [pltpu.VMEM(a.shape, F32)]
    )(a, r)


def tile_block(q, i, j):
    return (slice(i * q, (i + 1) * q), slice(j * q, (j + 1) * q))


def put_sibling(m_ref, diag_ref, side_ref, base, mine):
    q = side_ref.shape[1]
    other = 2 - base

    def put(i, j, value):
        m_ref[tile_block(q, i, j)] = value
        if i != j:
            m_ref[tile_block(q, j, i)] = value.T

    first, cross, second = unpack_diagonal(diag_ref)
    put(base, base, first)
    put(base, base + 1, cross)
    put(base + 1, base + 1, second)
    put(base, other + 1, side_ref[0:q, :])
    sender = mine if base == 0 else 1 - mine

    @pl.when(sender == 0)
    def _():
        put(base, other, side_ref[q : 2 * q, :])

    @pl.when(sender != 0)
    def _():
        put(base + 1, other + 1, side_ref[q : 2 * q, :])


def pack_diagonal(first, cross, second):
    q = first.shape[0]
    e = q // 2
    lane = lax.broadcasted_iota(jnp.int32, (e, q), 1)
    corners = jnp.where(lane < e, second[0:e, :], first[e:, :])
    return [cross, first[0:e, :], second[e:, :], corners]


def unpack_diagonal(ref):
    q = ref.shape[1]
    e = q // 2
    upper, lower, corners = ref[q : q + e, :], ref[q + e : 2 * q, :], ref[2 * q : 2 * q + e, :]
    first = jnp.concatenate([upper, jnp.concatenate([upper.T[e:, :], corners[:, e:]], axis=1)], axis=0)
    second = jnp.concatenate([jnp.concatenate([corners[:, 0:e], lower.T[0:e, :]], axis=1), lower], axis=0)
    return first, ref[0:q, :], second


def prepare_body(half, t_ref, early_ref, near_ref, side_ref, column_ref, first_ref, a_out, m_out, p_out, outer_out):
    n, q = 2 * half, half // 2
    width = t_ref.shape[1] - n
    mine = first_ref[0]
    put_sibling(m_out, near_ref, side_ref, 0, mine)
    at = 5 * q // 2
    row = jnp.concatenate([near_ref[at + i : at + i + 1, :] for i in range(n // q)], axis=1)
    p_out[...] = jnp.where(column_ref[...] == row, 1.0, 0.0).astype(BF16)
    here = pl.ds(pl.multiple_of(width + mine * half, half), half)
    there = pl.ds(pl.multiple_of(width + (1 - mine) * half, half), half)
    a_out[0:half, 0:half] = t_ref[:, here]
    a_out[0:half, half:n] = t_ref[:, there]
    first, cross, second = unpack_diagonal(early_ref)
    a_out[tile_block(q, 2, 2)] = first
    a_out[tile_block(q, 2, 3)] = cross
    a_out[tile_block(q, 3, 3)] = second
    outer_out[...] = t_ref[:, column_blocks(half, mine)[0]]


def first_body(steps, a_in, m_in, p_ref, far_ref, side_ref, first_ref, a_out, b_out, scale_out, m_work):
    n = a_in.shape[0]
    m_work[...] = m_in[...]
    put_sibling(m_work, far_ref, side_ref, 2, first_ref[0])
    moved = pick_right(m_work[...], p_ref[...], ((1,), (1,)))
    tiles = [slice(i * TILE, (i + 1) * TILE) for i in range(n // TILE)]
    largest = [functools.reduce(jnp.maximum, [ref[tile, tile] for tile in tiles]) for ref in (a_in, m_work)]
    scale = lax.rsqrt(sum(jnp.max(x, axis=(0, 1), keepdims=True) for x in largest))
    scale_out[...] = jnp.broadcast_to(scale, scale_out.shape)
    for i, rows in enumerate(tiles):
        later = slice(i * TILE, n)
        both = a_in[rows, later] + pick_left(p_ref[rows, :], moved[:, later], ((1,), (0,)))
        a_out[rows, later] = both * scale
    top = b_out.shape[0]
    on_diagonal = [lax.broadcasted_iota(jnp.int32, (top, top), axis) for axis in (0, 1)]
    b_out[...] = jnp.where(on_diagonal[0] == on_diagonal[1], 1.0, 0.0).astype(F32)
    eliminate(a_out, b_out, steps)


def rest_body(k, a_ref, b_ref, t_ref, mine_ref, others_ref, p_ref, scale_ref, first_ref, g_out, h_out):
    top, half, n, width = b_ref.shape[0], t_ref.shape[0], a_ref.shape[0], g_out.shape[1]
    own, last, before = slice(k * TILE, (k + 1) * TILE), slice((k + 1) * TILE, n), slice(0, (k + 1) * TILE)
    here, there = column_blocks(half, first_ref[0])
    inverse = invert_tile(a_ref[own, own])
    old = a_ref[own, last]
    panel = full(inverse, old)
    inverse_last = invert_tile(a_ref[last, last] - full(old, panel, ((0,), (0,))))
    scale = scale_ref[0:1, 0:1]
    g_out[0:half, :] = t_ref[:, 0:width] * scale
    g_out[half:, here] = mine_ref[...] * scale
    g_out[half:, there] = others_ref[...] * scale
    first = g_out[0:top, :]
    rest = g_out[top:, :] - full(a_ref[0:top, top:], first, ((0,), (0,)))
    right = full(inverse, rest[0:TILE, :])
    bottom = rest[TILE:, :] - full(old, right, ((0,), (0,)))
    factor = a_ref[0:top, own]
    g_out[0:top, :] = full(b_ref[...], first) - full(factor, right)
    g_out[own, :] = right
    factors = jnp.concatenate([a_ref[0:top, last] - full(factor, panel), panel], axis=0)
    h = pick_left(p_ref[before, :], g_out[before, there], ((0,), (0,)))
    diagonal = [lax.broadcasted_iota(jnp.int32, (TILE, TILE), axis) for axis in (0, 1)]
    identity = jnp.where(diagonal[0] == diagonal[1], 1.0, 0.0).astype(BF16)
    change = contract(p_ref[last, :], identity, ((0,), (0,))) - pick_left(p_ref[before, :], factors, ((0,), (0,)))
    solved = full(inverse_last, bottom)
    g_out[last, :] = solved
    h_out[...] = h + full(change, g_out[last, there])
    g_out[before, :] = g_out[before, :] - full(factors, solved)


def column_blocks(half, mine):
    return [pl.ds(pl.multiple_of(x * half, half), half) for x in (mine, 1 - mine)]


def send_body(h_ref, chunk_ref, send_out):
    send_out[...] = -three_pass(h_ref[...], chunk_ref[...], ((0,), (0,)))


def output_body(
    half, g_ref, p_ref, t_ref, mine_ref, others_ref, ext_ref, row_ref, first_ref, chunk_a, chunk_b, own_ref, sol_ref, keep_ref
):
    n, q = 2 * half, half // 2
    mine = first_ref[0]
    here, there = column_blocks(half, mine)
    g = g_ref[...]
    left = jnp.concatenate([t_ref[:, here], mine_ref[...]], axis=0)
    own_ref[...] = ext_ref[...] - three_pass(left, g, ((0,), (0,)))
    target = lax.broadcasted_iota(jnp.int32, (half, n), 0) + mine * half
    onehot = jnp.where(row_ref[...].astype(jnp.int32) == target, 1.0, 0.0).astype(BF16)
    sol_ref[...] = -pick_left(onehot, g, ((1,), (0,)))
    h = pick_left(p_ref[...], g_ref[:, here], ((0,), (0,)))
    for i, chunk in enumerate((chunk_a, chunk_b)):
        keep_ref[:, i * q : (i + 1) * q] = -three_pass(h, chunk[...], ((0,), (0,)))


def cross_body(keep_ref, first_part, second_part, first_ref, out_ref):
    half, q = keep_ref.shape[0], first_part.shape[1]
    mine = first_ref[0]
    here, _ = column_blocks(half, mine)
    out_ref[:, here] = keep_ref[...]
    for i, part in enumerate((first_part, second_part)):
        out_ref[:, pl.ds(pl.multiple_of((1 - mine) * half + i * q, q), q)] = part[...]


def pack_iface_body(half, width, t_ref, map_ref, first_ref, diag_ref, side_ref, outer_ref, row_ref, column_ref):
    q, n = half // 2, 2 * half
    mine = first_ref[0]
    here, there = width + mine * half, width + (1 - mine) * half

    def cut(row, column):
        return t_ref[pl.ds(pl.multiple_of(row, q), q), pl.ds(pl.multiple_of(column, q), q)]

    at = 0
    for block in pack_diagonal(cut(0, here), cut(0, here + q), cut(q, here + q)):
        diag_ref[at : at + block.shape[0], :] = block
        at += block.shape[0]
    side_ref[0:q, :] = cut(0, there + q)
    side_ref[q : 2 * q, :] = cut(mine * q, there + mine * q)
    spans = column_blocks(half, mine)
    outer_ref[...] = t_ref[:, spans[1]]
    row = jnp.concatenate([map_ref[:, span] for span in spans], axis=1).astype(F32)
    row_ref[...] = row
    column_ref[...] = jnp.broadcast_to(row, (8, n)).T[:, 0:1]
    parts = [row[:, i * q : (i + 1) * q] for i in range(n // q)]
    diag_ref[at:, :] = jnp.concatenate(parts + parts, axis=0)[0:8, :]


def pack_outer_body(t_ref, mine_ref, first_ref, *chunks):
    half = t_ref.shape[0]
    mine = first_ref[0]
    for i, chunk in enumerate(chunks):
        width = chunk.shape[1]
        chunk[0:half, :] = t_ref[:, pl.ds(pl.multiple_of(mine * half + i * width, width), width)]
        chunk[half:, :] = mine_ref[:, i * width : (i + 1) * width]


def sibling(x):
    size = lax.axis_size("leaf")
    return lax.ppermute(x, "leaf", [(i, i ^ size // 2) for i in range(size)])


def across(x):
    return lax.ppermute(x, "sib", [(0, 1), (1, 0)])


def kernel(body, outs, places, scratch=(), flops=1e8):
    return pl.pallas_call(
        body,
        out_shape=outs,
        in_specs=[pl.BlockSpec(memory_space=place) for place in places],
        scratch_shapes=list(scratch),
        compiler_params=pltpu.CompilerParams(vmem_limit_bytes=VMEM_LIMIT),
        cost_estimate=pl.CostEstimate(flops=int(flops), bytes_accessed=1 << 20, transcendentals=0),
    )


def two_shards(t_int, t_ext, iface_map):
    t_int, t_ext = t_int[0], t_ext[0]
    half, n = t_int.shape[0], iface_map.shape[1]
    width = t_int.shape[1] - n
    tiles = n // TILE
    q = half // 2
    f = lambda *shape: jax.ShapeDtypeStruct(shape, F32)
    vmem, smem = pltpu.VMEM, pltpu.SMEM
    mine = lax.axis_index("sib").astype(jnp.int32)
    first = mine.reshape(1)
    diag, side, outer, own_row, column = kernel(
        functools.partial(pack_iface_body, half, width),
        (f(5 * q // 2 + 8, q), f(2 * q, q), f(half, half), f(1, n), f(n, 1)),
        [vmem, vmem, smem],
    )(t_int, iface_map, first)
    near = sibling(diag)
    diag_other = across(diag)
    far = across(near)
    near_side = sibling(side)
    outer_mine = across(outer)
    near, near_side = lax.optimization_barrier((near, near_side))
    far_side = across(near_side)
    chunks = kernel(pack_outer_body, [f(n, q)] * 2, [vmem, vmem, smem])(t_int, outer_mine, first)
    *chunks, _ = lax.optimization_barrier((*chunks, near_side))
    near_r = [sibling(chunk) for chunk in chunks]
    first_late, *_ = lax.optimization_barrier((first, *chunks))
    a, m, onehot, outer = kernel(
        functools.partial(prepare_body, half),
        (f(n, n), f(n, n), jax.ShapeDtypeStruct((n, n), BF16), f(half, half)),
        [vmem] * 5 + [smem],
    )(t_int, diag_other, near, near_side, column, first_late)
    outer_others = across(outer)
    top = (tiles - 2) * TILE
    a, b, scale = kernel(
        functools.partial(first_body, range(tiles - 2)),
        (f(n, n), f(top, top), f(8, TILE)),
        [vmem] * 5 + [smem],
        [pltpu.VMEM((n, n), F32)],
        10e9,
    )(a, m, onehot, far, far_side, first)
    g, h = kernel(
        functools.partial(rest_body, tiles - 2), (f(n, width), f(n, half)), [vmem] * 7 + [smem], (), 10e9
    )(a, b, t_int, outer_mine, outer_others, onehot, scale, first)
    cross_a, cross_b = [
        across(kernel(send_body, f(half, q), [vmem] * 2, (), 5e9)(h, chunk)) for chunk in near_r
    ]
    own_map, solution_op, keep = kernel(
        functools.partial(output_body, half),
        (f(half, width), f(half, width), f(half, half)),
        [vmem] * 7 + [smem] + [vmem] * 2,
        (),
        1e6,
    )(g, onehot, t_int, outer_mine, outer_others, t_ext, own_row, first, *near_r)
    cross_map = kernel(cross_body, f(half, width), [vmem] * 3 + [smem])(keep, cross_a, cross_b, first)
    return own_map[None], cross_map[None], solution_op[None]


def common_order(matrix, index_map):
    points = index_map.shape[0]
    inverse = jnp.zeros((points,), jnp.int32).at[index_map].set(jnp.arange(points, dtype=jnp.int32))
    picked = matrix[inverse]
    outer_width = matrix.shape[1] - points
    return (picked[:, :outer_width], picked[:, outer_width + inverse])


def many_shards(t_int, t_ext, iface_map):
    shard_rows = t_ext.shape[1]
    first_row = lax.axis_index("sib") * shard_rows
    near_rows, other_map = sibling((t_int, iface_map))
    own_rows = lax.all_gather(t_int, "sib", axis=1, tiled=True)
    other_rows = lax.all_gather(near_rows, "sib", axis=1, tiled=True)
    own_outer, own_iface = common_order(own_rows[0], iface_map[0])
    other_outer, other_iface = common_order(other_rows[0], other_map[0])
    g = solve(own_iface + other_iface, own_outer)
    product = lambda left, right: full(left, right, ((0,), (0,)))
    left = lax.dynamic_slice_in_dim(own_outer, first_row, shard_rows, 1)
    left_g = lax.dynamic_slice_in_dim(g, first_row, shard_rows, 1)
    own_map = t_ext - product(left, g)[None]
    cross_map = -product(left_g, other_outer)[None]
    solution_op = -lax.dynamic_slice_in_dim(g, first_row, shard_rows, 0)[None]
    return own_map, cross_map, solution_op


def solution(mesh):
    placed = P("leaf", "sib", None)
    return jax.shard_map(
        two_shards if mesh.shape["sib"] == 2 else many_shards,
        mesh=mesh,
        in_specs=(placed, placed, P("leaf", None)),
        out_specs=(placed, placed, placed),
        check_vma=False,
    )
```

```python
import functools

import jax
import jax.numpy as jnp
from jax import lax
from jax.experimental import pallas as pl
from jax.experimental.pallas import tpu as pltpu
from jax.sharding import PartitionSpec as P

F32 = jnp.float32
BF16 = jnp.bfloat16
TILE = 128
VMEM_LIMIT = 48 * 2**20


def split3(x):
    high = x.astype(BF16).astype(F32)
    rest = x - high
    middle = rest.astype(BF16).astype(F32)
    return high, middle, rest - middle


def contract(left, right, dims):
    return lax.dot_general(left, right, (dims, ((), ())), preferred_element_type=F32)


def full(left, right, dims=((1,), (0,))):
    (left_dim,), (right_dim,) = dims
    ah, am, al = (part.astype(BF16) for part in split3(left))
    bh, bm, bl = (part.astype(BF16) for part in split3(right))
    return contract(
        jnp.concatenate([ah, ah, am, am, ah, al], axis=left_dim),
        jnp.concatenate([bh, bm, bh, bm, bl, bh], axis=right_dim),
        dims,
    )


def three_pass(left, right, dims):
    lh, rh = left.astype(BF16), right.astype(BF16)
    ll, rl = (left - lh.astype(F32)).astype(BF16), (right - rh.astype(F32)).astype(BF16)
    return contract(lh, rh, dims) + (contract(lh, rl, dims) + contract(ll, rh, dims))


def pick_left(onehot, x, dims):
    high, middle, low = (part.astype(BF16) for part in split3(x))
    return contract(onehot, high, dims) + (contract(onehot, middle, dims) + contract(onehot, low, dims))


def pick_right(x, onehot, dims):
    high, middle, low = (part.astype(BF16) for part in split3(x))
    return contract(high, onehot, dims) + (contract(middle, onehot, dims) + contract(low, onehot, dims))


def over_lanes(x, lane):
    return jnp.broadcast_to(x[:, lane : lane + 1], (8, TILE))


def over_rows(x, row):
    return jnp.broadcast_to(x[row : row + 1, :], (8, TILE))


def invert_tile(work, slabs=2):
    width = 8 * slabs
    lane = lax.broadcasted_iota(jnp.int32, (8, TILE), 1)
    row = lax.broadcasted_iota(jnp.int32, (8, TILE), 0)
    lane_all = lax.broadcasted_iota(jnp.int32, (TILE, TILE), 1)
    is_row = [row == j for j in range(8)]

    def slab_list(x, base):
        return [x[base + 8 * s : base + 8 * s + 8, :] for s in range(slabs)]

    old = slab_list(work, 0)
    for base in range(0, TILE, width):
        after = base + width
        columns = [[over_lanes(x, base + m) for x in old] for m in range(width)]
        following = slab_list(work, after) if after < TILE else []
        factors = [[over_lanes(x, base + m) for x in following] for m in range(width)]
        inside = (lane >= base) & (lane < after)
        new = [
            jnp.where(inside, jnp.where(lane - base - 8 * s == row, 1.0, 0.0).astype(F32), old[s])
            for s in range(slabs)
        ]
        corner = [over_rows(columns[0][0], 0), over_rows(columns[1][0], 0), over_rows(columns[1][0], 1)]
        scale = [None] * slabs
        for j in range(width):
            js, jr = divmod(j, 8)
            if j % 2 == 0:
                a, b, c = corner
                inverse = pltpu.reciprocal(a, approx=True)
                inverse_next = a * pltpu.reciprocal(a * c - b * b, approx=True)
            else:
                inverse = inverse_next
            scale[js] = inverse if jr == 0 else jnp.where(is_row[jr], inverse, scale[js])
            here = list(columns[j])
            here[js] = jnp.where(is_row[jr], 0.0, here[js])
            scaled = [c * inverse for c in here]
            for m in range(j + 1, width):
                picked = over_rows(columns[m][js], jr)
                if j % 2 == 1 and m <= j + 2:
                    columns[m] = [x - (h * picked) * inverse for x, h in zip(columns[m], here)]
                else:
                    columns[m] = [x - h * picked for x, h in zip(columns[m], scaled)]
            if j % 2 == 1 and j + 1 < width:
                ms, mr = divmod(j + 1, 8)
                left, right = columns[j + 1][ms], columns[j + 2][ms]
                corner = [over_rows(left, mr), over_rows(right, mr), over_rows(right, mr + 1)]
            picked = over_rows(new[js], jr)
            new = [x - h * picked for x, h in zip(new, scaled)]
        new = [x * y for x, y in zip(new, scale)]
        panel = jnp.concatenate(new, axis=0)
        sign = jnp.where(lane < base, -1.0, jnp.where(inside, 0.0, 1.0)).astype(F32)
        ah, am, al = split3(jnp.concatenate([x * sign for x in old], axis=0))
        bh, bm, bl = split3(panel)
        left = jnp.concatenate([ah, ah, am, am, ah, al], axis=0).astype(BF16)
        right = jnp.concatenate([bh, bm, bh, bm, bl, bh], axis=0).astype(BF16)
        change = contract(left, right, ((0,), (0,)))
        inside_all = (lane_all >= base) & (lane_all < after)
        rest = jnp.where(inside_all, 0.0, work) - change
        parts = [rest[:base], panel, rest[after:]]
        if following:
            rows = [over_rows(new[m // 8], m % 8) for m in range(width)]
            old = []
            for s in range(slabs):
                sums = []
                for q in range(4):
                    terms = [factors[m][s] * rows[m] for m in range(q, width, 4)]
                    sums.append(functools.reduce(lambda x, y: x + y, terms))
                old.append(jnp.where(inside, 0.0, following[s]) - ((sums[0] + sums[1]) + (sums[2] + sums[3])))
            parts = [rest[:base], panel, *old, rest[after + width :]]
        work = jnp.concatenate([x for x in parts if x.shape[0]], axis=0)
    return work


def eliminate(a_ref, g_ref, steps):
    size, rows_of_g = a_ref.shape[0], g_ref.shape[0]
    for k in steps:
        at, after = k * TILE, (k + 1) * TILE
        own = slice(at, after)
        inverse = invert_tile(a_ref[own, own])
        right = full(inverse, g_ref[own, :])
        g_ref[own, :] = right
        if after < size:
            old = a_ref[own, after:]
            panel = full(inverse, old)
            a_ref[own, after:] = panel
        for i in range(k + 1, size // TILE):
            rows = slice(i * TILE, (i + 1) * TILE)
            factor = old[:, (i - k - 1) * TILE : (i - k) * TILE]
            a_ref[rows, i * TILE :] = a_ref[rows, i * TILE :] - full(
                factor, panel[:, (i - k - 1) * TILE :], ((0,), (0,))
            )
            if (i + 1) * TILE <= rows_of_g:
                g_ref[rows, :] = g_ref[rows, :] - full(factor, right, ((0,), (0,)))
        for i in range(k):
            rows = slice(i * TILE, (i + 1) * TILE)
            factor = a_ref[rows, own]
            if after < size:
                a_ref[rows, after:] = a_ref[rows, after:] - full(factor, panel)
            g_ref[rows, :] = g_ref[rows, :] - full(factor, right)


def call(body, outs, scratch=(), **cost):
    return pl.pallas_call(
        body,
        out_shape=outs,
        scratch_shapes=list(scratch),
        compiler_params=pltpu.CompilerParams(vmem_limit_bytes=VMEM_LIMIT),
        **cost,
    )


def solve_body(a_ref, r_ref, g_ref, a_work):
    a_work[...] = a_ref[...]
    g_ref[...] = r_ref[...]
    eliminate(a_work, g_ref, range(a_ref.shape[0] // TILE))


def solve(a, r):
    return call(
        solve_body, jax.ShapeDtypeStruct(r.shape, F32), [pltpu.VMEM(a.shape, F32)]
    )(a, r)


def tile_block(q, i, j):
    return (slice(i * q, (i + 1) * q), slice(j * q, (j + 1) * q))


def put_sibling(m_ref, diag_ref, side_ref, base, mine):
    q = side_ref.shape[1]
    other = 2 - base

    def put(i, j, value):
        m_ref[tile_block(q, i, j)] = value
        if i != j:
            m_ref[tile_block(q, j, i)] = value.T

    first, cross, second = unpack_diagonal(diag_ref)
    put(base, base, first)
    put(base, base + 1, cross)
    put(base + 1, base + 1, second)
    put(base, other + 1, side_ref[0:q, :])
    sender = mine if base == 0 else 1 - mine

    @pl.when(sender == 0)
    def _():
        put(base, other, side_ref[q : 2 * q, :])

    @pl.when(sender != 0)
    def _():
        put(base + 1, other + 1, side_ref[q : 2 * q, :])


def pack_diagonal(first, cross, second):
    q = first.shape[0]
    e = q // 2
    lane = lax.broadcasted_iota(jnp.int32, (e, q), 1)
    corners = jnp.where(lane < e, second[0:e, :], first[e:, :])
    return [cross, first[0:e, :], second[e:, :], corners]


def unpack_diagonal(ref):
    q = ref.shape[1]
    e = q // 2
    upper, lower, corners = ref[q : q + e, :], ref[q + e : 2 * q, :], ref[2 * q : 2 * q + e, :]
    first = jnp.concatenate([upper, jnp.concatenate([upper.T[e:, :], corners[:, e:]], axis=1)], axis=0)
    second = jnp.concatenate([jnp.concatenate([corners[:, 0:e], lower.T[0:e, :]], axis=1), lower], axis=0)
    return first, ref[0:q, :], second


def prepare_body(half, t_ref, early_ref, near_ref, side_ref, column_ref, first_ref, a_out, m_out, p_out, outer_out):
    n, q = 2 * half, half // 2
    width = t_ref.shape[1] - n
    mine = first_ref[0]
    put_sibling(m_out, near_ref, side_ref, 0, mine)
    at = 2 * q
    row = jnp.concatenate([side_ref[at + i : at + i + 1, :] for i in range(n // q)], axis=1)
    p_out[...] = jnp.where(column_ref[...] == row, 1.0, 0.0).astype(BF16)
    here = pl.ds(pl.multiple_of(width + mine * half, half), half)
    there = pl.ds(pl.multiple_of(width + (1 - mine) * half, half), half)
    a_out[0:half, 0:half] = t_ref[:, here]
    a_out[0:half, half:n] = t_ref[:, there]
    first, cross, second = unpack_diagonal(early_ref)
    a_out[tile_block(q, 2, 2)] = first
    a_out[tile_block(q, 2, 3)] = cross
    a_out[tile_block(q, 3, 3)] = second
    outer_out[...] = t_ref[:, column_blocks(half, mine)[0]]


def first_body(steps, a_in, m_in, p_ref, far_ref, side_ref, first_ref, a_out, b_out, scale_out, m_work):
    n = a_in.shape[0]
    m_work[...] = m_in[...]
    put_sibling(m_work, far_ref, side_ref, 2, first_ref[0])
    moved = pick_right(m_work[...], p_ref[...], ((1,), (1,)))
    tiles = [slice(i * TILE, (i + 1) * TILE) for i in range(n // TILE)]
    largest = [functools.reduce(jnp.maximum, [ref[tile, tile] for tile in tiles]) for ref in (a_in, m_work)]
    scale = lax.rsqrt(sum(jnp.max(x, axis=(0, 1), keepdims=True) for x in largest))
    scale_out[...] = jnp.broadcast_to(scale, scale_out.shape)
    for i, rows in enumerate(tiles):
        later = slice(i * TILE, n)
        both = a_in[rows, later] + pick_left(p_ref[rows, :], moved[:, later], ((1,), (0,)))
        a_out[rows, later] = both * scale
    top = b_out.shape[0]
    on_diagonal = [lax.broadcasted_iota(jnp.int32, (top, top), axis) for axis in (0, 1)]
    b_out[...] = jnp.where(on_diagonal[0] == on_diagonal[1], 1.0, 0.0).astype(F32)
    eliminate(a_out, b_out, steps)


def middle_body(k, a_ref, b_ref, t_ref, mine_ref, others_ref, scale_ref, first_ref, a_out, g_out):
    top, half, n, width = b_ref.shape[0], t_ref.shape[0], a_ref.shape[0], g_out.shape[1]
    own, last = slice(k * TILE, (k + 1) * TILE), slice((k + 1) * TILE, n)
    inverse = invert_tile(a_ref[own, own])
    here, there = column_blocks(half, first_ref[0])
    scale = scale_ref[0:1, 0:1]
    g_out[0:half, :] = t_ref[:, 0:width] * scale
    g_out[half:, here] = mine_ref[...] * scale
    g_out[half:, there] = others_ref[...] * scale
    first = g_out[0:top, :]
    rest = g_out[top:, :] - full(a_ref[0:top, top:], first, ((0,), (0,)))
    first = full(b_ref[...], first)
    old = a_ref[own, last]
    panel = full(inverse, old)
    a_out[last, last] = a_ref[last, last] - full(old, panel, ((0,), (0,)))
    right = full(inverse, rest[0:TILE, :])
    g_out[own, :] = right
    g_out[last, :] = rest[TILE:, :] - full(old, right, ((0,), (0,)))
    factor = a_ref[0:top, own]
    a_out[0:top, last] = a_ref[0:top, last] - full(factor, panel)
    a_out[own, last] = panel
    g_out[0:top, :] = first - full(factor, right)


def column_blocks(half, mine):
    return [pl.ds(pl.multiple_of(x * half, half), half) for x in (mine, 1 - mine)]


def last_body(k, a_ref, g_ref, g_out):
    own, before = slice(k * TILE, (k + 1) * TILE), slice(0, k * TILE)
    right = full(invert_tile(a_ref[own, own]), g_ref[own, :])
    g_out[own, :] = right
    g_out[before, :] = g_ref[before, :] - full(a_ref[before, own], right)


def send_body(half, g_ref, p_ref, chunk_ref, first_ref, h_out, send_out):
    _, there = column_blocks(half, first_ref[0])
    h = pick_left(p_ref[...], g_ref[:, there], ((0,), (0,)))
    h_out[...] = h
    send_out[...] = -three_pass(h, chunk_ref[...], ((0,), (0,)))


def send_more_body(h_ref, chunk_ref, send_out):
    send_out[...] = -three_pass(h_ref[...], chunk_ref[...], ((0,), (0,)))


def output_body(
    half, g_ref, p_ref, t_ref, mine_ref, others_ref, ext_ref, row_ref, first_ref, chunk_a, chunk_b, own_ref, sol_ref, keep_ref
):
    n, q = 2 * half, half // 2
    mine = first_ref[0]
    here, there = column_blocks(half, mine)
    g = g_ref[...]
    left = jnp.concatenate([t_ref[:, here], mine_ref[...]], axis=0)
    own_ref[...] = ext_ref[...] - three_pass(left, g, ((0,), (0,)))
    target = lax.broadcasted_iota(jnp.int32, (half, n), 0) + mine * half
    onehot = jnp.where(row_ref[...].astype(jnp.int32) == target, 1.0, 0.0).astype(BF16)
    sol_ref[...] = -pick_left(onehot, g, ((1,), (0,)))
    h = pick_left(p_ref[...], g_ref[:, here], ((0,), (0,)))
    for i, chunk in enumerate((chunk_a, chunk_b)):
        keep_ref[:, i * q : (i + 1) * q] = -three_pass(h, chunk[...], ((0,), (0,)))


def cross_body(keep_ref, first_part, second_part, first_ref, out_ref):
    half, q = keep_ref.shape[0], first_part.shape[1]
    mine = first_ref[0]
    here, _ = column_blocks(half, mine)
    out_ref[:, here] = keep_ref[...]
    for i, part in enumerate((first_part, second_part)):
        out_ref[:, pl.ds(pl.multiple_of((1 - mine) * half + i * q, q), q)] = part[...]


def cut(t_ref, q, row, column):
    return t_ref[pl.ds(pl.multiple_of(row, q), q), pl.ds(pl.multiple_of(column, q), q)]


def pack_diagonal_body(half, width, t_ref, first_ref, diag_ref):
    q = half // 2
    here = width + first_ref[0] * half
    at = 0
    for block in pack_diagonal(cut(t_ref, q, 0, here), cut(t_ref, q, 0, here + q), cut(t_ref, q, q, here + q)):
        diag_ref[at : at + block.shape[0], :] = block
        at += block.shape[0]


def pack_side_body(half, width, t_ref, map_ref, first_ref, side_ref, outer_ref, row_ref, column_ref):
    q, n = half // 2, 2 * half
    mine = first_ref[0]
    there = width + (1 - mine) * half
    side_ref[0:q, :] = cut(t_ref, q, 0, there + q)
    side_ref[q : 2 * q, :] = cut(t_ref, q, mine * q, there + mine * q)
    spans = column_blocks(half, mine)
    outer_ref[...] = t_ref[:, spans[1]]
    row = jnp.concatenate([map_ref[:, span] for span in spans], axis=1).astype(F32)
    row_ref[...] = row
    column_ref[...] = jnp.broadcast_to(row, (8, n)).T[:, 0:1]
    parts = [row[:, i * q : (i + 1) * q] for i in range(n // q)]
    side_ref[2 * q :, :] = jnp.concatenate(parts + parts, axis=0)[0:8, :]


def pack_outer_body(t_ref, mine_ref, first_ref, *chunks):
    half = t_ref.shape[0]
    mine = first_ref[0]
    for i, chunk in enumerate(chunks):
        width = chunk.shape[1]
        chunk[0:half, :] = t_ref[:, pl.ds(pl.multiple_of(mine * half + i * width, width), width)]
        chunk[half:, :] = mine_ref[:, i * width : (i + 1) * width]


def sibling(x):
    size = lax.axis_size("leaf")
    return lax.ppermute(x, "leaf", [(i, i ^ size // 2) for i in range(size)])


def across(x):
    return lax.ppermute(x, "sib", [(0, 1), (1, 0)])


def kernel(body, outs, places, scratch=(), flops=1e8):
    return pl.pallas_call(
        body,
        out_shape=outs,
        in_specs=[pl.BlockSpec(memory_space=place) for place in places],
        scratch_shapes=list(scratch),
        compiler_params=pltpu.CompilerParams(vmem_limit_bytes=VMEM_LIMIT),
        cost_estimate=pl.CostEstimate(flops=int(flops), bytes_accessed=1 << 20, transcendentals=0),
    )


def two_shards(t_int, t_ext, iface_map):
    t_int, t_ext = t_int[0], t_ext[0]
    half, n = t_int.shape[0], iface_map.shape[1]
    width = t_int.shape[1] - n
    tiles = n // TILE
    q = half // 2
    f = lambda *shape: jax.ShapeDtypeStruct(shape, F32)
    vmem, smem = pltpu.VMEM, pltpu.SMEM
    mine = lax.axis_index("sib").astype(jnp.int32)
    first = mine.reshape(1)
    diag = kernel(functools.partial(pack_diagonal_body, half, width), f(5 * q // 2, q), [vmem, smem])(t_int, first)
    side, outer, own_row, column = kernel(
        functools.partial(pack_side_body, half, width),
        (f(2 * q + 8, q), f(half, half), f(1, n), f(n, 1)),
        [vmem, vmem, smem],
    )(t_int, iface_map, first)
    near = sibling(diag)
    diag_other = across(diag)
    far = across(near)
    near_side = sibling(side)
    outer_mine = across(outer)
    near, near_side = lax.optimization_barrier((near, near_side))
    far_side = across(near_side)
    chunks = kernel(pack_outer_body, [f(n, q)] * 2, [vmem, vmem, smem])(t_int, outer_mine, first)
    *chunks, _ = lax.optimization_barrier((*chunks, near_side))
    near_r = [sibling(chunk) for chunk in chunks]
    first_late, *_ = lax.optimization_barrier((first, *chunks))
    a, m, onehot, outer = kernel(
        functools.partial(prepare_body, half),
        (f(n, n), f(n, n), jax.ShapeDtypeStruct((n, n), BF16), f(half, half)),
        [vmem] * 5 + [smem],
    )(t_int, diag_other, near, near_side, column, first_late)
    outer_others = across(outer)
    top = (tiles - 2) * TILE
    a, b, scale = kernel(
        functools.partial(first_body, range(tiles - 2)),
        (f(n, n), f(top, top), f(8, TILE)),
        [vmem] * 5 + [smem],
        [pltpu.VMEM((n, n), F32)],
        10e9,
    )(a, m, onehot, far, far_side, first)
    a, g = kernel(
        functools.partial(middle_body, tiles - 2), (f(n, n), f(n, width)), [vmem] * 6 + [smem], (), 5e9
    )(a, b, t_int, outer_mine, outer_others, scale, first)
    g = kernel(functools.partial(last_body, tiles - 1), f(n, width), [vmem] * 2, (), 5e9)(a, g)
    h, send = kernel(
        functools.partial(send_body, half), (f(n, half), f(half, q)), [vmem] * 3 + [smem], (), 1e9
    )(g, onehot, near_r[0], first)
    cross_a = across(send)
    cross_b = across(kernel(send_more_body, f(half, q), [vmem] * 2, (), 5e9)(h, near_r[1]))
    own_map, solution_op, keep = kernel(
        functools.partial(output_body, half),
        (f(half, width), f(half, width), f(half, half)),
        [vmem] * 7 + [smem] + [vmem] * 2,
        (),
        1e6,
    )(g, onehot, t_int, outer_mine, outer_others, t_ext, own_row, first, *near_r)
    cross_map = kernel(cross_body, f(half, width), [vmem] * 3 + [smem])(keep, cross_a, cross_b, first)
    return own_map[None], cross_map[None], solution_op[None]


def common_order(matrix, index_map):
    points = index_map.shape[0]
    inverse = jnp.zeros((points,), jnp.int32).at[index_map].set(jnp.arange(points, dtype=jnp.int32))
    picked = matrix[inverse]
    outer_width = matrix.shape[1] - points
    return (picked[:, :outer_width], picked[:, outer_width + inverse])


def many_shards(t_int, t_ext, iface_map):
    shard_rows = t_ext.shape[1]
    first_row = lax.axis_index("sib") * shard_rows
    near_rows, other_map = sibling((t_int, iface_map))
    own_rows = lax.all_gather(t_int, "sib", axis=1, tiled=True)
    other_rows = lax.all_gather(near_rows, "sib", axis=1, tiled=True)
    own_outer, own_iface = common_order(own_rows[0], iface_map[0])
    other_outer, other_iface = common_order(other_rows[0], other_map[0])
    g = solve(own_iface + other_iface, own_outer)
    product = lambda left, right: lax.dot_general(
        left, right, (((0,), (0,)), ((), ())), precision=lax.Precision.HIGHEST, preferred_element_type=F32
    )
    left = lax.dynamic_slice_in_dim(own_outer, first_row, shard_rows, 1)
    left_g = lax.dynamic_slice_in_dim(g, first_row, shard_rows, 1)
    own_map = t_ext - product(left, g)[None]
    cross_map = -product(left_g, other_outer)[None]
    solution_op = -lax.dynamic_slice_in_dim(g, first_row, shard_rows, 0)[None]
    return own_map, cross_map, solution_op


def solution(mesh):
    placed = P("leaf", "sib", None)
    return jax.shard_map(
        two_shards if mesh.shape["sib"] == 2 else many_shards,
        mesh=mesh,
        in_specs=(placed, placed, P("leaf", None)),
        out_specs=(placed, placed, placed),
        check_vma=False,
    )
```

```python
import functools

import jax
import jax.numpy as jnp
from jax import lax
from jax.experimental import pallas as pl
from jax.experimental.pallas import tpu as pltpu
from jax.sharding import PartitionSpec as P

F32 = jnp.float32
BF16 = jnp.bfloat16
TILE = 128
VMEM_LIMIT = 48 * 2**20


def split3(x):
    high = x.astype(BF16).astype(F32)
    rest = x - high
    middle = rest.astype(BF16).astype(F32)
    return high, middle, rest - middle


def contract(left, right, dims):
    return lax.dot_general(left, right, (dims, ((), ())), preferred_element_type=F32)


def full(left, right, dims=((1,), (0,))):
    (left_dim,), (right_dim,) = dims
    ah, am, al = (part.astype(BF16) for part in split3(left))
    bh, bm, bl = (part.astype(BF16) for part in split3(right))
    return contract(
        jnp.concatenate([ah, ah, am, am, ah, al], axis=left_dim),
        jnp.concatenate([bh, bm, bh, bm, bl, bh], axis=right_dim),
        dims,
    )


def three_pass(left, right, dims):
    (left_dim,), (right_dim,) = dims
    lh, rh = left.astype(BF16), right.astype(BF16)
    ll, rl = (left - lh.astype(F32)).astype(BF16), (right - rh.astype(F32)).astype(BF16)
    return contract(
        jnp.concatenate([lh, lh, ll], axis=left_dim), jnp.concatenate([rh, rl, rh], axis=right_dim), dims
    )


def pick_left(onehot, x, dims):
    (left_dim,), (right_dim,) = dims
    parts = [part.astype(BF16) for part in split3(x)]
    return contract(jnp.concatenate([onehot] * 3, axis=left_dim), jnp.concatenate(parts, axis=right_dim), dims)


def pick_right(x, onehot, dims):
    (left_dim,), (right_dim,) = dims
    parts = [part.astype(BF16) for part in split3(x)]
    return contract(jnp.concatenate(parts, axis=left_dim), jnp.concatenate([onehot] * 3, axis=right_dim), dims)


def over_lanes(x, lane):
    return jnp.broadcast_to(x[:, lane : lane + 1], (8, TILE))


def over_rows(x, row):
    return jnp.broadcast_to(x[row : row + 1, :], (8, TILE))


def invert_tile(work, slabs=2):
    width = 8 * slabs
    lane = lax.broadcasted_iota(jnp.int32, (8, TILE), 1)
    row = lax.broadcasted_iota(jnp.int32, (8, TILE), 0)
    lane_all = lax.broadcasted_iota(jnp.int32, (TILE, TILE), 1)
    is_row = [row == j for j in range(8)]

    def slab_list(x, base):
        return [x[base + 8 * s : base + 8 * s + 8, :] for s in range(slabs)]

    old = slab_list(work, 0)
    for base in range(0, TILE, width):
        after = base + width
        columns = [[over_lanes(x, base + m) for x in old] for m in range(width)]
        following = slab_list(work, after) if after < TILE else []
        factors = [[over_lanes(x, base + m) for x in following] for m in range(width)]
        inside = (lane >= base) & (lane < after)
        new = [
            jnp.where(inside, jnp.where(lane - base - 8 * s == row, 1.0, 0.0).astype(F32), old[s])
            for s in range(slabs)
        ]
        corner = [over_rows(columns[0][0], 0), over_rows(columns[1][0], 0), over_rows(columns[1][0], 1)]
        scale = [None] * slabs
        for j in range(width):
            js, jr = divmod(j, 8)
            if j % 2 == 0:
                a, b, c = corner
                inverse = pltpu.reciprocal(a, approx=True)
                inverse_next = a * pltpu.reciprocal(a * c - b * b, approx=True)
            else:
                inverse = inverse_next
            scale[js] = inverse if jr == 0 else jnp.where(is_row[jr], inverse, scale[js])
            here = list(columns[j])
            here[js] = jnp.where(is_row[jr], 0.0, here[js])
            scaled = [c * inverse for c in here]
            for m in range(j + 1, width):
                picked = over_rows(columns[m][js], jr)
                if j % 2 == 1 and m <= j + 2:
                    columns[m] = [x - (h * picked) * inverse for x, h in zip(columns[m], here)]
                else:
                    columns[m] = [x - h * picked for x, h in zip(columns[m], scaled)]
            if j % 2 == 1 and j + 1 < width:
                ms, mr = divmod(j + 1, 8)
                left, right = columns[j + 1][ms], columns[j + 2][ms]
                corner = [over_rows(left, mr), over_rows(right, mr), over_rows(right, mr + 1)]
            picked = over_rows(new[js], jr)
            new = [x - h * picked for x, h in zip(new, scaled)]
        new = [x * y for x, y in zip(new, scale)]
        panel = jnp.concatenate(new, axis=0)
        sign = jnp.where(lane < base, -1.0, jnp.where(inside, 0.0, 1.0)).astype(F32)
        ah, am, al = split3(jnp.concatenate([x * sign for x in old], axis=0))
        bh, bm, bl = split3(panel)
        left = jnp.concatenate([ah, ah, am, am, ah, al], axis=0).astype(BF16)
        right = jnp.concatenate([bh, bm, bh, bm, bl, bh], axis=0).astype(BF16)
        change = contract(left, right, ((0,), (0,)))
        inside_all = (lane_all >= base) & (lane_all < after)
        rest = jnp.where(inside_all, 0.0, work) - change
        parts = [rest[:base], panel, rest[after:]]
        if following:
            rows = [over_rows(new[m // 8], m % 8) for m in range(width)]
            old = []
            for s in range(slabs):
                sums = []
                for q in range(4):
                    terms = [factors[m][s] * rows[m] for m in range(q, width, 4)]
                    sums.append(functools.reduce(lambda x, y: x + y, terms))
                old.append(jnp.where(inside, 0.0, following[s]) - ((sums[0] + sums[1]) + (sums[2] + sums[3])))
            parts = [rest[:base], panel, *old, rest[after + width :]]
        work = jnp.concatenate([x for x in parts if x.shape[0]], axis=0)
    return work


def eliminate(a_ref, g_ref, steps):
    size, rows_of_g = a_ref.shape[0], g_ref.shape[0]
    for k in steps:
        at, after = k * TILE, (k + 1) * TILE
        own = slice(at, after)
        inverse = invert_tile(a_ref[own, own])
        right = full(inverse, g_ref[own, :])
        g_ref[own, :] = right
        if after < size:
            old = a_ref[own, after:]
            panel = full(inverse, old)
            a_ref[own, after:] = panel
        for i in range(k + 1, size // TILE):
            rows = slice(i * TILE, (i + 1) * TILE)
            factor = old[:, (i - k - 1) * TILE : (i - k) * TILE]
            a_ref[rows, i * TILE :] = a_ref[rows, i * TILE :] - full(
                factor, panel[:, (i - k - 1) * TILE :], ((0,), (0,))
            )
            if (i + 1) * TILE <= rows_of_g:
                g_ref[rows, :] = g_ref[rows, :] - full(factor, right, ((0,), (0,)))
        for i in range(k):
            rows = slice(i * TILE, (i + 1) * TILE)
            factor = a_ref[rows, own]
            if after < size:
                a_ref[rows, after:] = a_ref[rows, after:] - full(factor, panel)
            g_ref[rows, :] = g_ref[rows, :] - full(factor, right)


def call(body, outs, scratch=(), **cost):
    return pl.pallas_call(
        body,
        out_shape=outs,
        scratch_shapes=list(scratch),
        compiler_params=pltpu.CompilerParams(vmem_limit_bytes=VMEM_LIMIT),
        **cost,
    )


def solve_body(a_ref, r_ref, g_ref, a_work):
    a_work[...] = a_ref[...]
    g_ref[...] = r_ref[...]
    eliminate(a_work, g_ref, range(a_ref.shape[0] // TILE))


def solve(a, r):
    return call(
        solve_body, jax.ShapeDtypeStruct(r.shape, F32), [pltpu.VMEM(a.shape, F32)]
    )(a, r)


def tile_block(q, i, j):
    return (slice(i * q, (i + 1) * q), slice(j * q, (j + 1) * q))


def put_sibling(m_ref, diag_ref, side_ref, base, mine):
    q = side_ref.shape[1]
    other = 2 - base

    def put(i, j, value):
        m_ref[tile_block(q, i, j)] = value
        if i != j:
            m_ref[tile_block(q, j, i)] = value.T

    first, cross, second = unpack_diagonal(diag_ref)
    put(base, base, first)
    put(base, base + 1, cross)
    put(base + 1, base + 1, second)
    put(base, other + 1, side_ref[0:q, :])
    sender = mine if base == 0 else 1 - mine

    @pl.when(sender == 0)
    def _():
        put(base, other, side_ref[q : 2 * q, :])

    @pl.when(sender != 0)
    def _():
        put(base + 1, other + 1, side_ref[q : 2 * q, :])


def pack_diagonal(first, cross, second):
    q = first.shape[0]
    e = q // 2
    lane = lax.broadcasted_iota(jnp.int32, (e, q), 1)
    corners = jnp.where(lane < e, second[0:e, :], first[e:, :])
    return [cross, first[0:e, :], second[e:, :], corners]


def unpack_diagonal(ref):
    q = ref.shape[1]
    e = q // 2
    upper, lower, corners = ref[q : q + e, :], ref[q + e : 2 * q, :], ref[2 * q : 2 * q + e, :]
    first = jnp.concatenate([upper, jnp.concatenate([upper.T[e:, :], corners[:, e:]], axis=1)], axis=0)
    second = jnp.concatenate([jnp.concatenate([corners[:, 0:e], lower.T[0:e, :]], axis=1), lower], axis=0)
    return first, ref[0:q, :], second


def prepare_body(half, t_ref, early_ref, near_ref, side_ref, column_ref, first_ref, a_out, m_out, p_out, outer_out):
    n, q = 2 * half, half // 2
    width = t_ref.shape[1] - n
    mine = first_ref[0]
    put_sibling(m_out, near_ref, side_ref, 0, mine)
    at = 2 * q
    row = jnp.concatenate([side_ref[at + i : at + i + 1, :] for i in range(n // q)], axis=1)
    p_out[...] = jnp.where(column_ref[...] == row, 1.0, 0.0).astype(BF16)
    here = pl.ds(pl.multiple_of(width + mine * half, half), half)
    there = pl.ds(pl.multiple_of(width + (1 - mine) * half, half), half)
    a_out[0:half, 0:half] = t_ref[:, here]
    a_out[0:half, half:n] = t_ref[:, there]
    first, cross, second = unpack_diagonal(early_ref)
    a_out[tile_block(q, 2, 2)] = first
    a_out[tile_block(q, 2, 3)] = cross
    a_out[tile_block(q, 3, 3)] = second
    outer_out[...] = t_ref[:, column_blocks(half, mine)[0]]


def first_body(steps, a_in, m_in, p_ref, far_ref, side_ref, first_ref, a_out, b_out, scale_out, m_work):
    n = a_in.shape[0]
    m_work[...] = m_in[...]
    put_sibling(m_work, far_ref, side_ref, 2, first_ref[0])
    moved = pick_right(m_work[...], p_ref[...], ((1,), (1,)))
    tiles = [slice(i * TILE, (i + 1) * TILE) for i in range(n // TILE)]
    largest = [functools.reduce(jnp.maximum, [ref[tile, tile] for tile in tiles]) for ref in (a_in, m_work)]
    scale = lax.rsqrt(sum(jnp.max(x, axis=(0, 1), keepdims=True) for x in largest))
    scale_out[...] = jnp.broadcast_to(scale, scale_out.shape)
    for i, rows in enumerate(tiles):
        later = slice(i * TILE, n)
        both = a_in[rows, later] + pick_left(p_ref[rows, :], moved[:, later], ((1,), (0,)))
        a_out[rows, later] = both * scale
    top = b_out.shape[0]
    on_diagonal = [lax.broadcasted_iota(jnp.int32, (top, top), axis) for axis in (0, 1)]
    b_out[...] = jnp.where(on_diagonal[0] == on_diagonal[1], 1.0, 0.0).astype(F32)
    eliminate(a_out, b_out, steps)


def middle_body(k, a_ref, b_ref, t_ref, mine_ref, others_ref, scale_ref, first_ref, a_out, g_out):
    top, half, n, width = b_ref.shape[0], t_ref.shape[0], a_ref.shape[0], g_out.shape[1]
    own, last = slice(k * TILE, (k + 1) * TILE), slice((k + 1) * TILE, n)
    inverse = invert_tile(a_ref[own, own])
    here, there = column_blocks(half, first_ref[0])
    scale = scale_ref[0:1, 0:1]
    g_out[0:half, :] = t_ref[:, 0:width] * scale
    g_out[half:, here] = mine_ref[...] * scale
    g_out[half:, there] = others_ref[...] * scale
    first = g_out[0:top, :]
    rest = g_out[top:, :] - full(a_ref[0:top, top:], first, ((0,), (0,)))
    first = full(b_ref[...], first)
    old = a_ref[own, last]
    panel = full(inverse, old)
    a_out[last, last] = a_ref[last, last] - full(old, panel, ((0,), (0,)))
    right = full(inverse, rest[0:TILE, :])
    g_out[own, :] = right
    g_out[last, :] = rest[TILE:, :] - full(old, right, ((0,), (0,)))
    factor = a_ref[0:top, own]
    a_out[0:top, last] = a_ref[0:top, last] - full(factor, panel)
    a_out[own, last] = panel
    g_out[0:top, :] = first - full(factor, right)


def column_blocks(half, mine):
    return [pl.ds(pl.multiple_of(x * half, half), half) for x in (mine, 1 - mine)]


def last_body(k, a_ref, g_ref, g_out):
    own, before = slice(k * TILE, (k + 1) * TILE), slice(0, k * TILE)
    right = full(invert_tile(a_ref[own, own]), g_ref[own, :])
    g_out[own, :] = right
    g_out[before, :] = g_ref[before, :] - full(a_ref[before, own], right)


def send_body(half, g_ref, p_ref, chunk_ref, first_ref, h_out, send_out):
    _, there = column_blocks(half, first_ref[0])
    h = pick_left(p_ref[...], g_ref[:, there], ((0,), (0,)))
    h_out[...] = h
    send_out[...] = -three_pass(h, chunk_ref[...], ((0,), (0,)))


def send_more_body(h_ref, chunk_ref, send_out):
    send_out[...] = -three_pass(h_ref[...], chunk_ref[...], ((0,), (0,)))


def output_body(
    half, g_ref, p_ref, t_ref, mine_ref, others_ref, ext_ref, row_ref, first_ref, chunk_a, chunk_b, own_ref, sol_ref, keep_ref
):
    n, q = 2 * half, half // 2
    mine = first_ref[0]
    here, there = column_blocks(half, mine)
    g = g_ref[...]
    left = jnp.concatenate([t_ref[:, here], mine_ref[...]], axis=0)
    own_ref[...] = ext_ref[...] - three_pass(left, g, ((0,), (0,)))
    target = lax.broadcasted_iota(jnp.int32, (half, n), 0) + mine * half
    onehot = jnp.where(row_ref[...].astype(jnp.int32) == target, 1.0, 0.0).astype(BF16)
    sol_ref[...] = -pick_left(onehot, g, ((1,), (0,)))
    h = pick_left(p_ref[...], g_ref[:, here], ((0,), (0,)))
    for i, chunk in enumerate((chunk_a, chunk_b)):
        keep_ref[:, i * q : (i + 1) * q] = -three_pass(h, chunk[...], ((0,), (0,)))


def cross_body(keep_ref, first_part, second_part, first_ref, out_ref):
    half, q = keep_ref.shape[0], first_part.shape[1]
    mine = first_ref[0]
    here, _ = column_blocks(half, mine)
    out_ref[:, here] = keep_ref[...]
    for i, part in enumerate((first_part, second_part)):
        out_ref[:, pl.ds(pl.multiple_of((1 - mine) * half + i * q, q), q)] = part[...]


def cut(t_ref, q, row, column):
    return t_ref[pl.ds(pl.multiple_of(row, q), q), pl.ds(pl.multiple_of(column, q), q)]


def pack_diagonal_body(half, width, t_ref, first_ref, diag_ref):
    q = half // 2
    here = width + first_ref[0] * half
    at = 0
    for block in pack_diagonal(cut(t_ref, q, 0, here), cut(t_ref, q, 0, here + q), cut(t_ref, q, q, here + q)):
        diag_ref[at : at + block.shape[0], :] = block
        at += block.shape[0]


def pack_side_body(half, width, t_ref, map_ref, first_ref, side_ref, outer_ref, row_ref, column_ref):
    q, n = half // 2, 2 * half
    mine = first_ref[0]
    there = width + (1 - mine) * half
    side_ref[0:q, :] = cut(t_ref, q, 0, there + q)
    side_ref[q : 2 * q, :] = cut(t_ref, q, mine * q, there + mine * q)
    spans = column_blocks(half, mine)
    outer_ref[...] = t_ref[:, spans[1]]
    row = jnp.concatenate([map_ref[:, span] for span in spans], axis=1).astype(F32)
    row_ref[...] = row
    column_ref[...] = jnp.broadcast_to(row, (8, n)).T[:, 0:1]
    parts = [row[:, i * q : (i + 1) * q] for i in range(n // q)]
    side_ref[2 * q :, :] = jnp.concatenate(parts + parts, axis=0)[0:8, :]


def pack_outer_body(t_ref, mine_ref, first_ref, *chunks):
    half = t_ref.shape[0]
    mine = first_ref[0]
    for i, chunk in enumerate(chunks):
        width = chunk.shape[1]
        chunk[0:half, :] = t_ref[:, pl.ds(pl.multiple_of(mine * half + i * width, width), width)]
        chunk[half:, :] = mine_ref[:, i * width : (i + 1) * width]


def sibling(x):
    size = lax.axis_size("leaf")
    return lax.ppermute(x, "leaf", [(i, i ^ size // 2) for i in range(size)])


def across(x):
    return lax.ppermute(x, "sib", [(0, 1), (1, 0)])


def kernel(body, outs, places, scratch=(), flops=1e8):
    return pl.pallas_call(
        body,
        out_shape=outs,
        in_specs=[pl.BlockSpec(memory_space=place) for place in places],
        scratch_shapes=list(scratch),
        compiler_params=pltpu.CompilerParams(vmem_limit_bytes=VMEM_LIMIT),
        cost_estimate=pl.CostEstimate(flops=int(flops), bytes_accessed=1 << 20, transcendentals=0),
    )


def two_shards(t_int, t_ext, iface_map):
    t_int, t_ext = t_int[0], t_ext[0]
    half, n = t_int.shape[0], iface_map.shape[1]
    width = t_int.shape[1] - n
    tiles = n // TILE
    q = half // 2
    f = lambda *shape: jax.ShapeDtypeStruct(shape, F32)
    vmem, smem = pltpu.VMEM, pltpu.SMEM
    mine = lax.axis_index("sib").astype(jnp.int32)
    first = mine.reshape(1)
    diag = kernel(functools.partial(pack_diagonal_body, half, width), f(5 * q // 2, q), [vmem, smem])(t_int, first)
    side, outer, own_row, column = kernel(
        functools.partial(pack_side_body, half, width),
        (f(2 * q + 8, q), f(half, half), f(1, n), f(n, 1)),
        [vmem, vmem, smem],
    )(t_int, iface_map, first)
    near = sibling(diag)
    diag_other = across(diag)
    far = across(near)
    near_side = sibling(side)
    outer_mine = across(outer)
    near, near_side = lax.optimization_barrier((near, near_side))
    far_side = across(near_side)
    chunks = kernel(pack_outer_body, [f(n, q)] * 2, [vmem, vmem, smem])(t_int, outer_mine, first)
    first_late, *_ = lax.optimization_barrier((first, *chunks))
    a, m, onehot, outer = kernel(
        functools.partial(prepare_body, half),
        (f(n, n), f(n, n), jax.ShapeDtypeStruct((n, n), BF16), f(half, half)),
        [vmem] * 5 + [smem],
    )(t_int, diag_other, near, near_side, column, first_late)
    outer_others = across(outer)
    chunk_a, _ = lax.optimization_barrier((chunks[0], near_side))
    chunk_b, onehot = lax.optimization_barrier((chunks[1], onehot))
    near_r = [sibling(chunk_a), sibling(chunk_b)]
    top = (tiles - 2) * TILE
    a, b, scale = kernel(
        functools.partial(first_body, range(tiles - 2)),
        (f(n, n), f(top, top), f(8, TILE)),
        [vmem] * 5 + [smem],
        [pltpu.VMEM((n, n), F32)],
        10e9,
    )(a, m, onehot, far, far_side, first)
    a, g = kernel(
        functools.partial(middle_body, tiles - 2), (f(n, n), f(n, width)), [vmem] * 6 + [smem], (), 5e9
    )(a, b, t_int, outer_mine, outer_others, scale, first)
    g = kernel(functools.partial(last_body, tiles - 1), f(n, width), [vmem] * 2, (), 5e9)(a, g)
    h, send = kernel(
        functools.partial(send_body, half), (f(n, half), f(half, q)), [vmem] * 3 + [smem], (), 1e9
    )(g, onehot, near_r[0], first)
    cross_a = across(send)
    cross_b = across(kernel(send_more_body, f(half, q), [vmem] * 2, (), 5e9)(h, near_r[1]))
    own_map, solution_op, keep = kernel(
        functools.partial(output_body, half),
        (f(half, width), f(half, width), f(half, half)),
        [vmem] * 7 + [smem] + [vmem] * 2,
        (),
        1e6,
    )(g, onehot, t_int, outer_mine, outer_others, t_ext, own_row, first, *near_r)
    cross_map = kernel(cross_body, f(half, width), [vmem] * 3 + [smem])(keep, cross_a, cross_b, first)
    return own_map[None], cross_map[None], solution_op[None]


def common_order(matrix, index_map):
    points = index_map.shape[0]
    inverse = jnp.zeros((points,), jnp.int32).at[index_map].set(jnp.arange(points, dtype=jnp.int32))
    picked = matrix[inverse]
    outer_width = matrix.shape[1] - points
    return (picked[:, :outer_width], picked[:, outer_width + inverse])


def many_shards(t_int, t_ext, iface_map):
    shard_rows = t_ext.shape[1]
    first_row = lax.axis_index("sib") * shard_rows
    near_rows, other_map = sibling((t_int, iface_map))
    own_rows = lax.all_gather(t_int, "sib", axis=1, tiled=True)
    other_rows = lax.all_gather(near_rows, "sib", axis=1, tiled=True)
    own_outer, own_iface = common_order(own_rows[0], iface_map[0])
    other_outer, other_iface = common_order(other_rows[0], other_map[0])
    g = solve(own_iface + other_iface, own_outer)
    product = lambda left, right: lax.dot_general(
        left, right, (((0,), (0,)), ((), ())), precision=lax.Precision.HIGHEST, preferred_element_type=F32
    )
    left = lax.dynamic_slice_in_dim(own_outer, first_row, shard_rows, 1)
    left_g = lax.dynamic_slice_in_dim(g, first_row, shard_rows, 1)
    own_map = t_ext - product(left, g)[None]
    cross_map = -product(left_g, other_outer)[None]
    solution_op = -lax.dynamic_slice_in_dim(g, first_row, shard_rows, 0)[None]
    return own_map, cross_map, solution_op


def solution(mesh):
    placed = P("leaf", "sib", None)
    return jax.shard_map(
        two_shards if mesh.shape["sib"] == 2 else many_shards,
        mesh=mesh,
        in_specs=(placed, placed, P("leaf", None)),
        out_specs=(placed, placed, placed),
        check_vma=False,
    )
```

```python
import functools

import jax
import jax.numpy as jnp
from jax import lax
from jax.experimental import pallas as pl
from jax.experimental.pallas import tpu as pltpu
from jax.sharding import PartitionSpec as P

F32 = jnp.float32
BF16 = jnp.bfloat16
TILE = 128
VMEM_LIMIT = 48 * 2**20


def split3(x):
    high = x.astype(BF16).astype(F32)
    rest = x - high
    middle = rest.astype(BF16).astype(F32)
    return high, middle, rest - middle


def contract(left, right, dims):
    return lax.dot_general(left, right, (dims, ((), ())), preferred_element_type=F32)


def full(left, right, dims=((1,), (0,))):
    (left_dim,), (right_dim,) = dims
    ah, am, al = (part.astype(BF16) for part in split3(left))
    bh, bm, bl = (part.astype(BF16) for part in split3(right))
    return contract(
        jnp.concatenate([ah, ah, am, am, ah, al], axis=left_dim),
        jnp.concatenate([bh, bm, bh, bm, bl, bh], axis=right_dim),
        dims,
    )


def three_pass(left, right, dims):
    (left_dim,), (right_dim,) = dims
    lh, rh = left.astype(BF16), right.astype(BF16)
    ll, rl = (left - lh.astype(F32)).astype(BF16), (right - rh.astype(F32)).astype(BF16)
    return contract(
        jnp.concatenate([lh, lh, ll], axis=left_dim), jnp.concatenate([rh, rl, rh], axis=right_dim), dims
    )


def pick_left(onehot, x, dims):
    (left_dim,), (right_dim,) = dims
    parts = [part.astype(BF16) for part in split3(x)]
    return contract(jnp.concatenate([onehot] * 3, axis=left_dim), jnp.concatenate(parts, axis=right_dim), dims)


def pick_right(x, onehot, dims):
    (left_dim,), (right_dim,) = dims
    parts = [part.astype(BF16) for part in split3(x)]
    return contract(jnp.concatenate(parts, axis=left_dim), jnp.concatenate([onehot] * 3, axis=right_dim), dims)


def over_lanes(x, lane):
    return jnp.broadcast_to(x[:, lane : lane + 1], (8, TILE))


def over_rows(x, row):
    return jnp.broadcast_to(x[row : row + 1, :], (8, TILE))


def invert_tile(work, slabs=2):
    width = 8 * slabs
    lane = lax.broadcasted_iota(jnp.int32, (8, TILE), 1)
    row = lax.broadcasted_iota(jnp.int32, (8, TILE), 0)
    lane_all = lax.broadcasted_iota(jnp.int32, (TILE, TILE), 1)
    is_row = [row == j for j in range(8)]

    def slab_list(x, base):
        return [x[base + 8 * s : base + 8 * s + 8, :] for s in range(slabs)]

    old = slab_list(work, 0)
    for base in range(0, TILE, width):
        after = base + width
        columns = [[over_lanes(x, base + m) for x in old] for m in range(width)]
        following = slab_list(work, after) if after < TILE else []
        factors = [[over_lanes(x, base + m) for x in following] for m in range(width)]
        inside = (lane >= base) & (lane < after)
        new = [
            jnp.where(inside, jnp.where(lane - base - 8 * s == row, 1.0, 0.0).astype(F32), old[s])
            for s in range(slabs)
        ]
        corner = [over_rows(columns[0][0], 0), over_rows(columns[1][0], 0), over_rows(columns[1][0], 1)]
        scale = [None] * slabs
        for j in range(width):
            js, jr = divmod(j, 8)
            if j % 2 == 0:
                a, b, c = corner
                inverse = pltpu.reciprocal(a, approx=True)
                inverse_next = a * pltpu.reciprocal(a * c - b * b, approx=True)
            else:
                inverse = inverse_next
            scale[js] = inverse if jr == 0 else jnp.where(is_row[jr], inverse, scale[js])
            here = list(columns[j])
            here[js] = jnp.where(is_row[jr], 0.0, here[js])
            scaled = [c * inverse for c in here]
            for m in range(j + 1, width):
                picked = over_rows(columns[m][js], jr)
                if j % 2 == 1 and m <= j + 2:
                    columns[m] = [x - (h * picked) * inverse for x, h in zip(columns[m], here)]
                else:
                    columns[m] = [x - h * picked for x, h in zip(columns[m], scaled)]
            if j % 2 == 1 and j + 1 < width:
                ms, mr = divmod(j + 1, 8)
                left, right = columns[j + 1][ms], columns[j + 2][ms]
                corner = [over_rows(left, mr), over_rows(right, mr), over_rows(right, mr + 1)]
            picked = over_rows(new[js], jr)
            new = [x - h * picked for x, h in zip(new, scaled)]
        new = [x * y for x, y in zip(new, scale)]
        panel = jnp.concatenate(new, axis=0)
        sign = jnp.where(lane < base, -1.0, jnp.where(inside, 0.0, 1.0)).astype(F32)
        ah, am, al = split3(jnp.concatenate([x * sign for x in old], axis=0))
        bh, bm, bl = split3(panel)
        left = jnp.concatenate([ah, ah, am, am, ah, al], axis=0).astype(BF16)
        right = jnp.concatenate([bh, bm, bh, bm, bl, bh], axis=0).astype(BF16)
        change = contract(left, right, ((0,), (0,)))
        inside_all = (lane_all >= base) & (lane_all < after)
        rest = jnp.where(inside_all, 0.0, work) - change
        parts = [rest[:base], panel, rest[after:]]
        if following:
            rows = [over_rows(new[m // 8], m % 8) for m in range(width)]
            old = []
            for s in range(slabs):
                sums = []
                for q in range(4):
                    terms = [factors[m][s] * rows[m] for m in range(q, width, 4)]
                    sums.append(functools.reduce(lambda x, y: x + y, terms))
                old.append(jnp.where(inside, 0.0, following[s]) - ((sums[0] + sums[1]) + (sums[2] + sums[3])))
            parts = [rest[:base], panel, *old, rest[after + width :]]
        work = jnp.concatenate([x for x in parts if x.shape[0]], axis=0)
    return work


def eliminate(a_ref, g_ref, steps):
    size, rows_of_g = a_ref.shape[0], g_ref.shape[0]
    for k in steps:
        at, after = k * TILE, (k + 1) * TILE
        own = slice(at, after)
        inverse = invert_tile(a_ref[own, own])
        right = full(inverse, g_ref[own, :])
        g_ref[own, :] = right
        if after < size:
            old = a_ref[own, after:]
            panel = full(inverse, old)
            a_ref[own, after:] = panel
        for i in range(k + 1, size // TILE):
            rows = slice(i * TILE, (i + 1) * TILE)
            factor = old[:, (i - k - 1) * TILE : (i - k) * TILE]
            a_ref[rows, i * TILE :] = a_ref[rows, i * TILE :] - full(
                factor, panel[:, (i - k - 1) * TILE :], ((0,), (0,))
            )
            if (i + 1) * TILE <= rows_of_g:
                g_ref[rows, :] = g_ref[rows, :] - full(factor, right, ((0,), (0,)))
        for i in range(k):
            rows = slice(i * TILE, (i + 1) * TILE)
            factor = a_ref[rows, own]
            if after < size:
                a_ref[rows, after:] = a_ref[rows, after:] - full(factor, panel)
            g_ref[rows, :] = g_ref[rows, :] - full(factor, right)


def eliminate_two(a_ref, b_ref):
    size = a_ref.shape[0]
    first, second = slice(0, TILE), slice(TILE, 2 * TILE)

    def update(at, old, panel):
        for i in range(at, size // TILE):
            rows, offset = slice(i * TILE, (i + 1) * TILE), (i - at) * TILE
            factor = old[:, offset : offset + TILE]
            a_ref[rows, i * TILE :] = a_ref[rows, i * TILE :] - full(factor, panel[:, offset:], ((0,), (0,)))

    top = invert_tile(a_ref[first, first])
    old = a_ref[first, TILE:]
    panel = full(top, old)
    update(1, old, panel)
    cross, beyond = panel[:, :TILE], panel[:, TILE:]
    bottom = invert_tile(a_ref[second, second])
    old = a_ref[second, 2 * TILE :]
    panel = full(bottom, old)
    update(2, old, panel)
    a_ref[second, 2 * TILE :] = panel
    a_ref[first, 2 * TILE :] = beyond - full(cross, panel)
    side = full(cross, bottom)
    b_ref[first, first] = top + full(side, cross, ((1,), (1,)))
    b_ref[first, second] = -side
    b_ref[second, first] = -side.T
    b_ref[second, second] = bottom


def call(body, outs, scratch=(), **cost):
    return pl.pallas_call(
        body,
        out_shape=outs,
        scratch_shapes=list(scratch),
        compiler_params=pltpu.CompilerParams(vmem_limit_bytes=VMEM_LIMIT),
        **cost,
    )


def solve_body(a_ref, r_ref, g_ref, a_work):
    a_work[...] = a_ref[...]
    g_ref[...] = r_ref[...]
    eliminate(a_work, g_ref, range(a_ref.shape[0] // TILE))


def solve(a, r):
    return call(
        solve_body, jax.ShapeDtypeStruct(r.shape, F32), [pltpu.VMEM(a.shape, F32)]
    )(a, r)


def tile_block(q, i, j):
    return (slice(i * q, (i + 1) * q), slice(j * q, (j + 1) * q))


def put_sibling(m_ref, diag_ref, side_ref, base, mine):
    q = side_ref.shape[1]
    other = 2 - base

    def put(i, j, value):
        m_ref[tile_block(q, i, j)] = value
        if i != j:
            m_ref[tile_block(q, j, i)] = value.T

    first, cross, second = unpack_diagonal(diag_ref)
    put(base, base, first)
    put(base, base + 1, cross)
    put(base + 1, base + 1, second)
    put(base, other + 1, side_ref[0:q, :])
    sender = mine if base == 0 else 1 - mine

    @pl.when(sender == 0)
    def _():
        put(base, other, side_ref[q : 2 * q, :])

    @pl.when(sender != 0)
    def _():
        put(base + 1, other + 1, side_ref[q : 2 * q, :])


def pack_diagonal(first, cross, second):
    q = first.shape[0]
    e = q // 2
    lane = lax.broadcasted_iota(jnp.int32, (e, q), 1)
    corners = jnp.where(lane < e, second[0:e, :], first[e:, :])
    return [cross, first[0:e, :], second[e:, :], corners]


def unpack_diagonal(ref):
    q = ref.shape[1]
    e = q // 2
    upper, lower, corners = ref[q : q + e, :], ref[q + e : 2 * q, :], ref[2 * q : 2 * q + e, :]
    first = jnp.concatenate([upper, jnp.concatenate([upper.T[e:, :], corners[:, e:]], axis=1)], axis=0)
    second = jnp.concatenate([jnp.concatenate([corners[:, 0:e], lower.T[0:e, :]], axis=1), lower], axis=0)
    return first, ref[0:q, :], second


def prepare_body(half, t_ref, early_ref, near_ref, side_ref, column_ref, first_ref, a_out, m_out, p_out, outer_out):
    n, q = 2 * half, half // 2
    width = t_ref.shape[1] - n
    mine = first_ref[0]
    put_sibling(m_out, near_ref, side_ref, 0, mine)
    at = 2 * q
    row = jnp.concatenate([side_ref[at + i : at + i + 1, :] for i in range(n // q)], axis=1)
    p_out[...] = jnp.where(column_ref[...] == row, 1.0, 0.0).astype(BF16)
    here = pl.ds(pl.multiple_of(width + mine * half, half), half)
    there = pl.ds(pl.multiple_of(width + (1 - mine) * half, half), half)
    a_out[0:half, 0:half] = t_ref[:, here]
    a_out[0:half, half:n] = t_ref[:, there]
    first, cross, second = unpack_diagonal(early_ref)
    a_out[tile_block(q, 2, 2)] = first
    a_out[tile_block(q, 2, 3)] = cross
    a_out[tile_block(q, 3, 3)] = second
    outer_out[...] = t_ref[:, column_blocks(half, mine)[0]]


def first_body(a_in, m_in, p_ref, far_ref, side_ref, first_ref, a_out, b_out, scale_out, m_work):
    n = a_in.shape[0]
    m_work[...] = m_in[...]
    put_sibling(m_work, far_ref, side_ref, 2, first_ref[0])
    moved = pick_right(m_work[...], p_ref[...], ((1,), (1,)))
    tiles = [slice(i * TILE, (i + 1) * TILE) for i in range(n // TILE)]
    largest = [functools.reduce(jnp.maximum, [ref[tile, tile] for tile in tiles]) for ref in (a_in, m_work)]
    scale = lax.rsqrt(sum(jnp.max(x, axis=(0, 1), keepdims=True) for x in largest))
    scale_out[...] = jnp.broadcast_to(scale, scale_out.shape)
    for i, rows in enumerate(tiles):
        later = slice(i * TILE, n)
        both = a_in[rows, later] + pick_left(p_ref[rows, :], moved[:, later], ((1,), (0,)))
        a_out[rows, later] = both * scale
    eliminate_two(a_out, b_out)


def middle_body(k, a_ref, b_ref, t_ref, mine_ref, others_ref, scale_ref, first_ref, a_out, g_out):
    top, half, n, width = b_ref.shape[0], t_ref.shape[0], a_ref.shape[0], g_out.shape[1]
    own, last = slice(k * TILE, (k + 1) * TILE), slice((k + 1) * TILE, n)
    inverse = invert_tile(a_ref[own, own])
    here, there = column_blocks(half, first_ref[0])
    scale = scale_ref[0:1, 0:1]
    g_out[0:half, :] = t_ref[:, 0:width] * scale
    g_out[half:, here] = mine_ref[...] * scale
    g_out[half:, there] = others_ref[...] * scale
    first = g_out[0:top, :]
    rest = g_out[top:, :] - full(a_ref[0:top, top:], first, ((0,), (0,)))
    first = full(b_ref[...], first)
    old = a_ref[own, last]
    panel = full(inverse, old)
    a_out[last, last] = a_ref[last, last] - full(old, panel, ((0,), (0,)))
    right = full(inverse, rest[0:TILE, :])
    g_out[own, :] = right
    g_out[last, :] = rest[TILE:, :] - full(old, right, ((0,), (0,)))
    factor = a_ref[0:top, own]
    a_out[0:top, last] = a_ref[0:top, last] - full(factor, panel)
    a_out[own, last] = panel
    g_out[0:top, :] = first - full(factor, right)


def column_blocks(half, mine):
    return [pl.ds(pl.multiple_of(x * half, half), half) for x in (mine, 1 - mine)]


def last_body(k, a_ref, g_ref, g_out):
    own, before = slice(k * TILE, (k + 1) * TILE), slice(0, k * TILE)
    right = full(invert_tile(a_ref[own, own]), g_ref[own, :])
    g_out[own, :] = right
    g_out[before, :] = g_ref[before, :] - full(a_ref[before, own], right)


def send_body(half, g_ref, p_ref, chunk_ref, first_ref, h_out, send_out):
    _, there = column_blocks(half, first_ref[0])
    h = pick_left(p_ref[...], g_ref[:, there], ((0,), (0,)))
    h_out[...] = h
    send_out[...] = -three_pass(h, chunk_ref[...], ((0,), (0,)))


def send_more_body(h_ref, chunk_ref, send_out):
    send_out[...] = -three_pass(h_ref[...], chunk_ref[...], ((0,), (0,)))


def output_body(
    half, g_ref, p_ref, t_ref, mine_ref, others_ref, ext_ref, row_ref, first_ref, chunk_a, chunk_b, own_ref, sol_ref, keep_ref
):
    n, q = 2 * half, half // 2
    mine = first_ref[0]
    here, there = column_blocks(half, mine)
    g = g_ref[...]
    left = jnp.concatenate([t_ref[:, here], mine_ref[...]], axis=0)
    own_ref[...] = ext_ref[...] - three_pass(left, g, ((0,), (0,)))
    target = lax.broadcasted_iota(jnp.int32, (half, n), 0) + mine * half
    onehot = jnp.where(row_ref[...].astype(jnp.int32) == target, 1.0, 0.0).astype(BF16)
    sol_ref[...] = -pick_left(onehot, g, ((1,), (0,)))
    h = pick_left(p_ref[...], g_ref[:, here], ((0,), (0,)))
    for i, chunk in enumerate((chunk_a, chunk_b)):
        keep_ref[:, i * q : (i + 1) * q] = -three_pass(h, chunk[...], ((0,), (0,)))


def cross_body(keep_ref, first_part, second_part, first_ref, out_ref):
    half, q = keep_ref.shape[0], first_part.shape[1]
    mine = first_ref[0]
    here, _ = column_blocks(half, mine)
    out_ref[:, here] = keep_ref[...]
    for i, part in enumerate((first_part, second_part)):
        out_ref[:, pl.ds(pl.multiple_of((1 - mine) * half + i * q, q), q)] = part[...]


def cut(t_ref, q, row, column):
    return t_ref[pl.ds(pl.multiple_of(row, q), q), pl.ds(pl.multiple_of(column, q), q)]


def pack_diagonal_body(half, width, t_ref, first_ref, diag_ref):
    q = half // 2
    here = width + first_ref[0] * half
    at = 0
    for block in pack_diagonal(cut(t_ref, q, 0, here), cut(t_ref, q, 0, here + q), cut(t_ref, q, q, here + q)):
        diag_ref[at : at + block.shape[0], :] = block
        at += block.shape[0]


def pack_side_body(half, width, t_ref, map_ref, first_ref, side_ref, outer_ref, row_ref, column_ref):
    q, n = half // 2, 2 * half
    mine = first_ref[0]
    there = width + (1 - mine) * half
    side_ref[0:q, :] = cut(t_ref, q, 0, there + q)
    side_ref[q : 2 * q, :] = cut(t_ref, q, mine * q, there + mine * q)
    spans = column_blocks(half, mine)
    outer_ref[...] = t_ref[:, spans[1]]
    row = jnp.concatenate([map_ref[:, span] for span in spans], axis=1).astype(F32)
    row_ref[...] = row
    column_ref[...] = jnp.broadcast_to(row, (8, n)).T[:, 0:1]
    parts = [row[:, i * q : (i + 1) * q] for i in range(n // q)]
    side_ref[2 * q :, :] = jnp.concatenate(parts + parts, axis=0)[0:8, :]


def pack_outer_body(t_ref, mine_ref, first_ref, *chunks):
    half = t_ref.shape[0]
    mine = first_ref[0]
    for i, chunk in enumerate(chunks):
        width = chunk.shape[1]
        chunk[0:half, :] = t_ref[:, pl.ds(pl.multiple_of(mine * half + i * width, width), width)]
        chunk[half:, :] = mine_ref[:, i * width : (i + 1) * width]


def sibling(x):
    size = lax.axis_size("leaf")
    return lax.ppermute(x, "leaf", [(i, i ^ size // 2) for i in range(size)])


def across(x):
    return lax.ppermute(x, "sib", [(0, 1), (1, 0)])


def kernel(body, outs, places, scratch=(), flops=1e8):
    return pl.pallas_call(
        body,
        out_shape=outs,
        in_specs=[pl.BlockSpec(memory_space=place) for place in places],
        scratch_shapes=list(scratch),
        compiler_params=pltpu.CompilerParams(vmem_limit_bytes=VMEM_LIMIT),
        cost_estimate=pl.CostEstimate(flops=int(flops), bytes_accessed=1 << 20, transcendentals=0),
    )


def two_shards(t_int, t_ext, iface_map):
    t_int, t_ext = t_int[0], t_ext[0]
    half, n = t_int.shape[0], iface_map.shape[1]
    width = t_int.shape[1] - n
    tiles = n // TILE
    q = half // 2
    f = lambda *shape: jax.ShapeDtypeStruct(shape, F32)
    vmem, smem = pltpu.VMEM, pltpu.SMEM
    mine = lax.axis_index("sib").astype(jnp.int32)
    first = mine.reshape(1)
    diag = kernel(functools.partial(pack_diagonal_body, half, width), f(5 * q // 2, q), [vmem, smem])(t_int, first)
    side, outer, own_row, column = kernel(
        functools.partial(pack_side_body, half, width),
        (f(2 * q + 8, q), f(half, half), f(1, n), f(n, 1)),
        [vmem, vmem, smem],
    )(t_int, iface_map, first)
    near = sibling(diag)
    diag_other = across(diag)
    far = across(near)
    near_side = sibling(side)
    outer_mine = across(outer)
    near, near_side = lax.optimization_barrier((near, near_side))
    far_side = across(near_side)
    chunks = kernel(pack_outer_body, [f(n, q)] * 2, [vmem, vmem, smem])(t_int, outer_mine, first)
    first_late, *_ = lax.optimization_barrier((first, *chunks))
    a, m, onehot, outer = kernel(
        functools.partial(prepare_body, half),
        (f(n, n), f(n, n), jax.ShapeDtypeStruct((n, n), BF16), f(half, half)),
        [vmem] * 5 + [smem],
    )(t_int, diag_other, near, near_side, column, first_late)
    outer_others = across(outer)
    chunk_a, _ = lax.optimization_barrier((chunks[0], near_side))
    chunk_b, onehot = lax.optimization_barrier((chunks[1], onehot))
    near_r = [sibling(chunk_a), sibling(chunk_b)]
    top = 2 * TILE
    a, b, scale = kernel(
        first_body,
        (f(n, n), f(top, top), f(8, TILE)),
        [vmem] * 5 + [smem],
        [pltpu.VMEM((n, n), F32)],
        10e9,
    )(a, m, onehot, far, far_side, first)
    a, g = kernel(
        functools.partial(middle_body, tiles - 2), (f(n, n), f(n, width)), [vmem] * 6 + [smem], (), 5e9
    )(a, b, t_int, outer_mine, outer_others, scale, first)
    g = kernel(functools.partial(last_body, tiles - 1), f(n, width), [vmem] * 2, (), 5e9)(a, g)
    h, send = kernel(
        functools.partial(send_body, half), (f(n, half), f(half, q)), [vmem] * 3 + [smem], (), 1e9
    )(g, onehot, near_r[0], first)
    cross_a = across(send)
    cross_b = across(kernel(send_more_body, f(half, q), [vmem] * 2, (), 5e9)(h, near_r[1]))
    own_map, solution_op, keep = kernel(
        functools.partial(output_body, half),
        (f(half, width), f(half, width), f(half, half)),
        [vmem] * 7 + [smem] + [vmem] * 2,
        (),
        1e6,
    )(g, onehot, t_int, outer_mine, outer_others, t_ext, own_row, first, *near_r)
    cross_map = kernel(cross_body, f(half, width), [vmem] * 3 + [smem])(keep, cross_a, cross_b, first)
    return own_map[None], cross_map[None], solution_op[None]


def common_order(matrix, index_map):
    points = index_map.shape[0]
    inverse = jnp.zeros((points,), jnp.int32).at[index_map].set(jnp.arange(points, dtype=jnp.int32))
    picked = matrix[inverse]
    outer_width = matrix.shape[1] - points
    return (picked[:, :outer_width], picked[:, outer_width + inverse])


def many_shards(t_int, t_ext, iface_map):
    shard_rows = t_ext.shape[1]
    first_row = lax.axis_index("sib") * shard_rows
    near_rows, other_map = sibling((t_int, iface_map))
    own_rows = lax.all_gather(t_int, "sib", axis=1, tiled=True)
    other_rows = lax.all_gather(near_rows, "sib", axis=1, tiled=True)
    own_outer, own_iface = common_order(own_rows[0], iface_map[0])
    other_outer, other_iface = common_order(other_rows[0], other_map[0])
    g = solve(own_iface + other_iface, own_outer)
    product = lambda left, right: lax.dot_general(
        left, right, (((0,), (0,)), ((), ())), precision=lax.Precision.HIGHEST, preferred_element_type=F32
    )
    left = lax.dynamic_slice_in_dim(own_outer, first_row, shard_rows, 1)
    left_g = lax.dynamic_slice_in_dim(g, first_row, shard_rows, 1)
    own_map = t_ext - product(left, g)[None]
    cross_map = -product(left_g, other_outer)[None]
    solution_op = -lax.dynamic_slice_in_dim(g, first_row, shard_rows, 0)[None]
    return own_map, cross_map, solution_op


def solution(mesh):
    placed = P("leaf", "sib", None)
    return jax.shard_map(
        two_shards if mesh.shape["sib"] == 2 else many_shards,
        mesh=mesh,
        in_specs=(placed, placed, P("leaf", None)),
        out_specs=(placed, placed, placed),
        check_vma=False,
    )
```

```python
import functools

import jax
import jax.numpy as jnp
from jax import lax
from jax.experimental import pallas as pl
from jax.experimental.pallas import tpu as pltpu
from jax.sharding import PartitionSpec as P

F32 = jnp.float32
BF16 = jnp.bfloat16
TILE = 128
VMEM_LIMIT = 48 * 2**20


def split3(x):
    high = x.astype(BF16).astype(F32)
    rest = x - high
    middle = rest.astype(BF16).astype(F32)
    return high, middle, rest - middle


def contract(left, right, dims):
    return lax.dot_general(left, right, (dims, ((), ())), preferred_element_type=F32)


def full(left, right, dims=((1,), (0,))):
    (left_dim,), (right_dim,) = dims
    ah, am, al = (part.astype(BF16) for part in split3(left))
    bh, bm, bl = (part.astype(BF16) for part in split3(right))
    return contract(
        jnp.concatenate([ah, ah, am, am, ah, al], axis=left_dim),
        jnp.concatenate([bh, bm, bh, bm, bl, bh], axis=right_dim),
        dims,
    )


def three_pass(left, right, dims):
    (left_dim,), (right_dim,) = dims
    lh, rh = left.astype(BF16), right.astype(BF16)
    ll, rl = (left - lh.astype(F32)).astype(BF16), (right - rh.astype(F32)).astype(BF16)
    return contract(
        jnp.concatenate([lh, lh, ll], axis=left_dim), jnp.concatenate([rh, rl, rh], axis=right_dim), dims
    )


def pick_left(onehot, x, dims):
    (left_dim,), (right_dim,) = dims
    parts = [part.astype(BF16) for part in split3(x)]
    return contract(jnp.concatenate([onehot] * 3, axis=left_dim), jnp.concatenate(parts, axis=right_dim), dims)


def pick_right(x, onehot, dims):
    (left_dim,), (right_dim,) = dims
    parts = [part.astype(BF16) for part in split3(x)]
    return contract(jnp.concatenate(parts, axis=left_dim), jnp.concatenate([onehot] * 3, axis=right_dim), dims)


def over_lanes(x, lane):
    return jnp.broadcast_to(x[:, lane : lane + 1], (8, TILE))


def over_rows(x, row):
    return jnp.broadcast_to(x[row : row + 1, :], (8, TILE))


def invert_tile(work, slabs=2):
    width = 8 * slabs
    lane = lax.broadcasted_iota(jnp.int32, (8, TILE), 1)
    row = lax.broadcasted_iota(jnp.int32, (8, TILE), 0)
    lane_all = lax.broadcasted_iota(jnp.int32, (TILE, TILE), 1)
    is_row = [row == j for j in range(8)]

    def slab_list(x, base):
        return [x[base + 8 * s : base + 8 * s + 8, :] for s in range(slabs)]

    old = slab_list(work, 0)
    for base in range(0, TILE, width):
        after = base + width
        columns = [[over_lanes(x, base + m) for x in old] for m in range(width)]
        following = slab_list(work, after) if after < TILE else []
        factors = [[over_lanes(x, base + m) for x in following] for m in range(width)]
        inside = (lane >= base) & (lane < after)
        new = [
            jnp.where(inside, jnp.where(lane - base - 8 * s == row, 1.0, 0.0).astype(F32), old[s])
            for s in range(slabs)
        ]
        corner = [over_rows(columns[0][0], 0), over_rows(columns[1][0], 0), over_rows(columns[1][0], 1)]
        scale = [None] * slabs
        for j in range(width):
            js, jr = divmod(j, 8)
            if j % 2 == 0:
                a, b, c = corner
                inverse = pltpu.reciprocal(a, approx=True)
                inverse_next = a * pltpu.reciprocal(a * c - b * b, approx=True)
            else:
                inverse = inverse_next
            scale[js] = inverse if jr == 0 else jnp.where(is_row[jr], inverse, scale[js])
            here = list(columns[j])
            here[js] = jnp.where(is_row[jr], 0.0, here[js])
            scaled = [c * inverse for c in here]
            for m in range(j + 1, width):
                picked = over_rows(columns[m][js], jr)
                if j % 2 == 1 and m <= j + 2:
                    columns[m] = [x - (h * picked) * inverse for x, h in zip(columns[m], here)]
                else:
                    columns[m] = [x - h * picked for x, h in zip(columns[m], scaled)]
            if j % 2 == 1 and j + 1 < width:
                ms, mr = divmod(j + 1, 8)
                left, right = columns[j + 1][ms], columns[j + 2][ms]
                corner = [over_rows(left, mr), over_rows(right, mr), over_rows(right, mr + 1)]
            picked = over_rows(new[js], jr)
            new = [x - h * picked for x, h in zip(new, scaled)]
        new = [x * y for x, y in zip(new, scale)]
        panel = jnp.concatenate(new, axis=0)
        sign = jnp.where(lane < base, -1.0, jnp.where(inside, 0.0, 1.0)).astype(F32)
        ah, am, al = split3(jnp.concatenate([x * sign for x in old], axis=0))
        bh, bm, bl = split3(panel)
        left = jnp.concatenate([ah, ah, am, am, ah, al], axis=0).astype(BF16)
        right = jnp.concatenate([bh, bm, bh, bm, bl, bh], axis=0).astype(BF16)
        change = contract(left, right, ((0,), (0,)))
        inside_all = (lane_all >= base) & (lane_all < after)
        rest = jnp.where(inside_all, 0.0, work) - change
        parts = [rest[:base], panel, rest[after:]]
        if following:
            rows = [over_rows(new[m // 8], m % 8) for m in range(width)]
            old = []
            for s in range(slabs):
                sums = []
                for q in range(4):
                    terms = [factors[m][s] * rows[m] for m in range(q, width, 4)]
                    sums.append(functools.reduce(lambda x, y: x + y, terms))
                old.append(jnp.where(inside, 0.0, following[s]) - ((sums[0] + sums[1]) + (sums[2] + sums[3])))
            parts = [rest[:base], panel, *old, rest[after + width :]]
        work = jnp.concatenate([x for x in parts if x.shape[0]], axis=0)
    return work


def eliminate(a_ref, g_ref, steps):
    size, rows_of_g = a_ref.shape[0], g_ref.shape[0]
    for k in steps:
        at, after = k * TILE, (k + 1) * TILE
        own = slice(at, after)
        inverse = invert_tile(a_ref[own, own])
        right = full(inverse, g_ref[own, :])
        g_ref[own, :] = right
        if after < size:
            old = a_ref[own, after:]
            panel = full(inverse, old)
            a_ref[own, after:] = panel
        for i in range(k + 1, size // TILE):
            rows = slice(i * TILE, (i + 1) * TILE)
            factor = old[:, (i - k - 1) * TILE : (i - k) * TILE]
            a_ref[rows, i * TILE :] = a_ref[rows, i * TILE :] - full(
                factor, panel[:, (i - k - 1) * TILE :], ((0,), (0,))
            )
            if (i + 1) * TILE <= rows_of_g:
                g_ref[rows, :] = g_ref[rows, :] - full(factor, right, ((0,), (0,)))
        for i in range(k):
            rows = slice(i * TILE, (i + 1) * TILE)
            factor = a_ref[rows, own]
            if after < size:
                a_ref[rows, after:] = a_ref[rows, after:] - full(factor, panel)
            g_ref[rows, :] = g_ref[rows, :] - full(factor, right)


def call(body, outs, scratch=(), **cost):
    return pl.pallas_call(
        body,
        out_shape=outs,
        scratch_shapes=list(scratch),
        compiler_params=pltpu.CompilerParams(vmem_limit_bytes=VMEM_LIMIT),
        **cost,
    )


def solve_body(a_ref, r_ref, g_ref, a_work):
    a_work[...] = a_ref[...]
    g_ref[...] = r_ref[...]
    eliminate(a_work, g_ref, range(a_ref.shape[0] // TILE))


def solve(a, r):
    return call(
        solve_body, jax.ShapeDtypeStruct(r.shape, F32), [pltpu.VMEM(a.shape, F32)]
    )(a, r)


def tile_block(q, i, j):
    return (slice(i * q, (i + 1) * q), slice(j * q, (j + 1) * q))


def put_sibling(m_ref, diag_ref, side_ref, base, mine):
    q = side_ref.shape[1]
    other = 2 - base

    def put(i, j, value):
        m_ref[tile_block(q, i, j)] = value
        if i != j:
            m_ref[tile_block(q, j, i)] = value.T

    first, cross, second = unpack_diagonal(diag_ref)
    put(base, base, first)
    put(base, base + 1, cross)
    put(base + 1, base + 1, second)
    put(base, other + 1, side_ref[0:q, :])
    sender = mine if base == 0 else 1 - mine

    @pl.when(sender == 0)
    def _():
        put(base, other, side_ref[q : 2 * q, :])

    @pl.when(sender != 0)
    def _():
        put(base + 1, other + 1, side_ref[q : 2 * q, :])


def pack_diagonal(first, cross, second):
    q = first.shape[0]
    e = q // 2
    lane = lax.broadcasted_iota(jnp.int32, (e, q), 1)
    corners = jnp.where(lane < e, second[0:e, :], first[e:, :])
    return [cross, first[0:e, :], second[e:, :], corners]


def unpack_diagonal(ref):
    q = ref.shape[1]
    e = q // 2
    upper, lower, corners = ref[q : q + e, :], ref[q + e : 2 * q, :], ref[2 * q : 2 * q + e, :]
    first = jnp.concatenate([upper, jnp.concatenate([upper.T[e:, :], corners[:, e:]], axis=1)], axis=0)
    second = jnp.concatenate([jnp.concatenate([corners[:, 0:e], lower.T[0:e, :]], axis=1), lower], axis=0)
    return first, ref[0:q, :], second


def prepare_body(half, t_ref, early_ref, near_ref, side_ref, column_ref, first_ref, a_out, m_out, p_out, outer_out):
    n, q = 2 * half, half // 2
    width = t_ref.shape[1] - n
    mine = first_ref[0]
    put_sibling(m_out, near_ref, side_ref, 0, mine)
    at = 2 * q
    row = jnp.concatenate([side_ref[at + i : at + i + 1, :] for i in range(n // q)], axis=1)
    p_out[...] = jnp.where(column_ref[...] == row, 1.0, 0.0).astype(BF16)
    here = pl.ds(pl.multiple_of(width + mine * half, half), half)
    there = pl.ds(pl.multiple_of(width + (1 - mine) * half, half), half)
    a_out[0:half, 0:half] = t_ref[:, here]
    a_out[0:half, half:n] = t_ref[:, there]
    first, cross, second = unpack_diagonal(early_ref)
    a_out[tile_block(q, 2, 2)] = first
    a_out[tile_block(q, 2, 3)] = cross
    a_out[tile_block(q, 3, 3)] = second
    outer_out[...] = t_ref[:, column_blocks(half, mine)[0]]


def first_body(steps, a_in, m_in, p_ref, far_ref, side_ref, first_ref, a_out, b_out, scale_out, m_work):
    n = a_in.shape[0]
    m_work[...] = m_in[...]
    put_sibling(m_work, far_ref, side_ref, 2, first_ref[0])
    moved = pick_right(m_work[...], p_ref[...], ((1,), (1,)))
    tiles = [slice(i * TILE, (i + 1) * TILE) for i in range(n // TILE)]
    largest = [functools.reduce(jnp.maximum, [ref[tile, tile] for tile in tiles]) for ref in (a_in, m_work)]
    scale = lax.rsqrt(sum(jnp.max(x, axis=(0, 1), keepdims=True) for x in largest))
    scale_out[...] = jnp.broadcast_to(scale, scale_out.shape)
    for i, rows in enumerate(tiles):
        later = slice(i * TILE, n)
        both = a_in[rows, later] + pick_left(p_ref[rows, :], moved[:, later], ((1,), (0,)))
        a_out[rows, later] = both * scale
    top = b_out.shape[0]
    on_diagonal = [lax.broadcasted_iota(jnp.int32, (top, top), axis) for axis in (0, 1)]
    b_out[...] = jnp.where(on_diagonal[0] == on_diagonal[1], 1.0, 0.0).astype(F32)
    eliminate(a_out, b_out, steps)


def middle_body(k, a_ref, b_ref, t_ref, mine_ref, others_ref, scale_ref, first_ref, a_out, g_out):
    top, half, n, width = b_ref.shape[0], t_ref.shape[0], a_ref.shape[0], g_out.shape[1]
    own, last = slice(k * TILE, (k + 1) * TILE), slice((k + 1) * TILE, n)
    inverse = invert_tile(a_ref[own, own])
    here, there = column_blocks(half, first_ref[0])
    scale = scale_ref[0:1, 0:1]
    g_out[0:half, :] = t_ref[:, 0:width] * scale
    g_out[half:, here] = mine_ref[...] * scale
    g_out[half:, there] = others_ref[...] * scale
    first = g_out[0:top, :]
    rest = g_out[top:, :] - full(a_ref[0:top, top:], first, ((0,), (0,)))
    first = full(b_ref[...], first)
    old = a_ref[own, last]
    panel = full(inverse, old)
    a_out[last, last] = a_ref[last, last] - full(old, panel, ((0,), (0,)))
    right = full(inverse, rest[0:TILE, :])
    g_out[own, :] = right
    g_out[last, :] = rest[TILE:, :] - full(old, right, ((0,), (0,)))
    factor = a_ref[0:top, own]
    a_out[0:top, last] = a_ref[0:top, last] - full(factor, panel)
    a_out[own, last] = panel
    g_out[0:top, :] = first - full(factor, right)


def column_blocks(half, mine):
    return [pl.ds(pl.multiple_of(x * half, half), half) for x in (mine, 1 - mine)]


def last_body(k, half, a_ref, g_ref, p_ref, first_ref, g_out, h_out):
    own, before = slice(k * TILE, (k + 1) * TILE), slice(0, k * TILE)
    right = full(invert_tile(a_ref[own, own]), g_ref[own, :])
    g_out[own, :] = right
    g_out[before, :] = g_ref[before, :] - full(a_ref[before, own], right)
    _, there = column_blocks(half, first_ref[0])
    h_out[...] = pick_left(p_ref[...], g_out[:, there], ((0,), (0,)))


def send_body(half, g_ref, p_ref, chunk_ref, first_ref, h_out, send_out):
    _, there = column_blocks(half, first_ref[0])
    h = pick_left(p_ref[...], g_ref[:, there], ((0,), (0,)))
    h_out[...] = h
    send_out[...] = -three_pass(h, chunk_ref[...], ((0,), (0,)))


def send_more_body(h_ref, chunk_ref, send_out):
    send_out[...] = -three_pass(h_ref[...], chunk_ref[...], ((0,), (0,)))


def output_body(
    half, g_ref, p_ref, t_ref, mine_ref, others_ref, ext_ref, row_ref, first_ref, chunk_a, chunk_b, own_ref, sol_ref, keep_ref
):
    n, q = 2 * half, half // 2
    mine = first_ref[0]
    here, there = column_blocks(half, mine)
    g = g_ref[...]
    left = jnp.concatenate([t_ref[:, here], mine_ref[...]], axis=0)
    own_ref[...] = ext_ref[...] - three_pass(left, g, ((0,), (0,)))
    target = lax.broadcasted_iota(jnp.int32, (half, n), 0) + mine * half
    onehot = jnp.where(row_ref[...].astype(jnp.int32) == target, 1.0, 0.0).astype(BF16)
    sol_ref[...] = -pick_left(onehot, g, ((1,), (0,)))
    h = pick_left(p_ref[...], g_ref[:, here], ((0,), (0,)))
    for i, chunk in enumerate((chunk_a, chunk_b)):
        keep_ref[:, i * q : (i + 1) * q] = -three_pass(h, chunk[...], ((0,), (0,)))


def cross_body(keep_ref, first_part, second_part, first_ref, out_ref):
    half, q = keep_ref.shape[0], first_part.shape[1]
    mine = first_ref[0]
    here, _ = column_blocks(half, mine)
    out_ref[:, here] = keep_ref[...]
    for i, part in enumerate((first_part, second_part)):
        out_ref[:, pl.ds(pl.multiple_of((1 - mine) * half + i * q, q), q)] = part[...]


def cut(t_ref, q, row, column):
    return t_ref[pl.ds(pl.multiple_of(row, q), q), pl.ds(pl.multiple_of(column, q), q)]


def pack_diagonal_body(half, width, t_ref, first_ref, diag_ref):
    q = half // 2
    here = width + first_ref[0] * half
    at = 0
    for block in pack_diagonal(cut(t_ref, q, 0, here), cut(t_ref, q, 0, here + q), cut(t_ref, q, q, here + q)):
        diag_ref[at : at + block.shape[0], :] = block
        at += block.shape[0]


def pack_side_body(half, width, t_ref, map_ref, first_ref, side_ref, outer_ref, row_ref, column_ref):
    q, n = half // 2, 2 * half
    mine = first_ref[0]
    there = width + (1 - mine) * half
    side_ref[0:q, :] = cut(t_ref, q, 0, there + q)
    side_ref[q : 2 * q, :] = cut(t_ref, q, mine * q, there + mine * q)
    spans = column_blocks(half, mine)
    outer_ref[...] = t_ref[:, spans[1]]
    row = jnp.concatenate([map_ref[:, span] for span in spans], axis=1).astype(F32)
    row_ref[...] = row
    column_ref[...] = jnp.broadcast_to(row, (8, n)).T[:, 0:1]
    parts = [row[:, i * q : (i + 1) * q] for i in range(n // q)]
    side_ref[2 * q :, :] = jnp.concatenate(parts + parts, axis=0)[0:8, :]


def pack_outer_body(t_ref, mine_ref, first_ref, *chunks):
    half = t_ref.shape[0]
    mine = first_ref[0]
    for i, chunk in enumerate(chunks):
        width = chunk.shape[1]
        chunk[0:half, :] = t_ref[:, pl.ds(pl.multiple_of(mine * half + i * width, width), width)]
        chunk[half:, :] = mine_ref[:, i * width : (i + 1) * width]


def sibling(x):
    size = lax.axis_size("leaf")
    return lax.ppermute(x, "leaf", [(i, i ^ size // 2) for i in range(size)])


def across(x):
    return lax.ppermute(x, "sib", [(0, 1), (1, 0)])


def kernel(body, outs, places, scratch=(), flops=1e8):
    return pl.pallas_call(
        body,
        out_shape=outs,
        in_specs=[pl.BlockSpec(memory_space=place) for place in places],
        scratch_shapes=list(scratch),
        compiler_params=pltpu.CompilerParams(vmem_limit_bytes=VMEM_LIMIT),
        cost_estimate=pl.CostEstimate(flops=int(flops), bytes_accessed=1 << 20, transcendentals=0),
    )


def two_shards(t_int, t_ext, iface_map):
    t_int, t_ext = t_int[0], t_ext[0]
    half, n = t_int.shape[0], iface_map.shape[1]
    width = t_int.shape[1] - n
    tiles = n // TILE
    q = half // 2
    f = lambda *shape: jax.ShapeDtypeStruct(shape, F32)
    vmem, smem = pltpu.VMEM, pltpu.SMEM
    mine = lax.axis_index("sib").astype(jnp.int32)
    first = mine.reshape(1)
    diag = kernel(functools.partial(pack_diagonal_body, half, width), f(5 * q // 2, q), [vmem, smem])(t_int, first)
    side, outer, own_row, column = kernel(
        functools.partial(pack_side_body, half, width),
        (f(2 * q + 8, q), f(half, half), f(1, n), f(n, 1)),
        [vmem, vmem, smem],
    )(t_int, iface_map, first)
    near = sibling(diag)
    diag_other = across(diag)
    far = across(near)
    near_side = sibling(side)
    outer_mine = across(outer)
    near, near_side = lax.optimization_barrier((near, near_side))
    far_side = across(near_side)
    chunks = kernel(pack_outer_body, [f(n, q)] * 2, [vmem, vmem, smem])(t_int, outer_mine, first)
    first_late, *_ = lax.optimization_barrier((first, *chunks))
    a, m, onehot, outer = kernel(
        functools.partial(prepare_body, half),
        (f(n, n), f(n, n), jax.ShapeDtypeStruct((n, n), BF16), f(half, half)),
        [vmem] * 5 + [smem],
    )(t_int, diag_other, near, near_side, column, first_late)
    outer_others = across(outer)
    chunk_a, _ = lax.optimization_barrier((chunks[0], near_side))
    chunk_b, onehot = lax.optimization_barrier((chunks[1], onehot))
    near_r = [sibling(chunk_a), sibling(chunk_b)]
    top = (tiles - 2) * TILE
    a, b, scale = kernel(
        functools.partial(first_body, range(tiles - 2)),
        (f(n, n), f(top, top), f(8, TILE)),
        [vmem] * 5 + [smem],
        [pltpu.VMEM((n, n), F32)],
        10e9,
    )(a, m, onehot, far, far_side, first)
    a, g = kernel(
        functools.partial(middle_body, tiles - 2), (f(n, n), f(n, width)), [vmem] * 6 + [smem], (), 5e9
    )(a, b, t_int, outer_mine, outer_others, scale, first)
    g, h = kernel(
        functools.partial(last_body, tiles - 1, half), (f(n, width), f(n, half)), [vmem] * 3 + [smem], (), 5e9
    )(a, g, onehot, first)
    cross_a = across(kernel(send_more_body, f(half, q), [vmem] * 2, (), 1e9)(h, near_r[0]))
    cross_b = across(kernel(send_more_body, f(half, q), [vmem] * 2, (), 5e9)(h, near_r[1]))
    own_map, solution_op, keep = kernel(
        functools.partial(output_body, half),
        (f(half, width), f(half, width), f(half, half)),
        [vmem] * 7 + [smem] + [vmem] * 2,
        (),
        1e6,
    )(g, onehot, t_int, outer_mine, outer_others, t_ext, own_row, first, *near_r)
    cross_map = kernel(cross_body, f(half, width), [vmem] * 3 + [smem])(keep, cross_a, cross_b, first)
    return own_map[None], cross_map[None], solution_op[None]


def common_order(matrix, index_map):
    points = index_map.shape[0]
    inverse = jnp.zeros((points,), jnp.int32).at[index_map].set(jnp.arange(points, dtype=jnp.int32))
    picked = matrix[inverse]
    outer_width = matrix.shape[1] - points
    return (picked[:, :outer_width], picked[:, outer_width + inverse])


def many_shards(t_int, t_ext, iface_map):
    shard_rows = t_ext.shape[1]
    first_row = lax.axis_index("sib") * shard_rows
    near_rows, other_map = sibling((t_int, iface_map))
    own_rows = lax.all_gather(t_int, "sib", axis=1, tiled=True)
    other_rows = lax.all_gather(near_rows, "sib", axis=1, tiled=True)
    own_outer, own_iface = common_order(own_rows[0], iface_map[0])
    other_outer, other_iface = common_order(other_rows[0], other_map[0])
    g = solve(own_iface + other_iface, own_outer)
    product = lambda left, right: lax.dot_general(
        left, right, (((0,), (0,)), ((), ())), precision=lax.Precision.HIGHEST, preferred_element_type=F32
    )
    left = lax.dynamic_slice_in_dim(own_outer, first_row, shard_rows, 1)
    left_g = lax.dynamic_slice_in_dim(g, first_row, shard_rows, 1)
    own_map = t_ext - product(left, g)[None]
    cross_map = -product(left_g, other_outer)[None]
    solution_op = -lax.dynamic_slice_in_dim(g, first_row, shard_rows, 0)[None]
    return own_map, cross_map, solution_op


def solution(mesh):
    placed = P("leaf", "sib", None)
    return jax.shard_map(
        two_shards if mesh.shape["sib"] == 2 else many_shards,
        mesh=mesh,
        in_specs=(placed, placed, P("leaf", None)),
        out_specs=(placed, placed, placed),
        check_vma=False,
    )
```
